32 devices in a mesh: band: 4 (over y, core), row: 8 (over z, x).
Axes of the slice: x: 2, y: 2, z: 4, core: 2. Of those that a mesh axis runs over, the one named last changes fastest.
Arguments:
- observed: bfloat16 [224, 256, 680], P('band', 'row'), may hold values from -60 to 60
- row_taps: float32 [224, 25], P('band'), may hold values from 0 to 0.08
- col_taps: float32 [224, 25], P('band'), may hold values from 0 to 0.08
- spectral_basis: bfloat16 [224, 32], replicated, may hold values from -0.375 to 0.375
- ridge_weights: float32 [32], replicated, may hold values from 0.05 to 0.5
Outputs:
- coefficients: float32 [32, 256, 680], P(None, 'row', 'band')
- residual: float32 [32, 256, 680], P(None, 'row', 'band')
The draws below stay inside these ranges and needn't reach their ends.
All inputs are finite; a program needn't handle non-finite values.
Results may differ from the reference program's by a relative error of at most 0.01.
Values may be sent and summed in bfloat16 or wider, within the bound.
No kernel may reach another device: no remote copies, remote signals or barrier semaphores. Data moves between devices by JAX's collectives and lax.ppermute only.
A program may use at most 64 MiB of HBM per device.

```python
import math
import jax
import jax.numpy as jnp
from jax import lax

B = 224
K = 32
W = 680
TAPS = 25
ITERS = 2
H = 256


def draw_observed(key, part):
    position = jnp.arange(W, dtype=jnp.float32) / (W - 1)
    profile = 2.0 * jnp.exp(jnp.log(4.0) * position)
    values = jax.random.normal(key, (B, H, W), jnp.float32)
    values = jnp.clip(values * profile[None, None, :], -60.0, 60.0)
    return values.astype(jnp.bfloat16)


def block_levels(stream_key, extent, shards, low, top_value):
    gain = 1.0
    for dim, parts in shards:
        draws = jax.random.uniform(jax.random.fold_in(jax.random.fold_in(stream_key, 6), dim), (parts,), jnp.float32, low / len(shards), top_value / len(shards))
        gain = gain * jnp.repeat(jnp.exp(draws), extent[dim] // parts).reshape((-1,) + (1,) * (len(extent) - 1 - dim))
    return gain


def normal_values(rng, shape, spread, bound, kind=jnp.bfloat16):
    entries = spread * jax.random.normal(rng, shape, jnp.float32)
    return jnp.clip(entries, min=-bound, max=bound).astype(kind)


def setup_inputs(seed: int = 0) -> dict:
    streams_of = jax.random.split(jax.random.key(seed), 6)
    observed = draw_observed(jax.random.fold_in(streams_of[5], 71), 0)
    row_taps = jnp.clip(0.08 * jax.random.uniform(streams_of[1], (B, TAPS), jnp.float32) ** block_levels(streams_of[1], (B, TAPS), ((0, 4),), -0.2, 0.2), 0.0, 0.08)
    col_taps = jnp.clip(0.08 * jax.random.uniform(streams_of[2], (B, TAPS), jnp.float32) ** block_levels(streams_of[2], (B, TAPS), ((0, 4),), -0.2, 0.2), 0.0, 0.08)
    spectral_basis = normal_values(streams_of[3], (B, K), B ** -0.5, 0.375)
    ridge_weights = jnp.clip(jnp.exp(jax.random.uniform(streams_of[4], (K,), jnp.float32, math.log(0.05), math.log(0.5))), 0.05, 0.5)
    return dict(observed=observed, row_taps=row_taps, col_taps=col_taps, spectral_basis=spectral_basis, ridge_weights=ridge_weights)


def rows_plain(field, kernel):
    radius = (kernel.shape[0] - 1) // 2
    height = field.shape[0]
    padded = jnp.pad(field, ((radius, radius), (0, 0)))
    running = jnp.zeros(field.shape, jnp.float32)
    for offset in range(kernel.shape[0]):
        running = running + kernel[offset] * padded[offset:offset + height, :].astype(jnp.float32)
    return running


def cols_plain(field, kernel):
    radius = (kernel.shape[0] - 1) // 2
    width_cols = field.shape[1]
    padded = jnp.pad(field, ((0, 0), (radius, radius)))
    running = jnp.zeros(field.shape, jnp.float32)
    for offset in range(kernel.shape[0]):
        running = running + kernel[offset] * padded[:, offset:offset + width_cols]
    return running


def blur_plain(field, row_kernel, col_kernel):
    return cols_plain(rows_plain(field, row_kernel), col_kernel)


def adjoint_band(items):
    field, row_kernel, col_kernel = items
    return blur_plain(field, row_kernel[::-1], col_kernel[::-1]).astype(jnp.bfloat16)


def normal_band(items):
    field, row_kernel, col_kernel = items
    blurred = blur_plain(field, row_kernel, col_kernel).astype(jnp.bfloat16)
    return blur_plain(blurred, row_kernel[::-1], col_kernel[::-1]).astype(jnp.bfloat16)


def reference(observed, row_taps, col_taps, spectral_basis, ridge_weights):
    bands, height, width_cols = observed.shape
    comps = spectral_basis.shape[1]
    basis_wide = spectral_basis.astype(jnp.float32)
    adjoint_obs = lax.map(adjoint_band, (observed, row_taps, col_taps))
    rhs = jnp.dot(spectral_basis.T, adjoint_obs.reshape(bands, height * width_cols), preferred_element_type=jnp.float32).reshape(comps, height, width_cols)

    def normal_map(direction):
        spectra = jnp.dot(basis_wide, direction.reshape(comps, height * width_cols), precision=lax.Precision.HIGHEST)
        spectra = spectra.reshape(bands, height, width_cols).astype(jnp.bfloat16)
        returned = lax.map(normal_band, (spectra, row_taps, col_taps))
        projected = jnp.dot(spectral_basis.T, returned.reshape(bands, height * width_cols), preferred_element_type=jnp.float32).reshape(comps, height, width_cols)
        return projected + ridge_weights[:, None, None] * direction

    solution = jnp.zeros_like(rhs)
    residual = rhs
    direction = rhs
    norm_now = jnp.sum(residual * residual)
    for iteration in range(ITERS):
        mapped = normal_map(direction)
        alpha = norm_now / jnp.sum(direction * mapped)
        solution = solution + alpha * direction
        residual = residual - alpha * mapped
        norm_next = jnp.sum(residual * residual)
        direction = residual + (norm_next / norm_now) * direction
        norm_now = norm_next
    return solution, residual
```

```python
import functools

import jax
import jax.numpy as jnp
from jax import lax
from jax.experimental import pallas as pl
from jax.experimental.pallas import tpu as pltpu
from jax.sharding import PartitionSpec as P

LANES = 128
SUB = 8
BF = jnp.bfloat16
F32 = jnp.float32
VMEM_LIMIT = 50 * 1024 * 1024


def round_up(value, unit):
    return (value + unit - 1) // unit * unit


def group_size(count, most):
    return max(size for size in range(1, most + 1) if count % size == 0)


def dot(lhs, rhs):
    return lax.dot_general(lhs, rhs, (((1,), (0,)), ((), ())), preferred_element_type=F32)


def toeplitz(taps, rows, shift):
    lanes = taps.shape[1]
    pieces = []
    for first in range(0, rows, LANES):
        count = min(LANES, rows - first)
        wide = jnp.broadcast_to(taps, (count, lanes))
        pieces.append(pltpu.roll(wide, (shift + first) % lanes, 1, stride=1, stride_axis=0))
    return jnp.concatenate(pieces, axis=0) if len(pieces) > 1 else pieces[0]


def spread_basis(basis, group, kinds):
    bands = basis.shape[0]
    rows = jnp.arange(bands * SUB)
    lanes = jnp.arange(SUB * kinds)
    up = (rows[:, None] // SUB == jnp.arange(bands)[None, :]).astype(BF)
    out = (jnp.arange(kinds)[:, None] == lanes[None, :] % kinds).astype(BF)
    same = (rows[:, None] % SUB) == (lanes[None, :] // kinds)
    wide = dot(dot(up, basis).astype(BF), out)
    return jnp.where(same, wide, 0.0).astype(BF).reshape(bands // group, group * SUB, SUB * kinds)


def adjoint_kernel(columns, radius, obs_ref, row_ref, col_ref, mix_ref, out_ref, acc, ys):
    step = pl.program_id(0)
    group, height, _ = obs_ref.shape
    span = ys.shape[3]
    tiles = span // (2 * LANES)
    chunks = ys.shape[0]
    ext = chunks * SUB

    @pl.when(step == 0)
    def _():
        acc[...] = jnp.zeros_like(acc)

    last = columns // LANES * LANES
    width = 2 * LANES

    def one(b):
        cells = obs_ref[b]
        tail = cells[:, last:]
        pieces = [jnp.zeros((height, LANES), BF), cells[:, :last]]
        if columns > last:
            pieces.append(
                jnp.concatenate([tail, jnp.zeros((height, LANES - (columns - last)), BF)], axis=1)
            )
        have = sum(piece.shape[1] for piece in pieces)
        if have < span + 2 * LANES:
            pieces.append(jnp.zeros((height, span + 2 * LANES - have), BF))
        padded = jnp.concatenate(pieces, axis=1)
        stacked = jnp.concatenate(
            [padded[:, t * width : t * width + 2 * width] for t in range(tiles)], axis=0
        )
        edge = 2 * SUB
        ring = toeplitz(col_ref[b], width, -round_up(radius, SUB)).astype(BF)
        top, bottom = ring[:edge], ring[width - edge :]
        blank = jnp.zeros((edge, width), BF)
        near = lax.broadcasted_iota(jnp.int32, (edge, width), 1) < LANES
        rest = jnp.zeros((LANES - edge, width), BF)
        matrix = jnp.concatenate(
            [
                rest,
                jnp.where(near, bottom, blank),
                jnp.where(near, top, blank),
                ring[edge : width - edge],
                jnp.where(near, blank, bottom),
                jnp.where(near, blank, top),
                rest,
            ],
            axis=0,
        )
        mixed = dot(stacked, matrix).astype(BF)
        field = jnp.concatenate(
            [mixed[t * height : (t + 1) * height] for t in range(tiles)], axis=1
        )
        rows = toeplitz(row_ref[b], ext, -2 * radius)[:, :height]
        high = rows.astype(BF)
        low = (rows - high.astype(F32)).astype(BF)
        done = dot(high, field) + dot(low, field)
        for c in range(chunks):
            ys[c, b] = done[c * SUB : (c + 1) * SUB]

    @pl.loop(0, group)
    def _(b):
        one(b)

    for c in range(chunks):
        cells = ys[c].reshape(group * SUB, span).astype(BF)
        acc[c] += dot(mix_ref[0], cells)

    @pl.when(step == pl.num_programs(0) - 1)
    def _():
        out_ref[...] = acc[...].reshape(out_ref.shape).astype(out_ref.dtype)


def gram_kernel(halo, row_ref, row_flip_ref, col_ref, col_flip_ref, row_mask_ref, col_mask_ref, gr_ref, gl_ref):
    group, height, row_lanes = gr_ref.shape
    size = gl_ref.shape[1]
    for b in range(group):
        left = (toeplitz(col_flip_ref[b], size, -halo) * col_mask_ref[...]).astype(BF)
        right = toeplitz(col_ref[b], size, -halo).astype(BF)
        gl_ref[b] = dot(left, right).astype(BF)
        left = (toeplitz(row_flip_ref[b], height, 0) * row_mask_ref[...]).astype(BF)
        right = toeplitz(row_ref[b], row_lanes, 0).astype(BF)
        gr_ref[b] = dot(left, right).astype(BF)


def normal_kernel(columns, p_ref, own_ref, ridge_ref, sk_ref, pk_ref, gr_ref, gl_ref, out_ref, acc, xs, ys):
    step = pl.program_id(0)
    group, height, _ = gr_ref.shape
    ext, kinds, lanes = p_ref.shape
    chunks = height // SUB

    @pl.when(step == 0)
    def _():
        acc[...] = jnp.zeros_like(acc)
        xs[...] = jnp.zeros_like(xs)

    for c in range(0, ext, 2 * SUB):
        halves = []
        for s in (c, c + SUB):
            cells = p_ref[s : s + SUB].reshape(SUB * kinds, lanes)
            halves.append(dot(sk_ref[0], cells).reshape(group, SUB, lanes))
        xs[:, c : c + 2 * SUB, :] = jnp.concatenate(halves, axis=1).astype(BF)

    @pl.loop(0, group, step=8)
    def _(first):
        mids = []
        for b in range(8):
            mids.append(dot(gr_ref[first + b], xs[first + b]).astype(BF))
        for b in range(8):
            done = dot(mids[b], gl_ref[first + b])
            for c in range(chunks):
                ys[c, first + b] = done[c * SUB : (c + 1) * SUB]

    for c in range(chunks):
        acc[c] += dot(pk_ref[0], ys[c].reshape(group * SUB, lanes).astype(BF))

    @pl.when(step == pl.num_programs(0) - 1)
    def _():
        total = acc[...].reshape(height, kinds, lanes) + ridge_ref[...] * own_ref[...]
        lane = lax.broadcasted_iota(jnp.int32, total.shape, 2)
        out_ref[...] = jnp.where(lane < columns, total, 0.0)


def shift_both(low_edge, high_edge, axis):
    count = lax.axis_size(axis)
    from_before = lax.ppermute(high_edge, axis, [(i, i + 1) for i in range(count - 1)])
    from_after = lax.ppermute(low_edge, axis, [(i + 1, i) for i in range(count - 1)])
    return from_before, from_after


def local(observed, row_taps, col_taps, spectral_basis, ridge_weights):
    bands_here, height, columns_all = observed.shape
    taps = row_taps.shape[1]
    radius = (taps - 1) // 2
    halo = 2 * radius
    bands, kinds = spectral_basis.shape
    n_band = lax.axis_size("band")
    n_row = lax.axis_size("row")
    columns = columns_all // n_band
    lanes = round_up(columns + 2 * halo, 2 * LANES)
    me_band = lax.axis_index("band")
    me_row = lax.axis_index("row")
    core = me_band % 2
    chip = me_band // 2
    chips = n_band // 2

    def widen(values, width, lead=0):
        return jnp.pad(values, ((0, 0), (lead, width - taps - lead)))[:, None, :]

    every = lax.all_gather(jnp.concatenate([row_taps, col_taps], axis=1), "band", tiled=True)
    row_all, col_all = every[:, :taps], every[:, taps:]

    size = lanes
    at = jnp.arange(size)
    edge = me_band * columns - radius + at
    col_mask = ((edge >= 0) & (edge < columns_all) & (at < columns + 2 * radius)).astype(F32)[None]
    at = jnp.arange(LANES)
    edge = me_row * height - radius + at
    row_mask = ((edge >= 0) & (edge < height * n_row) & (at < height + 2 * radius)).astype(F32)[None]
    part = group_size(bands, 16)
    spec = lambda width: pl.BlockSpec((part, 1, width), lambda i: (i, 0, 0))
    whole = lambda shape: pl.BlockSpec(shape, lambda i: (0,) * len(shape))
    gr, gl = pl.pallas_call(
        functools.partial(gram_kernel, halo),
        grid=(bands // part,),
        in_specs=[spec(LANES), spec(LANES), spec(size), spec(size), whole((1, LANES)), whole((1, size))],
        out_specs=[
            pl.BlockSpec((part, height, LANES), lambda i: (i, 0, 0)),
            pl.BlockSpec((part, size, size), lambda i: (i, 0, 0)),
        ],
        out_shape=[
            jax.ShapeDtypeStruct((bands, height, LANES), BF),
            jax.ShapeDtypeStruct((bands, size, size), BF),
        ],
        compiler_params=pltpu.CompilerParams(vmem_limit_bytes=VMEM_LIMIT),
        cost_estimate=pl.CostEstimate(
            flops=bands * 2 * size**3, bytes_accessed=bands * size * size * 2, transcendentals=0
        ),
        name="gram",
    )(
        widen(row_all, LANES),
        widen(row_all[:, ::-1], LANES),
        widen(col_all, size),
        widen(col_all[:, ::-1], size),
        row_mask,
        col_mask,
    )

    few = group_size(bands_here, 32)
    span = round_up(columns_all, 2 * LANES)
    ext = height + 2 * radius
    chunks = ext // SUB
    basis_here = lax.dynamic_slice_in_dim(spectral_basis, me_band * bands_here, bands_here, 0)
    mix = jnp.swapaxes(spread_basis(basis_here, few, kinds), 1, 2)
    summed = pl.pallas_call(
        functools.partial(adjoint_kernel, columns_all, radius),
        grid=(bands_here // few,),
        in_specs=[
            pl.BlockSpec((few, height, columns_all), lambda i: (i, 0, 0)),
            pl.BlockSpec((few, 1, LANES), lambda i: (i, 0, 0)),
            pl.BlockSpec((few, 1, 2 * LANES), lambda i: (i, 0, 0)),
            pl.BlockSpec((1,) + mix.shape[1:], lambda i: (i, 0, 0)),
        ],
        out_specs=whole((ext, kinds, span)),
        out_shape=jax.ShapeDtypeStruct((ext, kinds, span), BF),
        scratch_shapes=[
            pltpu.VMEM((chunks, SUB * kinds, span), F32),
            pltpu.VMEM((chunks, few, SUB, span), F32),
        ],
        compiler_params=pltpu.CompilerParams(vmem_limit_bytes=VMEM_LIMIT),
        cost_estimate=pl.CostEstimate(
            flops=bands_here * 2 * 96 * 512 * 256, bytes_accessed=observed.size * 2, transcendentals=0
        ),
        name="adjoint",
    )(observed, widen(row_taps[:, ::-1], LANES), widen(col_taps, 2 * LANES, -radius % SUB), mix)

    half = kinds // 2
    keep = lax.dynamic_slice_in_dim(summed, core * half, half, 1)
    give = lax.dynamic_slice_in_dim(summed, (1 - core) * half, half, 1)
    pairs = [(i, i ^ 1) for i in range(n_band)]
    got = lax.ppermute(give, "band", pairs)
    pair = keep.astype(F32) + got.astype(F32)
    before, after = shift_both(pair[:radius].astype(BF), pair[ext - radius :].astype(BF), "row")
    rows = pair[radius : ext - radius]
    pad = ((0, height - radius), (0, 0), (0, 0))
    rows = rows + jnp.pad(before.astype(F32), pad) + jnp.pad(after.astype(F32), (pad[0][::-1],) + pad[1:])
    rows = jnp.pad(rows[:, :, :columns_all], ((0, 0), (0, 0), (halo, halo)))
    wide = 2 * columns + 2 * halo
    total = lax.dynamic_slice_in_dim(rows, chip * 2 * columns, wide, 2)
    for hop in range(1, chips):
        target = (chip + hop) % chips
        piece = lax.dynamic_slice_in_dim(rows, target * 2 * columns, wide, 2).astype(BF)
        moves = [(i, (i + 2 * hop) % n_band) for i in range(n_band)]
        total = total + lax.ppermute(piece, "band", moves).astype(F32)
    other = lax.ppermute(total, "band", pairs)
    first = jnp.where(core == 0, total, other)
    second = jnp.where(core == 0, other, total)
    total = jnp.concatenate([first, second], axis=1)
    window = lax.dynamic_slice_in_dim(total, core * columns, columns + 2 * halo, 2)
    v0 = jnp.pad(window[:, :, halo : halo + columns], ((0, 0), (0, 0), (0, lanes - columns)))
    window = jnp.pad(window.astype(BF), ((0, 0), (0, 0), (0, lanes - columns - 2 * halo)))

    group = group_size(bands, 32)
    sk = spread_basis(spectral_basis, group, kinds)
    pk = jnp.swapaxes(sk, 1, 2)
    ridge = jnp.broadcast_to(ridge_weights[:, None], (kinds, lanes))
    tall = height + 2 * halo
    block = lambda shape: pl.BlockSpec((group,) + shape, lambda i: (i, 0, 0))

    def normal_map(window, own):
        before, after = shift_both(window[:halo], window[height - halo :], "row")
        cells = jnp.concatenate([before, window, after], axis=0)
        return pl.pallas_call(
            functools.partial(normal_kernel, columns),
            grid=(bands // group,),
            in_specs=[
                whole((tall, kinds, lanes)),
                whole((height, kinds, lanes)),
                whole((kinds, lanes)),
                pl.BlockSpec((1,) + sk.shape[1:], lambda i: (i, 0, 0)),
                pl.BlockSpec((1,) + pk.shape[1:], lambda i: (i, 0, 0)),
                block((height, LANES)),
                block((size, size)),
            ],
            out_specs=whole((height, kinds, lanes)),
            out_shape=jax.ShapeDtypeStruct((height, kinds, lanes), F32),
            scratch_shapes=[
                pltpu.VMEM((height // SUB, SUB * kinds, lanes), F32),
                pltpu.VMEM((group, LANES, lanes), BF),
                pltpu.VMEM((height // SUB, group, SUB, lanes), F32),
            ],
            compiler_params=pltpu.CompilerParams(vmem_limit_bytes=VMEM_LIMIT),
            cost_estimate=pl.CostEstimate(
                flops=bands * 2 * 32 * 512 * 256, bytes_accessed=bands * size * size * 2, transcendentals=0
            ),
            name="normal",
        )(cells, own, ridge, sk, pk, gr, gl)

    v1 = normal_map(window, v0)
    near = v1[:, :, :columns].astype(BF)
    before, after = shift_both(near[:, :, :halo], near[:, :, columns - halo :], "band")
    window = jnp.concatenate(
        [before, near, after, jnp.zeros((height, kinds, lanes - columns - 2 * halo), BF)], axis=2
    )
    v2 = normal_map(window, v1)

    sums = jnp.stack(
        [jnp.sum(v0 * v0), jnp.sum(v0 * v1), jnp.sum(v1 * v1), jnp.sum(v0 * v2), jnp.sum(v1 * v2)]
    )
    everyone = n_band * n_row
    mine = jnp.broadcast_to(jnp.pad(sums, (0, LANES - 5))[None, None], (everyone, SUB, LANES))
    shared = lax.all_to_all(mine, ("band", "row"), 0, 0, tiled=True)
    sums = jnp.sum(shared[:, 0, :], axis=0)
    v00, v01, v11, v02, v12 = [sums[i] for i in range(5)]
    alpha = v00 / v01
    norm = v00 - 2.0 * alpha * v01 + alpha * alpha * v11
    ratio = norm / v00
    lead = 1.0 + ratio
    product = lead * lead * v01 - lead * alpha * (v02 + v11) + alpha * alpha * v12
    second = norm / product
    coefficients = (alpha + second * lead) * v0 - (second * alpha) * v1
    residual = v0 - (alpha + second * lead) * v1 + (second * alpha) * v2
    give_back = lambda field: jnp.swapaxes(field[:, :, :columns], 0, 1)
    return give_back(coefficients), give_back(residual)


def solution(mesh):
    in_specs = (P("band", "row", None), P("band", None), P("band", None), P(), P())
    out_specs = (P(None, "row", "band"), P(None, "row", "band"))
    return jax.shard_map(local, mesh=mesh, in_specs=in_specs, out_specs=out_specs, check_vma=False)
```

```python
import functools

import jax
import jax.numpy as jnp
from jax import lax
from jax.experimental import pallas as pl
from jax.experimental.pallas import tpu as pltpu
from jax.sharding import PartitionSpec as P

LANES = 128
SUB = 8
BF = jnp.bfloat16
F32 = jnp.float32
VMEM_LIMIT = 50 * 1024 * 1024


def round_up(value, unit):
    return (value + unit - 1) // unit * unit


def group_size(count, most):
    return max(size for size in range(1, most + 1) if count % size == 0)


def dot(lhs, rhs):
    return lax.dot_general(lhs, rhs, (((1,), (0,)), ((), ())), preferred_element_type=F32)


def toeplitz(taps, rows, shift):
    lanes = taps.shape[1]
    pieces = []
    for first in range(0, rows, LANES):
        count = min(LANES, rows - first)
        wide = jnp.broadcast_to(taps, (count, lanes))
        pieces.append(pltpu.roll(wide, (shift + first) % lanes, 1, stride=1, stride_axis=0))
    return jnp.concatenate(pieces, axis=0) if len(pieces) > 1 else pieces[0]


def spread_basis(basis, group, kinds):
    bands = basis.shape[0]
    rows = jnp.arange(bands * SUB)
    lanes = jnp.arange(SUB * kinds)
    up = (rows[:, None] // SUB == jnp.arange(bands)[None, :]).astype(BF)
    out = (jnp.arange(kinds)[:, None] == lanes[None, :] % kinds).astype(BF)
    same = (rows[:, None] % SUB) == (lanes[None, :] // kinds)
    wide = dot(dot(up, basis).astype(BF), out)
    return jnp.where(same, wide, 0.0).astype(BF).reshape(bands // group, group * SUB, SUB * kinds)


def component_first(spread, kinds):
    groups, deep, _ = spread.shape
    split = spread.reshape(groups, deep, SUB, kinds)
    return split.transpose(0, 3, 2, 1).reshape(groups, kinds * SUB, deep)


def adjoint_kernel(columns, radius, obs_ref, taps_ref, mix_ref, out_ref, acc, ys, mats, rows):
    step = pl.program_id(0)
    group, height, _ = obs_ref.shape
    span = ys.shape[3]
    width = 2 * LANES
    tiles = span // width
    chunks = ys.shape[0]
    ext = chunks * SUB
    edge = 2 * SUB
    last = columns // LANES * LANES
    batch = group_size(group, 4)

    @pl.when(step == 0)
    def _():
        acc[...] = jnp.zeros_like(acc)
        mats[...] = jnp.zeros_like(mats)

    @pl.loop(0, group, step=batch)
    def _(start):
        near = lax.broadcasted_iota(jnp.int32, (edge, width), 1) < LANES
        blank = jnp.zeros((edge, width), BF)
        for b in range(batch):
            b = start + b
            ring = toeplitz(taps_ref[b, 4:5], width, -round_up(radius, SUB)).astype(BF)
            top, bottom = ring[:edge], ring[width - edge :]
            mats[b, LANES - edge : LANES] = jnp.where(near, bottom, blank)
            mats[b, LANES : LANES + edge] = jnp.where(near, top, blank)
            mats[b, LANES + edge : LANES + width - edge] = ring[edge : width - edge]
            mats[b, LANES + width - edge : LANES + width] = jnp.where(near, blank, bottom)
            mats[b, LANES + width : LANES + width + edge] = jnp.where(near, blank, top)
            reach = toeplitz(taps_ref[b, 1:2, :LANES], ext, -2 * radius)[:, :height]
            high = reach.astype(BF)
            rows[b, 0] = high
            rows[b, 1] = (reach - high.astype(F32)).astype(BF)

    @pl.loop(0, group, step=batch)
    def _(start):
        fields = []
        for b in range(batch):
            cells = obs_ref[start + b]
            pieces = [jnp.zeros((height, LANES), BF), cells[:, :last]]
            if columns > last:
                fill = jnp.zeros((height, LANES - (columns - last)), BF)
                pieces.append(jnp.concatenate([cells[:, last:], fill], axis=1))
            have = sum(piece.shape[1] for piece in pieces)
            if have < span + width:
                pieces.append(jnp.zeros((height, span + width - have), BF))
            padded = jnp.concatenate(pieces, axis=1)
            stacked = jnp.concatenate(
                [padded[:, t * width : t * width + 2 * width] for t in range(tiles)], axis=0
            )
            mixed = dot(stacked, mats[start + b]).astype(BF)
            fields.append(
                jnp.concatenate([mixed[t * height : (t + 1) * height] for t in range(tiles)], axis=1)
            )
        for b in range(batch):
            done = dot(rows[start + b, 0], fields[b]) + dot(rows[start + b, 1], fields[b])
            for c in range(chunks):
                ys[c, start + b] = done[c * SUB : (c + 1) * SUB]

    for c in range(chunks):
        cells = ys[c].reshape(group * SUB, span).astype(BF)
        acc[c] += dot(mix_ref[0], cells)

    @pl.when(step == pl.num_programs(0) - 1)
    def _():
        out_ref[...] = acc[...].reshape(out_ref.shape).astype(out_ref.dtype)


def gram_kernel(halo, taps_ref, row_mask_ref, col_mask_ref, gr_ref, gl_ref):
    group, height, row_lanes = gr_ref.shape
    size = gl_ref.shape[1]
    for b in range(group):
        left = (toeplitz(taps_ref[b, 3:4, :size], size, -halo) * col_mask_ref[...]).astype(BF)
        right = toeplitz(taps_ref[b, 2:3, :size], size, -halo).astype(BF)
        gl_ref[b] = dot(left, right).astype(BF)
        left = (toeplitz(taps_ref[b, 1:2, :row_lanes], height, 0) * row_mask_ref[...]).astype(BF)
        right = toeplitz(taps_ref[b, 0:1, :row_lanes], row_lanes, 0).astype(BF)
        gr_ref[b] = dot(left, right).astype(BF)


def normal_kernel(
    columns, first, p_ref, own_ref, ridge_ref, sk_ref, pk_ref, gr_ref, gl_ref, out_ref, sums_ref, acc, xs, ys
):
    step = pl.program_id(0)
    group, height, _ = gr_ref.shape
    ext, kinds, lanes = p_ref.shape
    chunks = height // SUB

    @pl.when(step == 0)
    def _():
        acc[...] = jnp.zeros_like(acc)
        xs[...] = jnp.zeros_like(xs)

    for c in range(0, ext, 2 * SUB):
        halves = []
        for s in (c, c + SUB):
            cells = p_ref[s : s + SUB].reshape(SUB * kinds, lanes)
            halves.append(dot(sk_ref[0], cells).reshape(group, SUB, lanes))
        xs[:, c : c + 2 * SUB, :] = jnp.concatenate(halves, axis=1).astype(BF)

    @pl.loop(0, group, step=8)
    def _(start):
        mids = []
        for b in range(8):
            mids.append(dot(gr_ref[start + b], xs[start + b]).astype(BF))
        for b in range(8):
            done = dot(mids[b], gl_ref[start + b])
            for c in range(chunks):
                ys[c, start + b] = done[c * SUB : (c + 1) * SUB]

    for c in range(chunks):
        acc[c] += dot(pk_ref[0], ys[c].reshape(group * SUB, lanes).astype(BF))

    @pl.when(step == pl.num_programs(0) - 1)
    def _():
        lane = lax.broadcasted_iota(jnp.int32, (kinds, SUB, lanes), 2)
        totals = [jnp.zeros((SUB, lanes), F32) for _ in range(3)]
        for c in range(chunks):
            own = own_ref[:, c * SUB : (c + 1) * SUB, :]
            image = acc[c].reshape(kinds, SUB, lanes) + ridge_ref[...] * own
            image = jnp.where(lane < columns, image, 0.0)
            out_ref[:, c * SUB : (c + 1) * SUB, :] = image
            pairs = [own * image]
            if first:
                pairs += [own * own, image * image]
            for i, pair in enumerate(pairs):
                totals[i] = totals[i] + jnp.sum(pair, axis=0)
        flat = [
            jnp.sum(
                jnp.concatenate(
                    [total[:, i : i + LANES] for i in range(0, lanes, LANES)], axis=0
                ),
                axis=0,
                keepdims=True,
            )
            for total in totals
        ]
        row = lax.broadcasted_iota(jnp.int32, (SUB, LANES), 0)
        packed = jnp.zeros((SUB, LANES), F32)
        for i, line in enumerate(flat):
            packed = packed + jnp.where(row == i, jnp.broadcast_to(line, (SUB, LANES)), 0.0)
        sums_ref[...] = packed


def combine_kernel(shared_ref, v0_ref, v1_ref, v2_ref, coef_ref, res_ref):
    columns = coef_ref.shape[2]
    lines = jnp.sum(shared_ref[...], axis=0)
    v01, v00, v11, v12 = [jnp.sum(lines[i : i + 1], axis=1, keepdims=True) for i in range(4)]
    alpha = v00 / v01
    norm = v00 - 2.0 * alpha * v01 + alpha * alpha * v11
    lead = 1.0 + norm / v00
    product = lead * lead * v01 - 2.0 * lead * alpha * v11 + alpha * alpha * v12
    second = norm / product
    one = alpha + second * lead
    two = second * alpha
    for k in range(coef_ref.shape[0]):
        v0, v1, v2 = v0_ref[k], v1_ref[k], v2_ref[k]
        coef_ref[k] = (one * v0 - two * v1)[:, :columns]
        res_ref[k] = (v0 - one * v1 + two * v2)[:, :columns]


def shift_both(low_edge, high_edge, axis):
    count = lax.axis_size(axis)
    from_before = lax.ppermute(high_edge, axis, [(i, i + 1) for i in range(count - 1)])
    from_after = lax.ppermute(low_edge, axis, [(i + 1, i) for i in range(count - 1)])
    return from_before, from_after


def local(observed, row_taps, col_taps, spectral_basis, ridge_weights):
    bands_here, height, columns_all = observed.shape
    taps = row_taps.shape[1]
    radius = (taps - 1) // 2
    halo = 2 * radius
    bands, kinds = spectral_basis.shape
    n_band = lax.axis_size("band")
    n_row = lax.axis_size("row")
    columns = columns_all // n_band
    lanes = round_up(columns + 2 * halo, 2 * LANES)
    me_band = lax.axis_index("band")
    me_row = lax.axis_index("row")
    core = me_band % 2
    chip = me_band // 2
    chips = n_band // 2

    size = lanes

    def widen(values, lead=0):
        return jnp.pad(values, ((0, 0), (lead, 2 * LANES - taps - lead)))[:, None]

    plain = jnp.concatenate([row_taps, col_taps], axis=1)
    everyone = [(plain, me_band)]
    for hop in range(1, n_band):
        moves = [(i, (i + hop) % n_band) for i in range(n_band)]
        everyone.append((lax.ppermute(plain, "band", moves), (me_band - hop) % n_band))
    basis_here = lax.dynamic_slice_in_dim(spectral_basis, me_band * bands_here, bands_here, 0)
    basis_all = jnp.concatenate(
        [lax.dynamic_slice_in_dim(spectral_basis, at * bands_here, bands_here, 0) for _, at in everyone]
    )
    every = jnp.concatenate([values for values, _ in everyone])

    def variants(values):
        row, col = values[:, :taps], values[:, taps:]
        return [widen(row), widen(row[:, ::-1]), widen(col), widen(col[:, ::-1])]

    taps_all = jnp.concatenate(variants(every), axis=1)
    taps_here = jnp.concatenate(variants(plain) + [widen(col_taps, -radius % SUB)], axis=1)

    at = jnp.arange(size)
    edge = me_band * columns - radius + at
    col_mask = ((edge >= 0) & (edge < columns_all) & (at < columns + 2 * radius)).astype(F32)[None]
    at = jnp.arange(LANES)
    edge = me_row * height - radius + at
    row_mask = ((edge >= 0) & (edge < height * n_row) & (at < height + 2 * radius)).astype(F32)[None]
    part = group_size(bands, 16)
    whole = lambda shape: pl.BlockSpec(shape, lambda i: (0,) * len(shape))
    gr, gl = pl.pallas_call(
        functools.partial(gram_kernel, halo),
        grid=(bands // part,),
        in_specs=[
            pl.BlockSpec((part,) + taps_all.shape[1:], lambda i: (i, 0, 0)),
            whole((1, LANES)),
            whole((1, size)),
        ],
        out_specs=[
            pl.BlockSpec((part, height, LANES), lambda i: (i, 0, 0)),
            pl.BlockSpec((part, size, size), lambda i: (i, 0, 0)),
        ],
        out_shape=[
            jax.ShapeDtypeStruct((bands, height, LANES), BF),
            jax.ShapeDtypeStruct((bands, size, size), BF),
        ],
        compiler_params=pltpu.CompilerParams(vmem_limit_bytes=VMEM_LIMIT),
        cost_estimate=pl.CostEstimate(
            flops=bands * 2 * size**3, bytes_accessed=bands * size * size * 2, transcendentals=0
        ),
        name="gram",
    )(taps_all, row_mask, col_mask)

    few = group_size(bands_here, 32)
    span = round_up(columns_all, 2 * LANES)
    ext = height + 2 * radius
    chunks = ext // SUB
    mix = jnp.swapaxes(spread_basis(basis_here, few, kinds), 1, 2)
    summed = pl.pallas_call(
        functools.partial(adjoint_kernel, columns_all, radius),
        grid=(bands_here // few,),
        in_specs=[
            pl.BlockSpec((few, height, columns_all), lambda i: (i, 0, 0)),
            pl.BlockSpec((few,) + taps_here.shape[1:], lambda i: (i, 0, 0)),
            pl.BlockSpec((1,) + mix.shape[1:], lambda i: (i, 0, 0)),
        ],
        out_specs=whole((ext, kinds, span)),
        out_shape=jax.ShapeDtypeStruct((ext, kinds, span), BF),
        scratch_shapes=[
            pltpu.VMEM((chunks, SUB * kinds, span), F32),
            pltpu.VMEM((chunks, few, SUB, span), F32),
            pltpu.VMEM((few, 4 * LANES, 2 * LANES), BF),
            pltpu.VMEM((few, 2, ext, height), BF),
        ],
        compiler_params=pltpu.CompilerParams(vmem_limit_bytes=VMEM_LIMIT),
        cost_estimate=pl.CostEstimate(
            flops=bands_here * 2 * 96 * 512 * 256, bytes_accessed=observed.size * 2, transcendentals=0
        ),
        name="adjoint",
    )(observed, taps_here, mix)

    half = kinds // 2
    keep = lax.dynamic_slice_in_dim(summed, core * half, half, 1)
    give = lax.dynamic_slice_in_dim(summed, (1 - core) * half, half, 1)
    pairs = [(i, i ^ 1) for i in range(n_band)]
    got = lax.ppermute(give, "band", pairs)
    pair = keep.astype(F32) + got.astype(F32)
    before, after = shift_both(pair[:radius].astype(BF), pair[ext - radius :].astype(BF), "row")
    rows = pair[radius : ext - radius]
    pad = ((0, height - radius), (0, 0), (0, 0))
    rows = rows + jnp.pad(before.astype(F32), pad) + jnp.pad(after.astype(F32), (pad[0][::-1],) + pad[1:])
    rows = jnp.pad(rows[:, :, :columns_all], ((0, 0), (0, 0), (halo, halo)))
    wide = 2 * columns + 2 * halo
    total = lax.dynamic_slice_in_dim(rows, chip * 2 * columns, wide, 2)
    for hop in range(1, chips):
        target = (chip + hop) % chips
        piece = lax.dynamic_slice_in_dim(rows, target * 2 * columns, wide, 2).astype(BF)
        moves = [(i, (i + 2 * hop) % n_band) for i in range(n_band)]
        total = total + lax.ppermute(piece, "band", moves).astype(F32)
    other = lax.ppermute(total, "band", pairs)
    first = jnp.where(core == 0, total, other)
    second = jnp.where(core == 0, other, total)
    total = jnp.concatenate([first, second], axis=1)
    window = lax.dynamic_slice_in_dim(total, core * columns, columns + 2 * halo, 2)
    v0 = jnp.pad(window[:, :, halo : halo + columns], ((0, 0), (0, 0), (0, lanes - columns)))
    v0 = jnp.swapaxes(v0, 0, 1)
    window = jnp.pad(window.astype(BF), ((0, 0), (0, 0), (0, lanes - columns - 2 * halo)))

    group = group_size(bands, 32)
    sk = spread_basis(basis_all, group, kinds)
    pk = component_first(sk, kinds)
    ridge = jnp.broadcast_to(ridge_weights[:, None, None], (kinds, SUB, lanes))
    tall = height + 2 * halo
    block = lambda shape: pl.BlockSpec((group,) + shape, lambda i: (i, 0, 0))

    def normal_map(window, own, first):
        before, after = shift_both(window[:halo], window[height - halo :], "row")
        cells = jnp.concatenate([before, window, after], axis=0)
        return pl.pallas_call(
            functools.partial(normal_kernel, columns, first),
            grid=(bands // group,),
            in_specs=[
                whole((tall, kinds, lanes)),
                whole((kinds, height, lanes)),
                whole((kinds, SUB, lanes)),
                pl.BlockSpec((1,) + sk.shape[1:], lambda i: (i, 0, 0)),
                pl.BlockSpec((1,) + pk.shape[1:], lambda i: (i, 0, 0)),
                block((height, LANES)),
                block((size, size)),
            ],
            out_specs=[whole((kinds, height, lanes)), whole((SUB, LANES))],
            out_shape=[
                jax.ShapeDtypeStruct((kinds, height, lanes), F32),
                jax.ShapeDtypeStruct((SUB, LANES), F32),
            ],
            scratch_shapes=[
                pltpu.VMEM((height // SUB, SUB * kinds, lanes), F32),
                pltpu.VMEM((group, LANES, lanes), BF),
                pltpu.VMEM((height // SUB, group, SUB, lanes), F32),
            ],
            compiler_params=pltpu.CompilerParams(vmem_limit_bytes=VMEM_LIMIT),
            cost_estimate=pl.CostEstimate(
                flops=bands * 2 * 32 * 512 * 256, bytes_accessed=bands * size * size * 2, transcendentals=0
            ),
            name="normal",
        )(cells, own, ridge, sk, pk, gr, gl)

    v1, sums1 = normal_map(window, v0, True)
    near = jnp.swapaxes(v1[:, :, :columns].astype(BF), 0, 1)
    before, after = shift_both(near[:, :, :halo], near[:, :, columns - halo :], "band")
    window = jnp.concatenate(
        [before, near, after, jnp.zeros((height, kinds, lanes - columns - 2 * halo), BF)], axis=2
    )
    v2, sums2 = normal_map(window, v1, False)

    sums = jnp.concatenate([sums1[:3], sums2[:1], jnp.zeros((SUB - 4, LANES), F32)])
    mine = jnp.broadcast_to(sums[None], (n_band * n_row, SUB, LANES))
    shared = lax.all_to_all(mine, ("band", "row"), 0, 0, tiled=True)
    out = jax.ShapeDtypeStruct((kinds, height, columns), F32)
    return pl.pallas_call(
        combine_kernel,
        out_shape=[out, out],
        compiler_params=pltpu.CompilerParams(vmem_limit_bytes=VMEM_LIMIT),
        name="combine",
    )(shared, v0, v1, v2)


def solution(mesh):
    in_specs = (P("band", "row", None), P("band", None), P("band", None), P(), P())
    out_specs = (P(None, "row", "band"), P(None, "row", "band"))
    return jax.shard_map(local, mesh=mesh, in_specs=in_specs, out_specs=out_specs, check_vma=False)
```

```python
import functools

import jax
import jax.numpy as jnp
from jax import lax
from jax.experimental import pallas as pl
from jax.experimental.pallas import tpu as pltpu
from jax.sharding import PartitionSpec as P

LANES = 128
SUB = 8
BF = jnp.bfloat16
F32 = jnp.float32
VMEM_LIMIT = 50 * 1024 * 1024


def round_up(value, unit):
    return (value + unit - 1) // unit * unit


def group_size(count, most):
    return max(size for size in range(1, most + 1) if count % size == 0)


def packed_blocks(columns, halo):
    out = []
    for first in range(0, columns, LANES):
        out.append((first, round_up(min(first + LANES, columns) + 2 * halo, 2 * SUB)))
    return out


def dot(lhs, rhs):
    return lax.dot_general(lhs, rhs, (((1,), (0,)), ((), ())), preferred_element_type=F32)


def toeplitz(taps, rows, shift):
    lanes = taps.shape[1]
    pieces = []
    for first in range(0, rows, LANES):
        count = min(LANES, rows - first)
        wide = jnp.broadcast_to(taps, (count, lanes))
        pieces.append(pltpu.roll(wide, (shift + first) % lanes, 1, stride=1, stride_axis=0))
    return jnp.concatenate(pieces, axis=0) if len(pieces) > 1 else pieces[0]


def spread_basis(basis, group, kinds):
    bands = basis.shape[0]
    rows = jnp.arange(bands * SUB)
    lanes = jnp.arange(SUB * kinds)
    up = (rows[:, None] // SUB == jnp.arange(bands)[None, :]).astype(BF)
    out = (jnp.arange(kinds)[:, None] == lanes[None, :] % kinds).astype(BF)
    same = (rows[:, None] % SUB) == (lanes[None, :] // kinds)
    wide = dot(dot(up, basis).astype(BF), out)
    return jnp.where(same, wide, 0.0).astype(BF).reshape(bands // group, group * SUB, SUB * kinds)


def component_first(spread, kinds):
    groups, deep, _ = spread.shape
    split = spread.reshape(groups, deep, SUB, kinds)
    return split.transpose(0, 3, 2, 1).reshape(groups, kinds * SUB, deep)


def adjoint_kernel(columns, radius, obs_ref, taps_ref, mix_ref, out_ref, acc, ys, mats, rows):
    step = pl.program_id(0)
    group, height, _ = obs_ref.shape
    span = ys.shape[3]
    width = 2 * LANES
    tiles = span // width
    chunks = ys.shape[0]
    ext = chunks * SUB
    edge = 2 * SUB
    last = columns // LANES * LANES
    batch = group_size(group, 4)

    @pl.when(step == 0)
    def _():
        acc[...] = jnp.zeros_like(acc)
        mats[...] = jnp.zeros_like(mats)

    @pl.loop(0, group, step=batch)
    def _(start):
        near = lax.broadcasted_iota(jnp.int32, (edge, width), 1) < LANES
        blank = jnp.zeros((edge, width), BF)
        for b in range(batch):
            b = start + b
            ring = toeplitz(taps_ref[b, 4:5], width, -round_up(radius, SUB)).astype(BF)
            top, bottom = ring[:edge], ring[width - edge :]
            mats[b, LANES - edge : LANES] = jnp.where(near, bottom, blank)
            mats[b, LANES : LANES + edge] = jnp.where(near, top, blank)
            mats[b, LANES + edge : LANES + width - edge] = ring[edge : width - edge]
            mats[b, LANES + width - edge : LANES + width] = jnp.where(near, blank, bottom)
            mats[b, LANES + width : LANES + width + edge] = jnp.where(near, blank, top)
            reach = toeplitz(taps_ref[b, 1:2, :LANES], ext, -2 * radius)[:, :height]
            high = reach.astype(BF)
            rows[b, 0] = high
            rows[b, 1] = (reach - high.astype(F32)).astype(BF)

    @pl.loop(0, group, step=batch)
    def _(start):
        fields = []
        for b in range(batch):
            cells = obs_ref[start + b]
            pieces = [jnp.zeros((height, LANES), BF), cells[:, :last]]
            if columns > last:
                fill = jnp.zeros((height, LANES - (columns - last)), BF)
                pieces.append(jnp.concatenate([cells[:, last:], fill], axis=1))
            have = sum(piece.shape[1] for piece in pieces)
            if have < span + width:
                pieces.append(jnp.zeros((height, span + width - have), BF))
            padded = jnp.concatenate(pieces, axis=1)
            stacked = jnp.concatenate(
                [padded[:, t * width : t * width + 2 * width] for t in range(tiles)], axis=0
            )
            mixed = dot(stacked, mats[start + b]).astype(BF)
            fields.append(
                jnp.concatenate([mixed[t * height : (t + 1) * height] for t in range(tiles)], axis=1)
            )
        for b in range(batch):
            done = dot(rows[start + b, 0], fields[b]) + dot(rows[start + b, 1], fields[b])
            for c in range(chunks):
                ys[c, start + b] = done[c * SUB : (c + 1) * SUB]

    for c in range(chunks):
        cells = ys[c].reshape(group * SUB, span).astype(BF)
        acc[c] += dot(mix_ref[0], cells)

    @pl.when(step == pl.num_programs(0) - 1)
    def _():
        out_ref[...] = acc[...].reshape(out_ref.shape).astype(out_ref.dtype)


def gram_kernel(columns, halo, taps_ref, row_mask_ref, col_mask_ref, gr_ref, gl_ref):
    group, height, row_lanes = gr_ref.shape
    size = col_mask_ref.shape[1]
    blocks = packed_blocks(columns, halo)
    tall = max(end for _, end in blocks)
    inner = round_up(columns + halo, 2 * SUB)
    for b in range(group):
        left = (toeplitz(taps_ref[b, 3:4, :size], tall, -halo) * col_mask_ref[...]).astype(BF)
        right = toeplitz(taps_ref[b, 2:3, :size], inner, -halo).astype(BF)
        right = jnp.concatenate([right, jnp.zeros((size - inner, size), BF)], axis=0)
        done = dot(left, right).astype(BF)
        at = 0
        for i, (start, end) in enumerate(blocks):
            gl_ref[b, at : at + end - start] = done[start:end, i * LANES : (i + 1) * LANES]
            at += end - start
        left = (toeplitz(taps_ref[b, 1:2, :row_lanes], height, 0) * row_mask_ref[...]).astype(BF)
        right = toeplitz(taps_ref[b, 0:1, :row_lanes], row_lanes, 0).astype(BF)
        gr_ref[b] = dot(left, right).astype(BF)


def normal_kernel(
    columns, halo, first, p_ref, own_ref, ridge_ref, sk_ref, pk_ref, gr_ref, gl_ref, out_ref, sums_ref, acc, xs, ys
):
    step = pl.program_id(0)
    group, height, _ = gr_ref.shape
    ext, kinds, lanes = p_ref.shape
    chunks = height // SUB

    @pl.when(step == 0)
    def _():
        acc[...] = jnp.zeros_like(acc)

    for c in range(0, ext, 2 * SUB):
        halves = []
        for s in (c, c + SUB):
            cells = p_ref[s : s + SUB].reshape(SUB * kinds, lanes)
            halves.append(dot(sk_ref[0], cells).reshape(group, SUB, lanes))
        xs[:, c : c + 2 * SUB, :] = jnp.concatenate(halves, axis=1).astype(BF)

    blocks = packed_blocks(columns, halo)
    mids = [dot(gr_ref[b, :, :ext], xs[b]).astype(BF) for b in range(group)]
    for b in range(group):
        parts = []
        at = 0
        for i in range(lanes // LANES):
            if i < len(blocks):
                start, end = blocks[i]
                part = [gl_ref[b, at : at + end - start]]
                at += end - start
                if start:
                    part = [jnp.zeros((start, LANES), BF)] + part
                if end < lanes:
                    part = part + [jnp.zeros((lanes - end, LANES), BF)]
                parts.append(jnp.concatenate(part, axis=0))
            else:
                parts.append(jnp.zeros((lanes, LANES), BF))
        done = dot(mids[b], jnp.concatenate(parts, axis=1))
        for c in range(chunks):
            ys[c, b] = done[c * SUB : (c + 1) * SUB]

    for c in range(chunks):
        acc[c] += dot(pk_ref[0], ys[c].reshape(group * SUB, lanes).astype(BF))

    @pl.when(step == pl.num_programs(0) - 1)
    def _():
        lane = lax.broadcasted_iota(jnp.int32, (kinds, SUB, lanes), 2)
        totals = [jnp.zeros((SUB, lanes), F32) for _ in range(3)]
        for c in range(chunks):
            own = own_ref[:, c * SUB : (c + 1) * SUB, :]
            image = acc[c].reshape(kinds, SUB, lanes) + ridge_ref[...] * own
            image = jnp.where(lane < columns, image, 0.0)
            out_ref[:, c * SUB : (c + 1) * SUB, :] = image
            pairs = [own * image]
            if first:
                pairs += [own * own, image * image]
            for i, pair in enumerate(pairs):
                totals[i] = totals[i] + jnp.sum(pair, axis=0)
        flat = [
            jnp.sum(
                jnp.concatenate(
                    [total[:, i : i + LANES] for i in range(0, lanes, LANES)], axis=0
                ),
                axis=0,
                keepdims=True,
            )
            for total in totals
        ]
        row = lax.broadcasted_iota(jnp.int32, (SUB, LANES), 0)
        packed = jnp.zeros((SUB, LANES), F32)
        for i, line in enumerate(flat):
            packed = packed + jnp.where(row == i, jnp.broadcast_to(line, (SUB, LANES)), 0.0)
        sums_ref[...] = packed


def combine_kernel(shared_ref, v0_ref, v1_ref, v2_ref, coef_ref, res_ref):
    columns = coef_ref.shape[2]
    lines = jnp.sum(shared_ref[...], axis=0)
    v01, v00, v11, v12 = [jnp.sum(lines[i : i + 1], axis=1, keepdims=True) for i in range(4)]
    alpha = v00 / v01
    norm = v00 - 2.0 * alpha * v01 + alpha * alpha * v11
    lead = 1.0 + norm / v00
    product = lead * lead * v01 - 2.0 * lead * alpha * v11 + alpha * alpha * v12
    second = norm / product
    one = alpha + second * lead
    two = second * alpha
    for k in range(coef_ref.shape[0]):
        v0, v1, v2 = v0_ref[k], v1_ref[k], v2_ref[k]
        coef_ref[k] = (one * v0 - two * v1)[:, :columns]
        res_ref[k] = (v0 - one * v1 + two * v2)[:, :columns]


def shift_both(low_edge, high_edge, axis):
    count = lax.axis_size(axis)
    from_before = lax.ppermute(high_edge, axis, [(i, i + 1) for i in range(count - 1)])
    from_after = lax.ppermute(low_edge, axis, [(i + 1, i) for i in range(count - 1)])
    return from_before, from_after


def local(observed, row_taps, col_taps, spectral_basis, ridge_weights):
    bands_here, height, columns_all = observed.shape
    taps = row_taps.shape[1]
    radius = (taps - 1) // 2
    halo = 2 * radius
    bands, kinds = spectral_basis.shape
    n_band = lax.axis_size("band")
    n_row = lax.axis_size("row")
    columns = columns_all // n_band
    lanes = round_up(columns + 2 * halo, 2 * LANES)
    me_band = lax.axis_index("band")
    me_row = lax.axis_index("row")
    core = me_band % 2
    chip = me_band // 2
    chips = n_band // 2

    size = lanes

    def widen(values, lead=0):
        return jnp.pad(values, ((0, 0), (lead, 2 * LANES - taps - lead)))[:, None]

    plain = jnp.concatenate([row_taps, col_taps], axis=1)
    everyone = [(plain, me_band)]
    for hop in range(1, n_band):
        moves = [(i, (i + hop) % n_band) for i in range(n_band)]
        everyone.append((lax.ppermute(plain, "band", moves), (me_band - hop) % n_band))
    basis_here = lax.dynamic_slice_in_dim(spectral_basis, me_band * bands_here, bands_here, 0)
    basis_all = jnp.concatenate(
        [lax.dynamic_slice_in_dim(spectral_basis, at * bands_here, bands_here, 0) for _, at in everyone]
    )
    every = jnp.concatenate([values for values, _ in everyone])

    def variants(values):
        row, col = values[:, :taps], values[:, taps:]
        return [widen(row), widen(row[:, ::-1]), widen(col), widen(col[:, ::-1])]

    taps_here = jnp.concatenate(variants(plain) + [widen(col_taps, -radius % SUB)], axis=1)

    whole = lambda shape: pl.BlockSpec(shape, lambda i: (0,) * len(shape))

    few = group_size(bands_here, 32)
    span = round_up(columns_all, 2 * LANES)
    ext = height + 2 * radius
    chunks = ext // SUB
    mix = jnp.swapaxes(spread_basis(basis_here, few, kinds), 1, 2)
    summed = pl.pallas_call(
        functools.partial(adjoint_kernel, columns_all, radius),
        grid=(bands_here // few,),
        in_specs=[
            pl.BlockSpec((few, height, columns_all), lambda i: (i, 0, 0)),
            pl.BlockSpec((few,) + taps_here.shape[1:], lambda i: (i, 0, 0)),
            pl.BlockSpec((1,) + mix.shape[1:], lambda i: (i, 0, 0)),
        ],
        out_specs=whole((ext, kinds, span)),
        out_shape=jax.ShapeDtypeStruct((ext, kinds, span), BF),
        scratch_shapes=[
            pltpu.VMEM((chunks, SUB * kinds, span), F32),
            pltpu.VMEM((chunks, few, SUB, span), F32),
            pltpu.VMEM((few, 4 * LANES, 2 * LANES), BF),
            pltpu.VMEM((few, 2, ext, height), BF),
        ],
        compiler_params=pltpu.CompilerParams(vmem_limit_bytes=VMEM_LIMIT),
        cost_estimate=pl.CostEstimate(
            flops=bands_here * 2 * 96 * 512 * 256, bytes_accessed=observed.size * 2, transcendentals=0
        ),
        name="adjoint",
    )(observed, taps_here, mix)

    summed, every = lax.optimization_barrier((summed, every))
    taps_all = jnp.concatenate(variants(every), axis=1)

    at = jnp.arange(size)
    edge = me_band * columns - radius + at
    col_mask = ((edge >= 0) & (edge < columns_all) & (at < columns + 2 * radius)).astype(F32)[None]
    at = jnp.arange(LANES)
    edge = me_row * height - radius + at
    row_mask = ((edge >= 0) & (edge < height * n_row) & (at < height + 2 * radius)).astype(F32)[None]
    part = group_size(bands, 16)
    deep = sum(end - start for start, end in packed_blocks(columns, halo))
    gr, gl = pl.pallas_call(
        functools.partial(gram_kernel, columns, halo),
        grid=(bands // part,),
        in_specs=[
            pl.BlockSpec((part,) + taps_all.shape[1:], lambda i: (i, 0, 0)),
            whole((1, LANES)),
            whole((1, size)),
        ],
        out_specs=[
            pl.BlockSpec((part, height, LANES), lambda i: (i, 0, 0)),
            pl.BlockSpec((part, deep, LANES), lambda i: (i, 0, 0)),
        ],
        out_shape=[
            jax.ShapeDtypeStruct((bands, height, LANES), BF),
            jax.ShapeDtypeStruct((bands, deep, LANES), BF),
        ],
        compiler_params=pltpu.CompilerParams(vmem_limit_bytes=VMEM_LIMIT),
        cost_estimate=pl.CostEstimate(
            flops=bands * 2 * size**3, bytes_accessed=bands * deep * LANES * 2, transcendentals=0
        ),
        name="gram",
    )(taps_all, row_mask, col_mask)

    half = kinds // 2
    keep = lax.dynamic_slice_in_dim(summed, core * half, half, 1)
    give = lax.dynamic_slice_in_dim(summed, (1 - core) * half, half, 1)
    pairs = [(i, i ^ 1) for i in range(n_band)]
    got = lax.ppermute(give, "band", pairs)
    pair = keep.astype(F32) + got.astype(F32)
    wide = min(columns_all, 2 * columns + (2 * halo if chips > 2 else halo))

    def window_start(which):
        return jnp.clip(2 * columns * which - halo, 0, columns_all - wide)

    def moves(hop, step):
        return [
            (b * n_row + r, (b + 2 * hop) % n_band * n_row + r + step)
            for b in range(n_band)
            for r in range(n_row)
            if 0 <= r + step < n_row
        ]

    total = None
    for hop in range(chips):
        piece = lax.dynamic_slice_in_dim(pair, window_start((chip + hop) % chips), wide, 2)
        above, here, below = piece[:radius], piece[radius : ext - radius], piece[ext - radius :]
        axes = ("band", "row")
        after = lax.ppermute(above.astype(BF), axes, moves(hop, -1)).astype(F32)
        before = lax.ppermute(below.astype(BF), axes, moves(hop, 1)).astype(F32)
        if hop:
            here = lax.ppermute(here.astype(BF), axes, moves(hop, 0)).astype(F32)
        rest = jnp.zeros((height - radius,) + here.shape[1:], F32)
        here = here + jnp.concatenate([before, rest]) + jnp.concatenate([rest, after])
        total = here if total is None else total + here
    other = lax.ppermute(total, "band", pairs)
    first = jnp.where(core == 0, total, other)
    second = jnp.where(core == 0, other, total)
    total = jnp.concatenate([first, second], axis=1)
    total = jnp.pad(total, ((0, 0), (0, 0), (halo, halo)))
    window = lax.dynamic_slice_in_dim(total, me_band * columns - window_start(chip), columns + 2 * halo, 2)
    v0 = jnp.pad(window[:, :, halo : halo + columns], ((0, 0), (0, 0), (0, lanes - columns)))
    v0 = jnp.swapaxes(v0, 0, 1)
    window = jnp.pad(window.astype(BF), ((0, 0), (0, 0), (0, lanes - columns - 2 * halo)))

    group = group_size(bands, 32)
    sk = spread_basis(basis_all, group, kinds)
    pk = component_first(sk, kinds)
    ridge = jnp.broadcast_to(ridge_weights[:, None, None], (kinds, SUB, lanes))
    tall = height + 2 * halo
    block = lambda shape: pl.BlockSpec((group,) + shape, lambda i: (i, 0, 0))

    def normal_map(window, own, first):
        before, after = shift_both(window[:halo], window[height - halo :], "row")
        cells = jnp.concatenate([before, window, after], axis=0)
        return pl.pallas_call(
            functools.partial(normal_kernel, columns, halo, first),
            grid=(bands // group,),
            in_specs=[
                whole((tall, kinds, lanes)),
                whole((kinds, height, lanes)),
                whole((kinds, SUB, lanes)),
                pl.BlockSpec((1,) + sk.shape[1:], lambda i: (i, 0, 0)),
                pl.BlockSpec((1,) + pk.shape[1:], lambda i: (i, 0, 0)),
                block((height, LANES)),
                block((deep, LANES)),
            ],
            out_specs=[whole((kinds, height, lanes)), whole((SUB, LANES))],
            out_shape=[
                jax.ShapeDtypeStruct((kinds, height, lanes), F32),
                jax.ShapeDtypeStruct((SUB, LANES), F32),
            ],
            scratch_shapes=[
                pltpu.VMEM((height // SUB, SUB * kinds, lanes), F32),
                pltpu.VMEM((group, tall, lanes), BF),
                pltpu.VMEM((height // SUB, group, SUB, lanes), F32),
            ],
            compiler_params=pltpu.CompilerParams(vmem_limit_bytes=VMEM_LIMIT),
            cost_estimate=pl.CostEstimate(
                flops=bands * 2 * 32 * 512 * 256, bytes_accessed=bands * deep * LANES * 2, transcendentals=0
            ),
            name="normal",
        )(cells, own, ridge, sk, pk, gr, gl)

    v1, sums1 = normal_map(window, v0, True)
    near = jnp.swapaxes(v1[:, :, :columns].astype(BF), 0, 1)
    before, after = shift_both(near[:, :, :halo], near[:, :, columns - halo :], "band")
    window = jnp.concatenate(
        [before, near, after, jnp.zeros((height, kinds, lanes - columns - 2 * halo), BF)], axis=2
    )
    v2, sums2 = normal_map(window, v1, False)

    sums = jnp.concatenate([sums1[:3], sums2[:1], jnp.zeros((SUB - 4, LANES), F32)])
    mine = jnp.broadcast_to(sums[None], (n_band * n_row, SUB, LANES))
    shared = lax.all_to_all(mine, ("band", "row"), 0, 0, tiled=True)
    out = jax.ShapeDtypeStruct((kinds, height, columns), F32)
    return pl.pallas_call(
        combine_kernel,
        out_shape=[out, out],
        compiler_params=pltpu.CompilerParams(vmem_limit_bytes=VMEM_LIMIT),
        name="combine",
    )(shared, v0, v1, v2)


def solution(mesh):
    in_specs = (P("band", "row", None), P("band", None), P("band", None), P(), P())
    out_specs = (P(None, "row", "band"), P(None, "row", "band"))
    return jax.shard_map(local, mesh=mesh, in_specs=in_specs, out_specs=out_specs, check_vma=False)
```

```python
import functools

import jax
import jax.numpy as jnp
from jax import lax
from jax.experimental import pallas as pl
from jax.experimental.pallas import tpu as pltpu
from jax.sharding import PartitionSpec as P

LANES = 128
SUB = 8
BF = jnp.bfloat16
F32 = jnp.float32
VMEM_LIMIT = 50 * 1024 * 1024


def round_up(value, unit):
    return (value + unit - 1) // unit * unit


def group_size(count, most):
    return max(size for size in range(1, most + 1) if count % size == 0)


def packed_blocks(columns, halo):
    out = []
    for first in range(0, columns, LANES):
        out.append((first, round_up(min(first + LANES, columns) + 2 * halo, 2 * SUB)))
    return out


def dot(lhs, rhs):
    return lax.dot_general(lhs, rhs, (((1,), (0,)), ((), ())), preferred_element_type=F32)


def toeplitz(taps, rows, shift):
    lanes = taps.shape[1]
    pieces = []
    for first in range(0, rows, LANES):
        count = min(LANES, rows - first)
        wide = jnp.broadcast_to(taps, (count, lanes))
        pieces.append(pltpu.roll(wide, (shift + first) % lanes, 1, stride=1, stride_axis=0))
    return jnp.concatenate(pieces, axis=0) if len(pieces) > 1 else pieces[0]


def chosen(shape, rule, kind=BF):
    row = lax.broadcasted_iota(jnp.int32, shape, 0)
    lane = lax.broadcasted_iota(jnp.int32, shape, 1)
    return jnp.where(rule(row, lane), 1.0, 0.0).astype(kind)


def placed_taps(both, places, kind):
    count = both.shape[1] // 2
    picks = []
    for first, lead, flip in places:

        def rule(row, lane):
            at = lane - lead
            here = (at >= 0) & (at < count)
            return here & (row == first + (count - 1 - at if flip else at))

        picks.append(chosen((both.shape[1], 2 * LANES), rule, kind))
    done = lax.dot_general(
        both.astype(kind),
        jnp.concatenate(picks, axis=1),
        (((1,), (0,)), ((), ())),
        precision=lax.Precision.HIGHEST if kind == F32 else None,
        preferred_element_type=F32,
    )
    return [done[:, i * 2 * LANES : (i + 1) * 2 * LANES] for i in range(len(places))]


def dot_rows(lhs, rhs):
    return lax.dot_general(lhs, rhs, (((1,), (1,)), ((), ())), preferred_element_type=F32)


def strip_plan(rows, width):
    beside = max(n for n in range(1, rows + 1) if rows % n == 0 and n * width <= LANES)
    return beside, rows // beside


def turn_lanes(cells, amount):
    rows, kinds, lanes = cells.shape
    flat = pltpu.roll(cells.reshape(rows * kinds, lanes), amount % lanes, 1)
    return flat.reshape(rows, kinds, lanes)


def keep_lanes(cells, first, width):
    lane = lax.broadcasted_iota(jnp.int32, cells.shape, 2)
    return jnp.where((lane >= first) & (lane < first + width), cells, 0.0)


def packed_strip(cells, first, width):
    beside, rows = strip_plan(cells.shape[0], width)
    total = None
    for g in range(beside):
        part = turn_lanes(cells[g * rows : (g + 1) * rows], g * width - first)[:, :, :LANES]
        part = keep_lanes(part, g * width, width)
        total = part if total is None else total + part
    return total


def unpacked_strip(packed, count, width, first, lanes):
    beside, rows = strip_plan(count, width)
    wide = packed.astype(F32)
    if lanes > LANES:
        rest = jnp.zeros(packed.shape[:2] + (lanes - LANES,), F32)
        wide = jnp.concatenate([wide, rest], axis=2)
    return jnp.concatenate(
        [keep_lanes(turn_lanes(wide, first - g * width), first, width) for g in range(beside)], axis=0
    )


def main_rows(columns, halo):
    full = columns // LANES
    rest = columns - full * LANES
    return full * halo + (strip_plan(halo, rest)[1] if rest else 0)


def packed_main(cells, columns):
    full = columns // LANES
    rest = columns - full * LANES
    parts = [cells[:, :, t * LANES : (t + 1) * LANES] for t in range(full)]
    if rest:
        parts.append(packed_strip(cells, full * LANES, rest))
    return jnp.concatenate(parts, axis=0)


def unpacked_main(packed, columns, halo, lanes):
    full = columns // LANES
    rest = columns - full * LANES
    kinds = packed.shape[1]
    total = jnp.zeros((halo, kinds, lanes), F32)
    for t in range(full):
        part = packed[t * halo : (t + 1) * halo]
        total = total + unpacked_wide(part, t * LANES + halo, lanes)
    if rest:
        total = total + unpacked_strip(packed[full * halo :], halo, rest, full * LANES + halo, lanes)
    return total


def unpacked_wide(part, first, lanes):
    wide = part.astype(F32)
    if lanes > LANES:
        rest = jnp.zeros(part.shape[:2] + (lanes - LANES,), F32)
        wide = jnp.concatenate([wide, rest], axis=2)
    return turn_lanes(wide, first)


def pack_kernel(columns, halo, near_ref, up_ref, down_ref, left_ref, right_ref):
    cells = near_ref[...].astype(F32)
    height = cells.shape[0]
    up_ref[...] = packed_main(cells[:halo], columns).astype(BF)
    down_ref[...] = packed_main(cells[height - halo :], columns).astype(BF)
    left_ref[...] = packed_strip(cells, 0, halo).astype(BF)
    right_ref[...] = packed_strip(cells, columns - halo, halo).astype(BF)


def window_pieces(columns, halo, near_ref, main_refs, side_refs, corner_refs, p_ref):
    height, _, lanes = near_ref.shape
    right = columns + halo
    own = turn_lanes(near_ref[...].astype(F32), halo)
    own = own + unpacked_strip(side_refs[0][...], height, halo, 0, lanes)
    own = own + unpacked_strip(side_refs[1][...], height, halo, right, lanes)
    p_ref[halo : halo + height] = own.astype(BF)
    rows = strip_plan(height, halo)[1]
    for main, corner, first, at in (
        (main_refs[0], corner_refs[0], height - halo, 0),
        (main_refs[1], corner_refs[1], 0, halo + height),
    ):
        total = unpacked_main(main[...], columns, halo, lanes)
        for packed, lane in ((corner[:rows], 0), (corner[rows:], right)):
            total = total + unpacked_strip(packed, height, halo, lane, lanes)[first : first + halo]
        p_ref[at : at + halo] = total.astype(BF)


def adjoint_kernel(
    columns, radius, place_ref, obs_ref, taps_ref, basis_ref, give_ref, keep_ref, acc, ys, mats, rows, lines
):
    step = pl.program_id(0)
    group, height, _ = obs_ref.shape
    span = ys.shape[3]
    width = 2 * LANES
    tiles = span // width
    chunks = ys.shape[0]
    ext = chunks * SUB
    edge = 2 * SUB
    last = columns // LANES * LANES
    batch = group_size(group, 4)

    @pl.when(step == 0)
    def _():
        acc[...] = jnp.zeros_like(acc)
        mats[...] = jnp.zeros_like(mats)
        both = taps_ref[...]
        taps = both.shape[1] // 2
        for i, line in enumerate(placed_taps(both, [(taps, -radius % SUB, False), (0, 0, True)], F32)):
            lines[i] = line[:, None]

    @pl.loop(0, group, step=batch)
    def _(start):
        near = lax.broadcasted_iota(jnp.int32, (edge, width), 1) < LANES
        blank = jnp.zeros((edge, width), BF)
        for b in range(batch):
            b = start + b
            ring = toeplitz(lines[0, step * group + b], width, -round_up(radius, SUB)).astype(BF)
            top, bottom = ring[:edge], ring[width - edge :]
            mats[b, LANES - edge : LANES] = jnp.where(near, bottom, blank)
            mats[b, LANES : LANES + edge] = jnp.where(near, top, blank)
            mats[b, LANES + edge : LANES + width - edge] = ring[edge : width - edge]
            mats[b, LANES + width - edge : LANES + width] = jnp.where(near, blank, bottom)
            mats[b, LANES + width : LANES + width + edge] = jnp.where(near, blank, top)
            reach = toeplitz(lines[1, step * group + b][:, :LANES], ext, -2 * radius)[:, :height]
            high = reach.astype(BF)
            rows[b, 0] = high
            rows[b, 1] = (reach - high.astype(F32)).astype(BF)

    @pl.loop(0, group, step=batch)
    def _(start):
        fields = []
        for b in range(batch):
            cells = obs_ref[start + b]
            pieces = [jnp.zeros((height, LANES), BF), cells[:, :last]]
            if columns > last:
                fill = jnp.zeros((height, LANES - (columns - last)), BF)
                pieces.append(jnp.concatenate([cells[:, last:], fill], axis=1))
            have = sum(piece.shape[1] for piece in pieces)
            if have < span + width:
                pieces.append(jnp.zeros((height, span + width - have), BF))
            padded = jnp.concatenate(pieces, axis=1)
            stacked = jnp.concatenate(
                [padded[:, t * width : t * width + 2 * width] for t in range(tiles)], axis=0
            )
            mixed = dot(stacked, mats[start + b]).astype(BF)
            fields.append(
                jnp.concatenate([mixed[t * height : (t + 1) * height] for t in range(tiles)], axis=1)
            )
        for b in range(batch):
            done = dot(rows[start + b, 0], fields[b]) + dot(rows[start + b, 1], fields[b])
            for c in range(chunks):
                ys[c, start + b] = done[c * SUB : (c + 1) * SUB]

    bands, kinds = basis_ref.shape
    first = place_ref[0] + step * group
    turn = place_ref[1]
    pick = chosen((SUB * kinds, kinds), lambda row, lane: lane == (row + turn) % kinds)
    wide = dot_rows(pick, basis_ref[...]).astype(BF)
    here = chosen((bands, group * SUB), lambda row, lane: row == first + lane // SUB)
    same = chosen((SUB * kinds, group * SUB), lambda row, lane: row // kinds == lane % SUB, F32)
    mix = (dot(wide, here) * same).astype(BF)
    for c in range(chunks):
        cells = ys[c].reshape(group * SUB, span).astype(BF)
        acc[c] += dot(mix, cells)

    @pl.when(step == pl.num_programs(0) - 1)
    def _():
        half = kinds // 2
        total = acc[...].reshape(ext, kinds, span).astype(BF)
        give_ref[...] = total[:, :half]
        keep_ref[...] = total[:, half:]


def gram_kernel(sizes, radius, place_ref, taps_ref, basis_ref, gr_ref, gl_ref, sk_ref, pk_ref):
    columns, columns_all, rows_all = sizes
    halo = 2 * radius
    group, height, row_lanes = gr_ref.shape
    size = 2 * LANES
    blocks = packed_blocks(columns, halo)
    tall = max(end for _, end in blocks)
    inner = round_up(columns + halo, 2 * SUB)
    both = taps_ref[...]
    taps = both.shape[1] // 2
    places = [(0, 0, False), (0, 0, True), (taps, 0, False), (taps, 0, True)]
    row_line, row_back, col_line, col_back = placed_taps(both, places, BF)
    row_line, row_back = row_line[:, :row_lanes], row_back[:, :row_lanes]

    def inside(lanes, first, count, limit):
        lane = lax.broadcasted_iota(jnp.int32, (1, lanes), 1)
        at = lane + first
        return jnp.where((at >= 0) & (at < limit) & (lane < count), 1.0, 0.0)

    col_mask = inside(size, place_ref[2], columns + halo, columns_all)
    row_mask = inside(row_lanes, place_ref[3], height + halo, rows_all)
    for b in range(group):
        left = (toeplitz(col_back[b : b + 1], tall, -halo) * col_mask).astype(BF)
        right = toeplitz(col_line[b : b + 1], inner, -halo).astype(BF)
        right = jnp.concatenate([right, jnp.zeros((size - inner, size), BF)], axis=0)
        done = dot(left, right).astype(BF)
        at = 0
        for i, (start, end) in enumerate(blocks):
            gl_ref[b, at : at + end - start] = done[start:end, i * LANES : (i + 1) * LANES]
            at += end - start
        left = (toeplitz(row_back[b : b + 1], height, 0) * row_mask).astype(BF)
        right = toeplitz(row_line[b : b + 1], row_lanes, 0).astype(BF)
        gr_ref[b] = dot(left, right).astype(BF)
    basis = basis_ref[...]
    kinds = basis.shape[1]
    up = chosen((group * SUB, group), lambda row, lane: row // SUB == lane)
    out = chosen((kinds, SUB * kinds), lambda row, lane: row == lane % kinds)
    same = chosen((group * SUB, SUB * kinds), lambda row, lane: row % SUB == lane // kinds, F32)
    sk_ref[...] = (dot(dot(up, basis).astype(BF), out) * same).astype(BF)
    up = chosen((SUB * kinds, kinds), lambda row, lane: row // SUB == lane)
    out = chosen((group, group * SUB), lambda row, lane: row == lane // SUB)
    same = chosen((SUB * kinds, group * SUB), lambda row, lane: row % SUB == lane % SUB, F32)
    pk_ref[0] = (dot(dot_rows(up, basis).astype(BF), out) * same).astype(BF)


def first_kernel(columns, halo, p_ref, *rest):
    normal_kernel(columns, halo, True, p_ref, *rest)


def second_kernel(columns, halo, near_ref, before, after, left, right, corner_before, corner_after, *rest):
    *rest, p_ref = rest

    @pl.when(pl.program_id(0) == 0)
    def _():
        window_pieces(
            columns, halo, near_ref, (before, after), (left, right), (corner_before, corner_after), p_ref
        )

    normal_kernel(columns, halo, False, p_ref, *rest)


def normal_kernel(
    columns, halo, first, p_ref, own_ref, ridge_ref, sk_ref, pk_ref, gr_ref, gl_ref, out_ref, sums_ref, acc, xs, ys
):
    step = pl.program_id(0)
    group, height, _ = gr_ref.shape
    ext, kinds, lanes = p_ref.shape
    chunks = height // SUB

    @pl.when(step == 0)
    def _():
        acc[...] = jnp.zeros_like(acc)

    for c in range(0, ext, 2 * SUB):
        halves = []
        for s in (c, c + SUB):
            cells = p_ref[s : s + SUB].reshape(SUB * kinds, lanes)
            halves.append(dot(sk_ref[...], cells).reshape(group, SUB, lanes))
        xs[:, c : c + 2 * SUB, :] = jnp.concatenate(halves, axis=1).astype(BF)

    blocks = packed_blocks(columns, halo)
    mids = [dot(gr_ref[b, :, :ext], xs[b]).astype(BF) for b in range(group)]
    for b in range(group):
        parts = []
        at = 0
        for i in range(lanes // LANES):
            if i < len(blocks):
                start, end = blocks[i]
                part = [gl_ref[b, at : at + end - start]]
                at += end - start
                if start:
                    part = [jnp.zeros((start, LANES), BF)] + part
                if end < lanes:
                    part = part + [jnp.zeros((lanes - end, LANES), BF)]
                parts.append(jnp.concatenate(part, axis=0))
            else:
                parts.append(jnp.zeros((lanes, LANES), BF))
        done = dot(mids[b], jnp.concatenate(parts, axis=1))
        for c in range(chunks):
            ys[c, b] = done[c * SUB : (c + 1) * SUB]

    gather = jnp.concatenate([pk_ref[i] for i in range(pk_ref.shape[0])], axis=1)
    for c in range(chunks):
        acc[c] += dot(gather, ys[c].reshape(group * SUB, lanes).astype(BF))

    @pl.when(step == pl.num_programs(0) - 1)
    def _():
        lane = lax.broadcasted_iota(jnp.int32, (kinds, SUB, lanes), 2)
        totals = [jnp.zeros((SUB, lanes), F32) for _ in range(3)]
        for c in range(chunks):
            own = own_ref[:, c * SUB : (c + 1) * SUB, :]
            image = acc[c].reshape(kinds, SUB, lanes) + ridge_ref[...] * own
            image = jnp.where(lane < columns, image, 0.0)
            out_ref[:, c * SUB : (c + 1) * SUB, :] = image
            pairs = [own * image]
            if first:
                pairs += [own * own, image * image]
            for i, pair in enumerate(pairs):
                totals[i] = totals[i] + jnp.sum(pair, axis=0)
        flat = [
            jnp.sum(
                jnp.concatenate(
                    [total[:, i : i + LANES] for i in range(0, lanes, LANES)], axis=0
                ),
                axis=0,
                keepdims=True,
            )
            for total in totals
        ]
        row = lax.broadcasted_iota(jnp.int32, (SUB, LANES), 0)
        packed = jnp.zeros((SUB, LANES), F32)
        for i, line in enumerate(flat):
            packed = packed + jnp.where(row == i, jnp.broadcast_to(line, (SUB, LANES)), 0.0)
        sums_ref[...] = packed


def combine_kernel(shared_ref, v0_ref, v1_ref, v2_ref, coef_ref, res_ref):
    columns = coef_ref.shape[2]
    lines = jnp.sum(shared_ref[...], axis=0)
    v01, v00, v11, v12 = [jnp.sum(lines[i : i + 1], axis=1, keepdims=True) for i in range(4)]
    alpha = v00 / v01
    norm = v00 - 2.0 * alpha * v01 + alpha * alpha * v11
    lead = 1.0 + norm / v00
    product = lead * lead * v01 - 2.0 * lead * alpha * v11 + alpha * alpha * v12
    second = norm / product
    one = alpha + second * lead
    two = second * alpha
    for k in range(coef_ref.shape[0]):
        v0, v1, v2 = v0_ref[k], v1_ref[k], v2_ref[k]
        coef_ref[k] = (one * v0 - two * v1)[:, :columns]
        res_ref[k] = (v0 - one * v1 + two * v2)[:, :columns]


def shift_both(low_edge, high_edge, axis):
    count = lax.axis_size(axis)
    from_before = lax.ppermute(high_edge, axis, [(i, i + 1) for i in range(count - 1)])
    from_after = lax.ppermute(low_edge, axis, [(i + 1, i) for i in range(count - 1)])
    return from_before, from_after


def local(observed, row_taps, col_taps, spectral_basis, ridge_weights):
    bands_here, height, columns_all = observed.shape
    taps = row_taps.shape[1]
    radius = (taps - 1) // 2
    halo = 2 * radius
    bands, kinds = spectral_basis.shape
    n_band = lax.axis_size("band")
    n_row = lax.axis_size("row")
    columns = columns_all // n_band
    lanes = round_up(columns + 2 * halo, 2 * LANES)
    me_band = lax.axis_index("band")
    me_row = lax.axis_index("row")
    core = me_band % 2
    chip = me_band // 2
    chips = n_band // 2

    plain = jnp.concatenate([row_taps, col_taps], axis=1)
    everyone = [(plain, me_band)]
    for hop in range(1, n_band):
        moves = [(i, (i + hop) % n_band) for i in range(n_band)]
        everyone.append((lax.ppermute(plain, "band", moves), (me_band - hop) % n_band))
    basis_all = jnp.concatenate(
        [lax.dynamic_slice_in_dim(spectral_basis, at * bands_here, bands_here, 0) for _, at in everyone]
    )
    every = jnp.concatenate([values for values, _ in everyone])

    half = kinds // 2
    place = jnp.stack(
        [me_band * bands_here, half * (1 - core), me_band * columns - radius, me_row * height - radius]
    ).astype(jnp.int32)
    whole = lambda shape: pl.BlockSpec(shape, lambda i: (0,) * len(shape))

    few = group_size(bands_here, 32)
    span = round_up(columns_all, 2 * LANES)
    ext = height + 2 * radius
    chunks = ext // SUB
    give, keep = pl.pallas_call(
        functools.partial(adjoint_kernel, columns_all, radius),
        grid=(bands_here // few,),
        in_specs=[
            pl.BlockSpec(memory_space=pltpu.SMEM),
            pl.BlockSpec((few, height, columns_all), lambda i: (i, 0, 0)),
            whole(plain.shape),
            whole((bands, kinds)),
        ],
        out_specs=[whole((ext, half, span))] * 2,
        out_shape=[jax.ShapeDtypeStruct((ext, half, span), BF)] * 2,
        scratch_shapes=[
            pltpu.VMEM((chunks, SUB * kinds, span), F32),
            pltpu.VMEM((chunks, few, SUB, span), F32),
            pltpu.VMEM((few, 4 * LANES, 2 * LANES), BF),
            pltpu.VMEM((few, 2, ext, height), BF),
            pltpu.VMEM((2, bands_here, 1, 2 * LANES), F32),
        ],
        compiler_params=pltpu.CompilerParams(vmem_limit_bytes=VMEM_LIMIT),
        cost_estimate=pl.CostEstimate(
            flops=bands_here * 2 * 96 * 512 * 256, bytes_accessed=observed.size * 2, transcendentals=0
        ),
        name="adjoint",
    )(place, observed, plain, spectral_basis)

    give, every = lax.optimization_barrier((give, every))

    part = group_size(bands, 32)
    deep = sum(end - start for start, end in packed_blocks(columns, halo))
    gr, gl, sk, pk = pl.pallas_call(
        functools.partial(gram_kernel, (columns, columns_all, height * n_row), radius),
        grid=(bands // part,),
        in_specs=[
            pl.BlockSpec(memory_space=pltpu.SMEM),
            pl.BlockSpec((part, 2 * taps), lambda i: (i, 0)),
            pl.BlockSpec((part, kinds), lambda i: (i, 0)),
        ],
        out_specs=[
            pl.BlockSpec((part, height, LANES), lambda i: (i, 0, 0)),
            pl.BlockSpec((part, deep, LANES), lambda i: (i, 0, 0)),
            pl.BlockSpec((part * SUB, SUB * kinds), lambda i: (i, 0)),
            pl.BlockSpec((1, SUB * kinds, part * SUB), lambda i: (i, 0, 0)),
        ],
        out_shape=[
            jax.ShapeDtypeStruct((bands, height, LANES), BF),
            jax.ShapeDtypeStruct((bands, deep, LANES), BF),
            jax.ShapeDtypeStruct((bands * SUB, SUB * kinds), BF),
            jax.ShapeDtypeStruct((bands // part, SUB * kinds, part * SUB), BF),
        ],
        compiler_params=pltpu.CompilerParams(vmem_limit_bytes=VMEM_LIMIT),
        cost_estimate=pl.CostEstimate(
            flops=bands * 2 * (2 * LANES) ** 3, bytes_accessed=bands * deep * LANES * 2, transcendentals=0
        ),
        name="gram",
    )(place, every, basis_all)

    pairs = [(i, i ^ 1) for i in range(n_band)]
    got = lax.ppermute(give, "band", pairs)
    pair = keep.astype(F32) + got.astype(F32)
    wide = min(columns_all, 2 * columns + (2 * halo if chips > 2 else halo))

    def window_start(which):
        return jnp.clip(2 * columns * which - halo, 0, columns_all - wide)

    def moves(hop, step):
        return [
            (b * n_row + r, (b + 2 * hop) % n_band * n_row + r + step)
            for b in range(n_band)
            for r in range(n_row)
            if 0 <= r + step < n_row
        ]

    total = None
    for hop in range(chips):
        piece = lax.dynamic_slice_in_dim(pair, window_start((chip + hop) % chips), wide, 2)
        above, here, below = piece[:radius], piece[radius : ext - radius], piece[ext - radius :]
        axes = ("band", "row")
        after = lax.ppermute(above.astype(BF), axes, moves(hop, -1)).astype(F32)
        before = lax.ppermute(below.astype(BF), axes, moves(hop, 1)).astype(F32)
        if hop:
            here = lax.ppermute(here.astype(BF), axes, moves(hop, 0)).astype(F32)
        rest = jnp.zeros((height - radius,) + here.shape[1:], F32)
        here = here + jnp.concatenate([before, rest]) + jnp.concatenate([rest, after])
        total = here if total is None else total + here
    other = lax.ppermute(total, "band", pairs)
    first = jnp.where(core == 0, total, other)
    second = jnp.where(core == 0, other, total)
    total = jnp.concatenate([first, second], axis=1)
    total = jnp.pad(total, ((0, 0), (0, 0), (halo, halo)))
    window = lax.dynamic_slice_in_dim(total, me_band * columns - window_start(chip), columns + 2 * halo, 2)
    v0 = jnp.pad(window[:, :, halo : halo + columns], ((0, 0), (0, 0), (0, lanes - columns)))
    v0 = jnp.swapaxes(v0, 0, 1)
    window = jnp.pad(window.astype(BF), ((0, 0), (0, 0), (0, lanes - columns - 2 * halo)))

    group = part
    ridge = jnp.broadcast_to(ridge_weights[:, None, None], (kinds, SUB, lanes))
    tall = height + 2 * halo
    block = lambda shape: pl.BlockSpec((group,) + shape, lambda i: (i, 0, 0))

    def normal_map(pieces, own, first):
        window = [pltpu.VMEM((tall, kinds, lanes), BF)] if not first else []
        return pl.pallas_call(
            functools.partial(first_kernel if first else second_kernel, columns, halo),
            grid=(bands // group,),
            in_specs=[whole(piece.shape) for piece in pieces]
            + [
                whole((kinds, height, lanes)),
                whole((kinds, SUB, lanes)),
                pl.BlockSpec((group * SUB, SUB * kinds), lambda i: (i, 0)),
                pl.BlockSpec((group // part, SUB * kinds, part * SUB), lambda i: (i, 0, 0)),
                block((height, LANES)),
                block((deep, LANES)),
            ],
            out_specs=[whole((kinds, height, lanes)), whole((SUB, LANES))],
            out_shape=[
                jax.ShapeDtypeStruct((kinds, height, lanes), F32),
                jax.ShapeDtypeStruct((SUB, LANES), F32),
            ],
            scratch_shapes=[
                pltpu.VMEM((height // SUB, SUB * kinds, lanes), F32),
                pltpu.VMEM((group, tall, lanes), BF),
                pltpu.VMEM((height // SUB, group, SUB, lanes), F32),
            ]
            + window,
            compiler_params=pltpu.CompilerParams(vmem_limit_bytes=VMEM_LIMIT),
            cost_estimate=pl.CostEstimate(
                flops=bands * 2 * 32 * 512 * 256, bytes_accessed=bands * deep * LANES * 2, transcendentals=0
            ),
            name="normal",
        )(*pieces, own, ridge, sk, pk, gr, gl)

    before, after = shift_both(window[:halo], window[height - halo :], "row")
    v1, sums1 = normal_map([jnp.concatenate([before, window, after], axis=0)], v0, True)
    near = jnp.swapaxes(v1.astype(BF), 0, 1)
    main = jax.ShapeDtypeStruct((main_rows(columns, halo), kinds, LANES), BF)
    side = jax.ShapeDtypeStruct((strip_plan(height, halo)[1], kinds, LANES), BF)
    up, down, left, right = pl.pallas_call(
        functools.partial(pack_kernel, columns, halo),
        out_shape=[main, main, side, side],
        compiler_params=pltpu.CompilerParams(vmem_limit_bytes=VMEM_LIMIT),
        name="pack",
    )(near)
    before, after = shift_both(up, down, "row")
    from_left, from_right = shift_both(left, right, "band")
    corners = jnp.concatenate([from_left, from_right], axis=0)
    corner_before, corner_after = shift_both(corners, corners, "row")
    pieces = [near, before, after, from_left, from_right, corner_before, corner_after]
    v2, sums2 = normal_map(pieces, v1, False)

    sums = jnp.concatenate([sums1[:3], sums2[:1], jnp.zeros((SUB - 4, LANES), F32)])
    mine = jnp.broadcast_to(sums[None], (n_band * n_row, SUB, LANES))
    shared = lax.all_to_all(mine, ("band", "row"), 0, 0, tiled=True)
    out = jax.ShapeDtypeStruct((kinds, height, columns), F32)
    return pl.pallas_call(
        combine_kernel,
        out_shape=[out, out],
        compiler_params=pltpu.CompilerParams(vmem_limit_bytes=VMEM_LIMIT),
        name="combine",
    )(shared, v0, v1, v2)


def solution(mesh):
    in_specs = (P("band", "row", None), P("band", None), P("band", None), P(), P())
    out_specs = (P(None, "row", "band"), P(None, "row", "band"))
    return jax.shard_map(local, mesh=mesh, in_specs=in_specs, out_specs=out_specs, check_vma=False)
```

```python
import functools

import jax
import jax.numpy as jnp
from jax import lax
from jax.experimental import pallas as pl
from jax.experimental.pallas import tpu as pltpu
from jax.sharding import PartitionSpec as P

LANES = 128
SUB = 8
BF = jnp.bfloat16
F32 = jnp.float32
VMEM_LIMIT = 50 * 1024 * 1024


def round_up(value, unit):
    return (value + unit - 1) // unit * unit


def group_size(count, most):
    return max(size for size in range(1, most + 1) if count % size == 0)


def packed_blocks(columns, halo):
    out = []
    for first in range(0, columns, LANES):
        out.append((first, round_up(min(first + LANES, columns) + 2 * halo, 2 * SUB)))
    return out


def dot(lhs, rhs):
    return lax.dot_general(lhs, rhs, (((1,), (0,)), ((), ())), preferred_element_type=F32)


def toeplitz(taps, rows, shift):
    lanes = taps.shape[1]
    pieces = []
    for first in range(0, rows, LANES):
        count = min(LANES, rows - first)
        wide = jnp.broadcast_to(taps, (count, lanes))
        pieces.append(pltpu.roll(wide, (shift + first) % lanes, 1, stride=1, stride_axis=0))
    return jnp.concatenate(pieces, axis=0) if len(pieces) > 1 else pieces[0]


def chosen(shape, rule, kind=BF):
    row = lax.broadcasted_iota(jnp.int32, shape, 0)
    lane = lax.broadcasted_iota(jnp.int32, shape, 1)
    return jnp.where(rule(row, lane), 1.0, 0.0).astype(kind)


def placed_taps(both, places, kind):
    count = both.shape[1] // 2
    picks = []
    for first, lead, flip in places:

        def rule(row, lane):
            at = lane - lead
            here = (at >= 0) & (at < count)
            return here & (row == first + (count - 1 - at if flip else at))

        picks.append(chosen((both.shape[1], 2 * LANES), rule, kind))
    done = lax.dot_general(
        both.astype(kind),
        jnp.concatenate(picks, axis=1),
        (((1,), (0,)), ((), ())),
        precision=lax.Precision.HIGHEST if kind == F32 else None,
        preferred_element_type=F32,
    )
    return [done[:, i * 2 * LANES : (i + 1) * 2 * LANES] for i in range(len(places))]


def dot_rows(lhs, rhs):
    return lax.dot_general(lhs, rhs, (((1,), (1,)), ((), ())), preferred_element_type=F32)


def strip_plan(rows, width):
    beside = max(n for n in range(1, rows + 1) if rows % n == 0 and n * width <= LANES)
    return beside, rows // beside


def turn_lanes(cells, amount):
    rows, kinds, lanes = cells.shape
    flat = pltpu.roll(cells.reshape(rows * kinds, lanes), amount % lanes, 1)
    return flat.reshape(rows, kinds, lanes)


def keep_lanes(cells, first, width):
    lane = lax.broadcasted_iota(jnp.int32, cells.shape, 2)
    return jnp.where((lane >= first) & (lane < first + width), cells, 0.0)


def packed_strip(cells, first, width):
    beside, rows = strip_plan(cells.shape[0], width)
    total = None
    for g in range(beside):
        part = turn_lanes(cells[g * rows : (g + 1) * rows], g * width - first)[:, :, :LANES]
        part = keep_lanes(part, g * width, width)
        total = part if total is None else total + part
    return total


def unpacked_strip(packed, count, width, first, lanes):
    beside, rows = strip_plan(count, width)
    wide = packed.astype(F32)
    if lanes > LANES:
        rest = jnp.zeros(packed.shape[:2] + (lanes - LANES,), F32)
        wide = jnp.concatenate([wide, rest], axis=2)
    return jnp.concatenate(
        [keep_lanes(turn_lanes(wide, first - g * width), first, width) for g in range(beside)], axis=0
    )


def main_rows(columns, halo):
    full = columns // LANES
    rest = columns - full * LANES
    return full * halo + (strip_plan(halo, rest)[1] if rest else 0)


def packed_main(cells, columns):
    full = columns // LANES
    rest = columns - full * LANES
    parts = [cells[:, :, t * LANES : (t + 1) * LANES] for t in range(full)]
    if rest:
        parts.append(packed_strip(cells, full * LANES, rest))
    return jnp.concatenate(parts, axis=0)


def unpacked_main(packed, columns, halo, lanes):
    full = columns // LANES
    rest = columns - full * LANES
    kinds = packed.shape[1]
    total = jnp.zeros((halo, kinds, lanes), F32)
    for t in range(full):
        part = packed[t * halo : (t + 1) * halo]
        total = total + unpacked_wide(part, t * LANES + halo, lanes)
    if rest:
        total = total + unpacked_strip(packed[full * halo :], halo, rest, full * LANES + halo, lanes)
    return total


def unpacked_wide(part, first, lanes):
    wide = part.astype(F32)
    if lanes > LANES:
        rest = jnp.zeros(part.shape[:2] + (lanes - LANES,), F32)
        wide = jnp.concatenate([wide, rest], axis=2)
    return turn_lanes(wide, first)


def pack_kernel(columns, halo, near_ref, up_ref, down_ref, left_ref, right_ref):
    cells = near_ref[...].astype(F32)
    height = cells.shape[0]
    up_ref[...] = packed_main(cells[:halo], columns).astype(BF)
    down_ref[...] = packed_main(cells[height - halo :], columns).astype(BF)
    left_ref[...] = packed_strip(cells, 0, halo).astype(BF)
    right_ref[...] = packed_strip(cells, columns - halo, halo).astype(BF)


def window_pieces(columns, halo, near_ref, main_refs, side_refs, corner_refs, p_ref):
    height, _, lanes = near_ref.shape
    right = columns + halo
    own = turn_lanes(near_ref[...].astype(F32), halo)
    own = own + unpacked_strip(side_refs[0][...], height, halo, 0, lanes)
    own = own + unpacked_strip(side_refs[1][...], height, halo, right, lanes)
    p_ref[halo : halo + height] = own.astype(BF)
    rows = strip_plan(height, halo)[1]
    for main, corner, first, at in (
        (main_refs[0], corner_refs[0], height - halo, 0),
        (main_refs[1], corner_refs[1], 0, halo + height),
    ):
        total = unpacked_main(main[...], columns, halo, lanes)
        for packed, lane in ((corner[:rows], 0), (corner[rows:], right)):
            total = total + unpacked_strip(packed, height, halo, lane, lanes)[first : first + halo]
        p_ref[at : at + halo] = total.astype(BF)


def adjoint_kernel(
    columns, radius, place_ref, obs_ref, taps_ref, basis_ref, give_ref, keep_ref, acc, ys, mats, rows, lines
):
    step = pl.program_id(0)
    group, height, _ = obs_ref.shape
    span = ys.shape[3]
    width = 2 * LANES
    tiles = span // width
    chunks = ys.shape[0]
    ext = chunks * SUB
    edge = 2 * SUB
    last = columns // LANES * LANES
    batch = group_size(group, 4)

    @pl.when(step == 0)
    def _():
        acc[...] = jnp.zeros_like(acc)
        mats[...] = jnp.zeros_like(mats)
        both = taps_ref[...]
        taps = both.shape[1] // 2
        for i, line in enumerate(placed_taps(both, [(taps, -radius % SUB, False), (0, 0, True)], F32)):
            lines[i] = line[:, None]

    @pl.loop(0, group, step=batch)
    def _(start):
        near = lax.broadcasted_iota(jnp.int32, (edge, width), 1) < LANES
        blank = jnp.zeros((edge, width), BF)
        for b in range(batch):
            b = start + b
            ring = toeplitz(lines[0, step * group + b], width, -round_up(radius, SUB)).astype(BF)
            top, bottom = ring[:edge], ring[width - edge :]
            mats[b, LANES - edge : LANES] = jnp.where(near, bottom, blank)
            mats[b, LANES : LANES + edge] = jnp.where(near, top, blank)
            mats[b, LANES + edge : LANES + width - edge] = ring[edge : width - edge]
            mats[b, LANES + width - edge : LANES + width] = jnp.where(near, blank, bottom)
            mats[b, LANES + width : LANES + width + edge] = jnp.where(near, blank, top)
            reach = toeplitz(lines[1, step * group + b][:, :LANES], ext, -2 * radius)[:, :height]
            high = reach.astype(BF)
            rows[b, 0] = high
            rows[b, 1] = (reach - high.astype(F32)).astype(BF)

    @pl.loop(0, group, step=batch)
    def _(start):
        fields = []
        for b in range(batch):
            cells = obs_ref[start + b]
            pieces = [jnp.zeros((height, LANES), BF), cells[:, :last]]
            if columns > last:
                fill = jnp.zeros((height, LANES - (columns - last)), BF)
                pieces.append(jnp.concatenate([cells[:, last:], fill], axis=1))
            have = sum(piece.shape[1] for piece in pieces)
            if have < span + width:
                pieces.append(jnp.zeros((height, span + width - have), BF))
            padded = jnp.concatenate(pieces, axis=1)
            stacked = jnp.concatenate(
                [padded[:, t * width : t * width + 2 * width] for t in range(tiles)], axis=0
            )
            mixed = dot(stacked, mats[start + b]).astype(BF)
            fields.append(
                jnp.concatenate([mixed[t * height : (t + 1) * height] for t in range(tiles)], axis=1)
            )
        for b in range(batch):
            done = dot(rows[start + b, 0], fields[b]) + dot(rows[start + b, 1], fields[b])
            for c in range(chunks):
                ys[c, start + b] = done[c * SUB : (c + 1) * SUB]

    bands, kinds = basis_ref.shape
    first = place_ref[0] + step * group
    turn = place_ref[1]
    pick = chosen((SUB * kinds, kinds), lambda row, lane: lane == (row + turn) % kinds)
    wide = dot_rows(pick, basis_ref[...]).astype(BF)
    here = chosen((bands, group * SUB), lambda row, lane: row == first + lane // SUB)
    same = chosen((SUB * kinds, group * SUB), lambda row, lane: row // kinds == lane % SUB, F32)
    mix = (dot(wide, here) * same).astype(BF)
    for c in range(chunks):
        cells = ys[c].reshape(group * SUB, span).astype(BF)
        acc[c] += dot(mix, cells)

    @pl.when(step == pl.num_programs(0) - 1)
    def _():
        half = kinds // 2
        total = acc[...].reshape(ext, kinds, span).astype(BF)
        give_ref[...] = total[:, :half]
        keep_ref[...] = total[:, half:]


def inside(lanes, first, count, limit):
    lane = lax.broadcasted_iota(jnp.int32, (1, lanes), 1)
    at = lane + first
    return jnp.where((at >= 0) & (at < limit) & (lane < count), 1.0, 0.0)


def gram_columns_kernel(columns, columns_all, radius, place_ref, taps_ref, gl_ref):
    halo = 2 * radius
    size = 2 * LANES
    blocks = packed_blocks(columns, halo)
    tall = max(end for _, end in blocks)
    inner = round_up(columns + halo, 2 * SUB)
    both = taps_ref[...]
    taps = both.shape[1] // 2
    line, back = placed_taps(both, [(taps, 0, False), (taps, 0, True)], BF)
    mask = inside(size, place_ref[2], columns + halo, columns_all)
    for b in range(both.shape[0]):
        left = (toeplitz(back[b : b + 1], tall, -halo) * mask).astype(BF)
        right = toeplitz(line[b : b + 1], inner, -halo).astype(BF)
        right = jnp.concatenate([right, jnp.zeros((size - inner, size), BF)], axis=0)
        done = dot(left, right).astype(BF)
        at = 0
        for i, (start, end) in enumerate(blocks):
            gl_ref[b, at : at + end - start] = done[start:end, i * LANES : (i + 1) * LANES]
            at += end - start


def gram_rows_kernel(rows_all, radius, place_ref, taps_ref, basis_ref, gr_ref, sk_ref, pk_ref):
    halo = 2 * radius
    group, height, lanes = gr_ref.shape
    both = taps_ref[...]
    line, back = [part[:, :lanes] for part in placed_taps(both, [(0, 0, False), (0, 0, True)], BF)]
    mask = inside(lanes, place_ref[3], height + halo, rows_all)
    for b in range(group):
        left = (toeplitz(back[b : b + 1], height, 0) * mask).astype(BF)
        right = toeplitz(line[b : b + 1], lanes, 0).astype(BF)
        gr_ref[b] = dot(left, right).astype(BF)
    basis = basis_ref[...]
    kinds = basis.shape[1]
    up = chosen((group * SUB, group), lambda row, lane: row // SUB == lane)
    out = chosen((kinds, SUB * kinds), lambda row, lane: row == lane % kinds)
    same = chosen((group * SUB, SUB * kinds), lambda row, lane: row % SUB == lane // kinds, F32)
    sk_ref[...] = (dot(dot(up, basis).astype(BF), out) * same).astype(BF)
    up = chosen((SUB * kinds, kinds), lambda row, lane: row // SUB == lane)
    out = chosen((group, group * SUB), lambda row, lane: row == lane // SUB)
    same = chosen((SUB * kinds, group * SUB), lambda row, lane: row % SUB == lane % SUB, F32)
    pk_ref[0] = (dot(dot_rows(up, basis).astype(BF), out) * same).astype(BF)


def lane_window(cells, first, width, lanes):
    have = cells.shape[1]
    base = max(first, 0) // LANES * LANES
    stop = min(have, round_up(first + width, LANES))
    part = cells[:, base:stop]
    size = max(stop - base, lanes)
    if size > stop - base:
        part = jnp.concatenate([part, jnp.zeros((cells.shape[0], size - (stop - base)), F32)], axis=1)
    if (base - first) % size:
        part = pltpu.roll(part, (base - first) % size, 1)
    lane = lax.broadcasted_iota(jnp.int32, (cells.shape[0], lanes), 1)
    low, high = max(0, -first), min(width, have - first)
    return jnp.where((lane >= low) & (lane < high), part[:, :lanes], 0.0)


def split_kernel(starts, wide, radius, place_ref, keep_ref, got_ref, *out_refs):
    chips = len(starts)
    ext, half, span = keep_ref.shape
    lanes = out_refs[0].shape[2]
    unit = 4
    for chip in range(chips):

        @pl.when(place_ref[4] == chip)
        def _():
            for r in range(0, ext, unit):
                pair = keep_ref[r : r + unit].astype(F32) + got_ref[r : r + unit].astype(F32)
                flat = pair.reshape(unit * half, span)
                for hop in range(chips):
                    part = lane_window(flat, starts[(chip + hop) % chips], wide, lanes)
                    part = part.reshape(unit, half, lanes)
                    above, here, below = out_refs[3 * hop : 3 * hop + 3]
                    if r < radius:
                        above[r : r + unit] = part.astype(above.dtype)
                    elif r < ext - radius:
                        here[r - radius : r - radius + unit] = part.astype(here.dtype)
                    else:
                        below[r - ext + radius : r - ext + radius + unit] = part.astype(below.dtype)


def merge_kernel(radius, *refs):
    *in_refs, out_ref = refs
    height = out_ref.shape[0]
    total = in_refs[1][...].astype(F32)
    for i in range(4, len(in_refs), 3):
        total = total + in_refs[i][...].astype(F32)
    first = sum(in_refs[i][...].astype(F32) for i in range(0, len(in_refs), 3))
    last = sum(in_refs[i][...].astype(F32) for i in range(2, len(in_refs), 3))
    out_ref[:radius] = total[:radius] + first
    out_ref[radius : height - radius] = total[radius : height - radius]
    out_ref[height - radius :] = total[height - radius :] + last


def window_kernel(starts, wide, columns, halo, place_ref, mine_ref, other_ref, window_ref, own_ref):
    height, half, lanes_in = mine_ref.shape
    lanes = window_ref.shape[2]
    unit = 4
    for band in range(2 * len(starts)):
        first = band * columns - starts[band // 2]

        @pl.when(place_ref[5] == band)
        def _():
            for r in range(0, height, unit):
                for core in range(2):
                    source = mine_ref if core == band % 2 else other_ref
                    flat = source[r : r + unit].reshape(unit * half, lanes_in)
                    kinds = slice(core * half, (core + 1) * half)
                    part = lane_window(flat, first - halo, columns + 2 * halo, lanes)
                    window_ref[r : r + unit, kinds] = part.reshape(unit, half, lanes).astype(BF)
                    part = lane_window(flat, first, columns, lanes)
                    own_ref[r : r + unit, kinds] = part.reshape(unit, half, lanes)


def first_kernel(columns, halo, before, window, after, *rest):
    normal_kernel(columns, halo, True, (before, window, after), *rest)


def second_kernel(columns, halo, near_ref, before, after, left, right, corner_before, corner_after, *rest):
    *rest, p_ref = rest

    @pl.when(pl.program_id(0) == 0)
    def _():
        window_pieces(
            columns, halo, near_ref, (before, after), (left, right), (corner_before, corner_after), p_ref
        )

    normal_kernel(columns, halo, False, (p_ref,), *rest)


def normal_kernel(
    columns, halo, first, p_refs, own_ref, ridge_ref, sk_ref, pk_ref, gr_ref, gl_ref, out_ref, sums_ref, acc, xs, ys
):
    step = pl.program_id(0)
    group, height, _ = gr_ref.shape
    _, kinds, lanes = p_refs[0].shape
    sources = [(ref, s) for ref in p_refs for s in range(0, ref.shape[0], SUB)]
    ext = SUB * len(sources)
    chunks = height // SUB

    @pl.when(step == 0)
    def _():
        acc[...] = jnp.zeros_like(acc)

    for c in range(0, ext, 2 * SUB):
        halves = []
        for ref, s in sources[c // SUB : c // SUB + 2]:
            cells = ref[s : s + SUB].reshape(SUB * kinds, lanes)
            halves.append(dot(sk_ref[...], cells).reshape(group, SUB, lanes))
        xs[:, c : c + 2 * SUB, :] = jnp.concatenate(halves, axis=1).astype(BF)

    blocks = packed_blocks(columns, halo)
    mids = [dot(gr_ref[b, :, :ext], xs[b]).astype(BF) for b in range(group)]
    for b in range(group):
        parts = []
        at = 0
        for i in range(lanes // LANES):
            if i < len(blocks):
                start, end = blocks[i]
                part = [gl_ref[b, at : at + end - start]]
                at += end - start
                if start:
                    part = [jnp.zeros((start, LANES), BF)] + part
                if end < lanes:
                    part = part + [jnp.zeros((lanes - end, LANES), BF)]
                parts.append(jnp.concatenate(part, axis=0))
            else:
                parts.append(jnp.zeros((lanes, LANES), BF))
        done = dot(mids[b], jnp.concatenate(parts, axis=1))
        for c in range(chunks):
            ys[c, b] = done[c * SUB : (c + 1) * SUB]

    gather = jnp.concatenate([pk_ref[i] for i in range(pk_ref.shape[0])], axis=1)
    for c in range(chunks):
        acc[c] += dot(gather, ys[c].reshape(group * SUB, lanes).astype(BF))

    @pl.when(step == pl.num_programs(0) - 1)
    def _():
        lane = lax.broadcasted_iota(jnp.int32, (kinds, SUB, lanes), 2)
        totals = [jnp.zeros((SUB, lanes), F32) for _ in range(3)]
        for c in range(chunks):
            own = own_ref[:, c * SUB : (c + 1) * SUB, :]
            image = acc[c].reshape(kinds, SUB, lanes) + ridge_ref[...] * own
            image = jnp.where(lane < columns, image, 0.0)
            out_ref[:, c * SUB : (c + 1) * SUB, :] = image
            pairs = [own * image]
            if first:
                pairs += [own * own, image * image]
            for i, pair in enumerate(pairs):
                totals[i] = totals[i] + jnp.sum(pair, axis=0)
        flat = [
            jnp.sum(
                jnp.concatenate(
                    [total[:, i : i + LANES] for i in range(0, lanes, LANES)], axis=0
                ),
                axis=0,
                keepdims=True,
            )
            for total in totals
        ]
        row = lax.broadcasted_iota(jnp.int32, (SUB, LANES), 0)
        packed = jnp.zeros((SUB, LANES), F32)
        for i, line in enumerate(flat):
            packed = packed + jnp.where(row == i, jnp.broadcast_to(line, (SUB, LANES)), 0.0)
        sums_ref[...] = packed


def combine_kernel(shared_ref, v0_ref, v1_ref, v2_ref, coef_ref, res_ref):
    columns = coef_ref.shape[2]
    lines = jnp.sum(shared_ref[...], axis=0)
    v01, v00, v11, v12 = [jnp.sum(lines[i : i + 1], axis=1, keepdims=True) for i in range(4)]
    alpha = v00 / v01
    norm = v00 - 2.0 * alpha * v01 + alpha * alpha * v11
    lead = 1.0 + norm / v00
    product = lead * lead * v01 - 2.0 * lead * alpha * v11 + alpha * alpha * v12
    second = norm / product
    one = alpha + second * lead
    two = second * alpha
    for k in range(coef_ref.shape[0]):
        v0, v1, v2 = v0_ref[k], v1_ref[k], v2_ref[k]
        coef_ref[k] = (one * v0 - two * v1)[:, :columns]
        res_ref[k] = (v0 - one * v1 + two * v2)[:, :columns]


def shift_both(low_edge, high_edge, axis):
    count = lax.axis_size(axis)
    from_before = lax.ppermute(high_edge, axis, [(i, i + 1) for i in range(count - 1)])
    from_after = lax.ppermute(low_edge, axis, [(i + 1, i) for i in range(count - 1)])
    return from_before, from_after


def local(observed, row_taps, col_taps, spectral_basis, ridge_weights):
    bands_here, height, columns_all = observed.shape
    taps = row_taps.shape[1]
    radius = (taps - 1) // 2
    halo = 2 * radius
    bands, kinds = spectral_basis.shape
    n_band = lax.axis_size("band")
    n_row = lax.axis_size("row")
    columns = columns_all // n_band
    lanes = round_up(columns + 2 * halo, 2 * LANES)
    me_band = lax.axis_index("band")
    me_row = lax.axis_index("row")
    core = me_band % 2
    chip = me_band // 2
    chips = n_band // 2

    plain = jnp.concatenate([row_taps, col_taps], axis=1)
    everyone = [(plain, me_band)]
    for hop in range(1, n_band):
        moves = [(i, (i + hop) % n_band) for i in range(n_band)]
        everyone.append((lax.ppermute(plain, "band", moves), (me_band - hop) % n_band))
    basis_all = jnp.concatenate(
        [lax.dynamic_slice_in_dim(spectral_basis, at * bands_here, bands_here, 0) for _, at in everyone]
    )
    every = jnp.concatenate([values for values, _ in everyone])

    half = kinds // 2
    place = jnp.stack(
        [
            me_band * bands_here,
            half * (1 - core),
            me_band * columns - radius,
            me_row * height - radius,
            chip,
            me_band,
        ]
    ).astype(jnp.int32)
    whole = lambda shape: pl.BlockSpec(shape, lambda i: (0,) * len(shape))

    few = group_size(bands_here, 32)
    span = round_up(columns_all, 2 * LANES)
    ext = height + 2 * radius
    chunks = ext // SUB
    give, keep = pl.pallas_call(
        functools.partial(adjoint_kernel, columns_all, radius),
        grid=(bands_here // few,),
        in_specs=[
            pl.BlockSpec(memory_space=pltpu.SMEM),
            pl.BlockSpec((few, height, columns_all), lambda i: (i, 0, 0)),
            whole(plain.shape),
            whole((bands, kinds)),
        ],
        out_specs=[whole((ext, half, span))] * 2,
        out_shape=[jax.ShapeDtypeStruct((ext, half, span), BF)] * 2,
        scratch_shapes=[
            pltpu.VMEM((chunks, SUB * kinds, span), F32),
            pltpu.VMEM((chunks, few, SUB, span), F32),
            pltpu.VMEM((few, 4 * LANES, 2 * LANES), BF),
            pltpu.VMEM((few, 2, ext, height), BF),
            pltpu.VMEM((2, bands_here, 1, 2 * LANES), F32),
        ],
        compiler_params=pltpu.CompilerParams(vmem_limit_bytes=VMEM_LIMIT),
        cost_estimate=pl.CostEstimate(
            flops=bands_here * 2 * 96 * 512 * 256, bytes_accessed=observed.size * 2, transcendentals=0
        ),
        name="adjoint",
    )(place, observed, plain, spectral_basis)


    part = group_size(bands, 32)
    deep = sum(end - start for start, end in packed_blocks(columns, halo))
    taps_spec = pl.BlockSpec((part, 2 * taps), lambda i: (i, 0))
    smem = pl.BlockSpec(memory_space=pltpu.SMEM)
    params = pltpu.CompilerParams(vmem_limit_bytes=VMEM_LIMIT)
    gr, sk, pk = pl.pallas_call(
        functools.partial(gram_rows_kernel, height * n_row, radius),
        grid=(bands // part,),
        in_specs=[smem, taps_spec, pl.BlockSpec((part, kinds), lambda i: (i, 0))],
        out_specs=[
            pl.BlockSpec((part, height, LANES), lambda i: (i, 0, 0)),
            pl.BlockSpec((part * SUB, SUB * kinds), lambda i: (i, 0)),
            pl.BlockSpec((1, SUB * kinds, part * SUB), lambda i: (i, 0, 0)),
        ],
        out_shape=[
            jax.ShapeDtypeStruct((bands, height, LANES), BF),
            jax.ShapeDtypeStruct((bands * SUB, SUB * kinds), BF),
            jax.ShapeDtypeStruct((bands // part, SUB * kinds, part * SUB), BF),
        ],
        compiler_params=params,
        cost_estimate=pl.CostEstimate(
            flops=bands * 2 * LANES**3, bytes_accessed=bands * height * LANES * 2, transcendentals=0
        ),
        name="gram_rows",
    )(place, every, basis_all)
    gl = pl.pallas_call(
        functools.partial(gram_columns_kernel, columns, columns_all, radius),
        grid=(bands // part,),
        in_specs=[smem, taps_spec],
        out_specs=pl.BlockSpec((part, deep, LANES), lambda i: (i, 0, 0)),
        out_shape=jax.ShapeDtypeStruct((bands, deep, LANES), BF),
        compiler_params=params,
        cost_estimate=pl.CostEstimate(
            flops=bands * 2 * (2 * LANES) ** 3, bytes_accessed=bands * deep * LANES * 2, transcendentals=0
        ),
        name="gram_columns",
    )(place, every)

    pairs = [(i, i ^ 1) for i in range(n_band)]
    got = lax.ppermute(give, "band", pairs)
    wide = min(columns_all, 2 * columns + (2 * halo if chips > 2 else halo))
    wide_lanes = round_up(wide, LANES)
    starts = [min(max(2 * columns * c - halo, 0), columns_all - wide) for c in range(chips)]
    vmem = pl.BlockSpec(memory_space=pltpu.VMEM)
    shape = lambda rows, kind: jax.ShapeDtypeStruct((rows, half, wide_lanes), kind)
    sends = pl.pallas_call(
        functools.partial(split_kernel, starts, wide, radius),
        in_specs=[smem, vmem, vmem],
        out_shape=[
            shape(rows, F32 if rows == height and hop == 0 else BF)
            for hop in range(chips)
            for rows in (radius, height, radius)
        ],
        compiler_params=params,
        name="split",
    )(place, keep, got)

    def moves(hop, step):
        return [
            (b * n_row + r, (b + 2 * hop) % n_band * n_row + r + step)
            for b in range(n_band)
            for r in range(n_row)
            if 0 <= r + step < n_row
        ]

    parts = []
    axes = ("band", "row")
    for hop in range(chips):
        above, here, below = sends[3 * hop : 3 * hop + 3]
        after = lax.ppermute(above, axes, moves(hop, -1))
        before = lax.ppermute(below, axes, moves(hop, 1))
        if hop:
            here = lax.ppermute(here, axes, moves(hop, 0))
        parts += [before, here, after]
    parts[1], gr, sk, pk = lax.optimization_barrier((parts[1], gr, sk, pk))
    total = pl.pallas_call(
        functools.partial(merge_kernel, radius),
        out_shape=shape(height, F32),
        compiler_params=params,
        name="merge",
    )(*parts)
    other = lax.ppermute(total, "band", pairs)
    window, v0 = pl.pallas_call(
        functools.partial(window_kernel, starts, wide, columns, halo),
        in_specs=[smem, vmem, vmem],
        out_shape=[
            jax.ShapeDtypeStruct((height, kinds, lanes), BF),
            jax.ShapeDtypeStruct((height, kinds, lanes), F32),
        ],
        compiler_params=params,
        name="window",
    )(place, total, other)
    v0 = jnp.swapaxes(v0, 0, 1)

    group = part
    ridge = jnp.broadcast_to(ridge_weights[:, None, None], (kinds, SUB, lanes))
    tall = height + 2 * halo
    block = lambda shape: pl.BlockSpec((group,) + shape, lambda i: (i, 0, 0))

    def normal_map(pieces, own, first):
        window = [pltpu.VMEM((tall, kinds, lanes), BF)] if not first else []
        return pl.pallas_call(
            functools.partial(first_kernel if first else second_kernel, columns, halo),
            grid=(bands // group,),
            in_specs=[whole(piece.shape) for piece in pieces]
            + [
                whole((kinds, height, lanes)),
                whole((kinds, SUB, lanes)),
                pl.BlockSpec((group * SUB, SUB * kinds), lambda i: (i, 0)),
                pl.BlockSpec((group // part, SUB * kinds, part * SUB), lambda i: (i, 0, 0)),
                block((height, LANES)),
                block((deep, LANES)),
            ],
            out_specs=[whole((kinds, height, lanes)), whole((SUB, LANES))],
            out_shape=[
                jax.ShapeDtypeStruct((kinds, height, lanes), F32),
                jax.ShapeDtypeStruct((SUB, LANES), F32),
            ],
            scratch_shapes=[
                pltpu.VMEM((height // SUB, SUB * kinds, lanes), F32),
                pltpu.VMEM((group, tall, lanes), BF),
                pltpu.VMEM((height // SUB, group, SUB, lanes), F32),
            ]
            + window,
            compiler_params=pltpu.CompilerParams(vmem_limit_bytes=VMEM_LIMIT),
            cost_estimate=pl.CostEstimate(
                flops=bands * 2 * 32 * 512 * 256, bytes_accessed=bands * deep * LANES * 2, transcendentals=0
            ),
            name="normal",
        )(*pieces, own, ridge, sk, pk, gr, gl)

    before, after = shift_both(window[:halo], window[height - halo :], "row")
    v1, sums1 = normal_map([before, window, after], v0, True)
    near = jnp.swapaxes(v1.astype(BF), 0, 1)
    main = jax.ShapeDtypeStruct((main_rows(columns, halo), kinds, LANES), BF)
    side = jax.ShapeDtypeStruct((strip_plan(height, halo)[1], kinds, LANES), BF)
    up, down, left, right = pl.pallas_call(
        functools.partial(pack_kernel, columns, halo),
        out_shape=[main, main, side, side],
        compiler_params=pltpu.CompilerParams(vmem_limit_bytes=VMEM_LIMIT),
        name="pack",
    )(near)
    before, after = shift_both(up, down, "row")
    from_left, from_right = shift_both(left, right, "band")
    corners = jnp.concatenate([from_left, from_right], axis=0)
    corner_before, corner_after = shift_both(corners, corners, "row")
    pieces = [near, before, after, from_left, from_right, corner_before, corner_after]
    v2, sums2 = normal_map(pieces, v1, False)

    sums = jnp.concatenate([sums1[:3], sums2[:1], jnp.zeros((SUB - 4, LANES), F32)])
    mine = jnp.broadcast_to(sums[None], (n_band * n_row, SUB, LANES))
    shared = lax.all_to_all(mine, ("band", "row"), 0, 0, tiled=True)
    out = jax.ShapeDtypeStruct((kinds, height, columns), F32)
    return pl.pallas_call(
        combine_kernel,
        out_shape=[out, out],
        compiler_params=pltpu.CompilerParams(vmem_limit_bytes=VMEM_LIMIT),
        name="combine",
    )(shared, v0, v1, v2)


def solution(mesh):
    in_specs = (P("band", "row", None), P("band", None), P("band", None), P(), P())
    out_specs = (P(None, "row", "band"), P(None, "row", "band"))
    return jax.shard_map(local, mesh=mesh, in_specs=in_specs, out_specs=out_specs, check_vma=False)
```

```python
import functools

import jax
import jax.numpy as jnp
from jax import lax
from jax.experimental import pallas as pl
from jax.experimental.pallas import tpu as pltpu
from jax.sharding import PartitionSpec as P

LANES = 128
SUB = 8
BF = jnp.bfloat16
F32 = jnp.float32
VMEM_LIMIT = 50 * 1024 * 1024
SMALL_LIMIT = 20 * 1024 * 1024


def round_up(value, unit):
    return (value + unit - 1) // unit * unit


def group_size(count, most):
    return max(size for size in range(1, most + 1) if count % size == 0)


def packed_blocks(columns, halo):
    out = []
    for first in range(0, columns, LANES):
        out.append((first, round_up(min(first + LANES, columns) + 2 * halo, 2 * SUB)))
    return out


def dot(lhs, rhs):
    return lax.dot_general(lhs, rhs, (((1,), (0,)), ((), ())), preferred_element_type=F32)


def toeplitz(taps, rows, shift):
    lanes = taps.shape[1]
    pieces = []
    for first in range(0, rows, LANES):
        count = min(LANES, rows - first)
        wide = jnp.broadcast_to(taps, (count, lanes))
        pieces.append(pltpu.roll(wide, (shift + first) % lanes, 1, stride=1, stride_axis=0))
    return jnp.concatenate(pieces, axis=0) if len(pieces) > 1 else pieces[0]


def chosen(shape, rule, kind=BF):
    row = lax.broadcasted_iota(jnp.int32, shape, 0)
    lane = lax.broadcasted_iota(jnp.int32, shape, 1)
    return jnp.where(rule(row, lane), 1.0, 0.0).astype(kind)


def placed_taps(both, places, kind):
    count = both.shape[1] // 2
    picks = []
    for first, lead, flip in places:

        def rule(row, lane):
            at = lane - lead
            here = (at >= 0) & (at < count)
            return here & (row == first + (count - 1 - at if flip else at))

        picks.append(chosen((both.shape[1], 2 * LANES), rule, kind))
    done = lax.dot_general(
        both.astype(kind),
        jnp.concatenate(picks, axis=1),
        (((1,), (0,)), ((), ())),
        precision=lax.Precision.HIGHEST if kind == F32 else None,
        preferred_element_type=F32,
    )
    return [done[:, i * 2 * LANES : (i + 1) * 2 * LANES] for i in range(len(places))]


def dot_rows(lhs, rhs):
    return lax.dot_general(lhs, rhs, (((1,), (1,)), ((), ())), preferred_element_type=F32)


def strip_plan(rows, width):
    beside = max(n for n in range(1, rows + 1) if rows % n == 0 and n * width <= LANES)
    return beside, rows // beside


def turn_lanes(cells, amount):
    rows, kinds, lanes = cells.shape
    flat = pltpu.roll(cells.reshape(rows * kinds, lanes), amount % lanes, 1)
    return flat.reshape(rows, kinds, lanes)


def keep_lanes(cells, first, width):
    lane = lax.broadcasted_iota(jnp.int32, cells.shape, 2)
    return jnp.where((lane >= first) & (lane < first + width), cells, 0.0)


def packed_strip(cells, first, width):
    beside, rows = strip_plan(cells.shape[0], width)
    total = None
    for g in range(beside):
        part = turn_lanes(cells[g * rows : (g + 1) * rows], g * width - first)[:, :, :LANES]
        part = keep_lanes(part, g * width, width)
        total = part if total is None else total + part
    return total


def unpacked_strip(packed, count, width, first, lanes):
    beside, rows = strip_plan(count, width)
    wide = packed.astype(F32)
    if lanes > LANES:
        rest = jnp.zeros(packed.shape[:2] + (lanes - LANES,), F32)
        wide = jnp.concatenate([wide, rest], axis=2)
    return jnp.concatenate(
        [keep_lanes(turn_lanes(wide, first - g * width), first, width) for g in range(beside)], axis=0
    )


def main_rows(columns, halo):
    full = columns // LANES
    rest = columns - full * LANES
    return full * halo + (strip_plan(halo, rest)[1] if rest else 0)


def packed_main(cells, columns):
    full = columns // LANES
    rest = columns - full * LANES
    parts = [cells[:, :, t * LANES : (t + 1) * LANES] for t in range(full)]
    if rest:
        parts.append(packed_strip(cells, full * LANES, rest))
    return jnp.concatenate(parts, axis=0)


def unpacked_main(packed, columns, halo, lanes):
    full = columns // LANES
    rest = columns - full * LANES
    kinds = packed.shape[1]
    total = jnp.zeros((halo, kinds, lanes), F32)
    for t in range(full):
        part = packed[t * halo : (t + 1) * halo]
        total = total + unpacked_wide(part, t * LANES + halo, lanes)
    if rest:
        total = total + unpacked_strip(packed[full * halo :], halo, rest, full * LANES + halo, lanes)
    return total


def unpacked_wide(part, first, lanes):
    wide = part.astype(F32)
    if lanes > LANES:
        rest = jnp.zeros(part.shape[:2] + (lanes - LANES,), F32)
        wide = jnp.concatenate([wide, rest], axis=2)
    return turn_lanes(wide, first)


def pack_kernel(columns, halo, near_ref, up_ref, down_ref, left_ref, right_ref):
    cells = near_ref[...].astype(F32)
    height = cells.shape[0]
    up_ref[...] = packed_main(cells[:halo], columns).astype(BF)
    down_ref[...] = packed_main(cells[height - halo :], columns).astype(BF)
    left_ref[...] = packed_strip(cells, 0, halo).astype(BF)
    right_ref[...] = packed_strip(cells, columns - halo, halo).astype(BF)


def window_pieces(columns, halo, near_ref, main_refs, side_refs, corner_refs, p_ref):
    height, _, lanes = near_ref.shape
    right = columns + halo
    own = turn_lanes(near_ref[...].astype(F32), halo)
    own = own + unpacked_strip(side_refs[0][...], height, halo, 0, lanes)
    own = own + unpacked_strip(side_refs[1][...], height, halo, right, lanes)
    p_ref[halo : halo + height] = own.astype(BF)
    rows = strip_plan(height, halo)[1]
    for main, corner, first, at in (
        (main_refs[0], corner_refs[0], height - halo, 0),
        (main_refs[1], corner_refs[1], 0, halo + height),
    ):
        total = unpacked_main(main[...], columns, halo, lanes)
        for packed, lane in ((corner[:rows], 0), (corner[rows:], right)):
            total = total + unpacked_strip(packed, height, halo, lane, lanes)[first : first + halo]
        p_ref[at : at + halo] = total.astype(BF)


def adjoint_kernel(
    columns, radius, place_ref, obs_ref, taps_ref, basis_ref, give_ref, keep_ref, acc, ys, mats, rows, lines
):
    step = pl.program_id(0)
    group, height, _ = obs_ref.shape
    span = ys.shape[3]
    width = 2 * LANES
    tiles = span // width
    chunks = ys.shape[0]
    ext = chunks * SUB
    edge = 2 * SUB
    last = columns // LANES * LANES
    batch = group_size(group, 7)

    @pl.when(step == 0)
    def _():
        acc[...] = jnp.zeros_like(acc)
        mats[...] = jnp.zeros_like(mats)
        both = taps_ref[...]
        taps = both.shape[1] // 2
        for i, line in enumerate(placed_taps(both, [(taps, -radius % SUB, False), (0, 0, True)], F32)):
            lines[i] = line[:, None]

    @pl.loop(0, group, step=batch)
    def _(start):
        near = lax.broadcasted_iota(jnp.int32, (edge, width), 1) < LANES
        blank = jnp.zeros((edge, width), BF)
        for b in range(batch):
            b = start + b
            ring = toeplitz(lines[0, step * group + b], width, -round_up(radius, SUB)).astype(BF)
            top, bottom = ring[:edge], ring[width - edge :]
            mats[b, LANES - edge : LANES] = jnp.where(near, bottom, blank)
            mats[b, LANES : LANES + edge] = jnp.where(near, top, blank)
            mats[b, LANES + edge : LANES + width - edge] = ring[edge : width - edge]
            mats[b, LANES + width - edge : LANES + width] = jnp.where(near, blank, bottom)
            mats[b, LANES + width : LANES + width + edge] = jnp.where(near, blank, top)
            reach = toeplitz(lines[1, step * group + b][:, :LANES], ext, -2 * radius)[:, :height]
            high = reach.astype(BF)
            rows[b, 0] = high
            rows[b, 1] = (reach - high.astype(F32)).astype(BF)

    @pl.loop(0, group, step=batch)
    def _(start):
        fields = []
        for b in range(batch):
            cells = obs_ref[start + b]
            pieces = [jnp.zeros((height, LANES), BF), cells[:, :last]]
            if columns > last:
                fill = jnp.zeros((height, LANES - (columns - last)), BF)
                pieces.append(jnp.concatenate([cells[:, last:], fill], axis=1))
            have = sum(piece.shape[1] for piece in pieces)
            if have < span + width:
                pieces.append(jnp.zeros((height, span + width - have), BF))
            padded = jnp.concatenate(pieces, axis=1)
            stacked = jnp.concatenate(
                [padded[:, t * width : t * width + 2 * width] for t in range(tiles)], axis=0
            )
            mixed = dot(stacked, mats[start + b]).astype(BF)
            fields.append(
                jnp.concatenate([mixed[t * height : (t + 1) * height] for t in range(tiles)], axis=1)
            )
        for b in range(batch):
            done = dot(rows[start + b, 0], fields[b]) + dot(rows[start + b, 1], fields[b])
            for c in range(chunks):
                ys[c, start + b] = done[c * SUB : (c + 1) * SUB]

    bands, kinds = basis_ref.shape
    first = place_ref[0] + step * group
    turn = place_ref[1]
    pick = chosen((SUB * kinds, kinds), lambda row, lane: lane == (row + turn) % kinds)
    wide = dot_rows(pick, basis_ref[...]).astype(BF)
    here = chosen((bands, group * SUB), lambda row, lane: row == first + lane // SUB)
    same = chosen((SUB * kinds, group * SUB), lambda row, lane: row // kinds == lane % SUB, F32)
    mix = (dot(wide, here) * same).astype(BF)
    for c in range(chunks):
        cells = ys[c].reshape(group * SUB, span).astype(BF)
        acc[c] += dot(mix, cells)

    @pl.when(step == pl.num_programs(0) - 1)
    def _():
        half = kinds // 2
        total = acc[...].reshape(ext, kinds, span).astype(BF)
        give_ref[...] = total[:, :half]
        keep_ref[...] = total[:, half:]


def inside(lanes, first, count, limit):
    lane = lax.broadcasted_iota(jnp.int32, (1, lanes), 1)
    at = lane + first
    return jnp.where((at >= 0) & (at < limit) & (lane < count), 1.0, 0.0)


def gram_columns_kernel(columns, columns_all, radius, place_ref, taps_ref, gl_ref):
    halo = 2 * radius
    size = 2 * LANES
    blocks = packed_blocks(columns, halo)
    tall = max(end for _, end in blocks)
    inner = round_up(columns + halo, 2 * SUB)
    both = taps_ref[...]
    taps = both.shape[1] // 2
    line, back = placed_taps(both, [(taps, 0, False), (taps, 0, True)], BF)
    mask = inside(size, place_ref[2], columns + halo, columns_all)
    for b in range(both.shape[0]):
        left = (toeplitz(back[b : b + 1], tall, -halo) * mask).astype(BF)
        right = toeplitz(line[b : b + 1], inner, -halo).astype(BF)
        right = jnp.concatenate([right, jnp.zeros((size - inner, size), BF)], axis=0)
        done = dot(left, right).astype(BF)
        at = 0
        for i, (start, end) in enumerate(blocks):
            gl_ref[b, at : at + end - start] = done[start:end, i * LANES : (i + 1) * LANES]
            at += end - start


def gram_rows_kernel(rows_all, radius, place_ref, taps_ref, basis_ref, gr_ref, sk_ref, pk_ref):
    halo = 2 * radius
    group, height, lanes = gr_ref.shape
    both = taps_ref[...]
    line, back = [part[:, :lanes] for part in placed_taps(both, [(0, 0, False), (0, 0, True)], BF)]
    mask = inside(lanes, place_ref[3], height + halo, rows_all)
    for b in range(group):
        left = (toeplitz(back[b : b + 1], height, 0) * mask).astype(BF)
        right = toeplitz(line[b : b + 1], lanes, 0).astype(BF)
        gr_ref[b] = dot(left, right).astype(BF)
    basis = basis_ref[...]
    kinds = basis.shape[1]
    up = chosen((group * SUB, group), lambda row, lane: row // SUB == lane)
    out = chosen((kinds, SUB * kinds), lambda row, lane: row == lane % kinds)
    same = chosen((group * SUB, SUB * kinds), lambda row, lane: row % SUB == lane // kinds, F32)
    sk_ref[...] = (dot(dot(up, basis).astype(BF), out) * same).astype(BF)
    up = chosen((SUB * kinds, kinds), lambda row, lane: row // SUB == lane)
    out = chosen((group, group * SUB), lambda row, lane: row == lane // SUB)
    same = chosen((SUB * kinds, group * SUB), lambda row, lane: row % SUB == lane % SUB, F32)
    pk_ref[0] = (dot(dot_rows(up, basis).astype(BF), out) * same).astype(BF)


def lane_window(cells, first, width, lanes):
    have = cells.shape[1]
    base = max(first, 0) // LANES * LANES
    stop = min(have, round_up(first + width, LANES))
    part = cells[:, base:stop]
    size = max(stop - base, lanes)
    if size > stop - base:
        part = jnp.concatenate([part, jnp.zeros((cells.shape[0], size - (stop - base)), F32)], axis=1)
    if (base - first) % size:
        part = pltpu.roll(part, (base - first) % size, 1)
    lane = lax.broadcasted_iota(jnp.int32, (cells.shape[0], lanes), 1)
    low, high = max(0, -first), min(width, have - first)
    return jnp.where((lane >= low) & (lane < high), part[:, :lanes], 0.0)


def split_kernel(starts, wide, radius, place_ref, keep_ref, got_ref, *out_refs):
    chips = len(starts)
    ext, half, span = keep_ref.shape
    lanes = out_refs[0].shape[2]
    unit = 4
    for chip in range(chips):

        @pl.when(place_ref[4] == chip)
        def _():
            for r in range(0, ext, unit):
                pair = keep_ref[r : r + unit].astype(F32) + got_ref[r : r + unit].astype(F32)
                flat = pair.reshape(unit * half, span)
                for hop in range(chips):
                    part = lane_window(flat, starts[(chip + hop) % chips], wide, lanes)
                    part = part.reshape(unit, half, lanes)
                    above, here, below = out_refs[3 * hop : 3 * hop + 3]
                    if r < radius:
                        above[r : r + unit] = part.astype(above.dtype)
                    elif r < ext - radius:
                        here[r - radius : r - radius + unit] = part.astype(here.dtype)
                    else:
                        below[r - ext + radius : r - ext + radius + unit] = part.astype(below.dtype)


def merge_kernel(radius, *refs):
    *in_refs, out_ref = refs
    height = out_ref.shape[0]
    total = in_refs[1][...].astype(F32)
    for i in range(4, len(in_refs), 3):
        total = total + in_refs[i][...].astype(F32)
    first = sum(in_refs[i][...].astype(F32) for i in range(0, len(in_refs), 3))
    last = sum(in_refs[i][...].astype(F32) for i in range(2, len(in_refs), 3))
    out_ref[:radius] = total[:radius] + first
    out_ref[radius : height - radius] = total[radius : height - radius]
    out_ref[height - radius :] = total[height - radius :] + last


def window_kernel(starts, wide, columns, halo, place_ref, mine_ref, other_ref, window_ref, own_ref):
    height, half, lanes_in = mine_ref.shape
    lanes = window_ref.shape[2]
    unit = 4
    for band in range(2 * len(starts)):
        first = band * columns - starts[band // 2]

        @pl.when(place_ref[5] == band)
        def _():
            for r in range(0, height, unit):
                for core in range(2):
                    source = mine_ref if core == band % 2 else other_ref
                    flat = source[r : r + unit].reshape(unit * half, lanes_in)
                    kinds = slice(core * half, (core + 1) * half)
                    part = lane_window(flat, first - halo, columns + 2 * halo, lanes)
                    window_ref[r : r + unit, kinds] = part.reshape(unit, half, lanes).astype(BF)
                    part = lane_window(flat, first, columns, lanes)
                    own_ref[r : r + unit, kinds] = part.reshape(unit, half, lanes)


def first_kernel(columns, halo, group, before, window, after, *rest):
    normal_kernel(columns, halo, group, True, (before, window, after), *rest)


def second_kernel(
    columns, halo, group, near_ref, before, after, left, right, corner_before, corner_after, *rest
):
    *rest, p_ref = rest

    @pl.when(pl.program_id(0) == 0)
    def _():
        window_pieces(
            columns, halo, near_ref, (before, after), (left, right), (corner_before, corner_after), p_ref
        )

    normal_kernel(columns, halo, group, False, (p_ref,), *rest)


def normal_kernel(
    columns, halo, group, first, p_refs, own_ref, ridge_ref, sk_ref, pk_ref, gr_ref, gl_ref, out_ref, sums_ref, acc, xs, ys
):
    step = pl.program_id(0)
    height = gr_ref.shape[1]
    from_band = step * group
    _, kinds, lanes = p_refs[0].shape
    sources = [(ref, s) for ref in p_refs for s in range(0, ref.shape[0], SUB)]
    ext = SUB * len(sources)
    chunks = height // SUB

    @pl.when(step == 0)
    def _():
        acc[...] = jnp.zeros_like(acc)

    spread = sk_ref[pl.ds(pl.multiple_of(from_band * SUB, group * SUB), group * SUB)]
    for c in range(0, ext, 2 * SUB):
        halves = []
        for ref, s in sources[c // SUB : c // SUB + 2]:
            cells = ref[s : s + SUB].reshape(SUB * kinds, lanes)
            halves.append(dot(spread, cells).reshape(group, SUB, lanes))
        xs[:, c : c + 2 * SUB, :] = jnp.concatenate(halves, axis=1).astype(BF)

    blocks = packed_blocks(columns, halo)
    mids = [dot(gr_ref[from_band + b, :, :ext], xs[b]).astype(BF) for b in range(group)]
    for b in range(group):
        parts = []
        at = 0
        for i in range(lanes // LANES):
            if i < len(blocks):
                start, end = blocks[i]
                part = [gl_ref[from_band + b, at : at + end - start]]
                at += end - start
                if start:
                    part = [jnp.zeros((start, LANES), BF)] + part
                if end < lanes:
                    part = part + [jnp.zeros((lanes - end, LANES), BF)]
                parts.append(jnp.concatenate(part, axis=0))
            else:
                parts.append(jnp.zeros((lanes, LANES), BF))
        done = dot(mids[b], jnp.concatenate(parts, axis=1))
        for c in range(chunks):
            ys[c, b] = done[c * SUB : (c + 1) * SUB]

    gather = pk_ref[step]
    for c in range(chunks):
        acc[c] += dot(gather, ys[c].reshape(group * SUB, lanes).astype(BF))

    @pl.when(step == pl.num_programs(0) - 1)
    def _():
        lane = lax.broadcasted_iota(jnp.int32, (kinds, SUB, lanes), 2)
        totals = [jnp.zeros((SUB, lanes), F32) for _ in range(3)]
        for c in range(chunks):
            own = own_ref[:, c * SUB : (c + 1) * SUB, :]
            image = acc[c].reshape(kinds, SUB, lanes) + ridge_ref[...] * own
            image = jnp.where(lane < columns, image, 0.0)
            out_ref[:, c * SUB : (c + 1) * SUB, :] = image
            pairs = [own * image]
            if first:
                pairs += [own * own, image * image]
            for i, pair in enumerate(pairs):
                totals[i] = totals[i] + jnp.sum(pair, axis=0)
        flat = [
            jnp.sum(
                jnp.concatenate(
                    [total[:, i : i + LANES] for i in range(0, lanes, LANES)], axis=0
                ),
                axis=0,
                keepdims=True,
            )
            for total in totals
        ]
        row = lax.broadcasted_iota(jnp.int32, (SUB, LANES), 0)
        packed = jnp.zeros((SUB, LANES), F32)
        for i, line in enumerate(flat):
            packed = packed + jnp.where(row == i, jnp.broadcast_to(line, (SUB, LANES)), 0.0)
        sums_ref[...] = packed


def combine_kernel(shared_ref, v0_ref, v1_ref, v2_ref, coef_ref, res_ref):
    columns = coef_ref.shape[2]
    lines = jnp.sum(shared_ref[...], axis=0)
    v01, v00, v11, v12 = [jnp.sum(lines[i : i + 1], axis=1, keepdims=True) for i in range(4)]
    alpha = v00 / v01
    norm = v00 - 2.0 * alpha * v01 + alpha * alpha * v11
    lead = 1.0 + norm / v00
    product = lead * lead * v01 - 2.0 * lead * alpha * v11 + alpha * alpha * v12
    second = norm / product
    one = alpha + second * lead
    two = second * alpha
    for k in range(coef_ref.shape[0]):
        v0, v1, v2 = v0_ref[k], v1_ref[k], v2_ref[k]
        coef_ref[k] = (one * v0 - two * v1)[:, :columns]
        res_ref[k] = (v0 - one * v1 + two * v2)[:, :columns]


def shift_both(low_edge, high_edge, axis):
    count = lax.axis_size(axis)
    from_before = lax.ppermute(high_edge, axis, [(i, i + 1) for i in range(count - 1)])
    from_after = lax.ppermute(low_edge, axis, [(i + 1, i) for i in range(count - 1)])
    return from_before, from_after


def local(observed, row_taps, col_taps, spectral_basis, ridge_weights):
    bands_here, height, columns_all = observed.shape
    taps = row_taps.shape[1]
    radius = (taps - 1) // 2
    halo = 2 * radius
    bands, kinds = spectral_basis.shape
    n_band = lax.axis_size("band")
    n_row = lax.axis_size("row")
    columns = columns_all // n_band
    lanes = round_up(columns + 2 * halo, 2 * LANES)
    me_band = lax.axis_index("band")
    me_row = lax.axis_index("row")
    core = me_band % 2
    chip = me_band // 2
    chips = n_band // 2

    plain = jnp.concatenate([row_taps, col_taps], axis=1)
    everyone = [(plain, me_band)]
    for hop in range(1, n_band):
        moves = [(i, (i + hop) % n_band) for i in range(n_band)]
        everyone.append((lax.ppermute(plain, "band", moves), (me_band - hop) % n_band))
    basis_all = jnp.concatenate(
        [lax.dynamic_slice_in_dim(spectral_basis, at * bands_here, bands_here, 0) for _, at in everyone]
    )
    every = jnp.concatenate([values for values, _ in everyone])

    half = kinds // 2
    place = jnp.stack(
        [
            me_band * bands_here,
            half * (1 - core),
            me_band * columns - radius,
            me_row * height - radius,
            chip,
            me_band,
        ]
    ).astype(jnp.int32)
    whole = lambda shape: pl.BlockSpec(shape, lambda i: (0,) * len(shape))

    few = group_size(bands_here, 32)
    span = round_up(columns_all, 2 * LANES)
    ext = height + 2 * radius
    chunks = ext // SUB
    give, keep = pl.pallas_call(
        functools.partial(adjoint_kernel, columns_all, radius),
        grid=(bands_here // few,),
        in_specs=[
            pl.BlockSpec(memory_space=pltpu.SMEM),
            pl.BlockSpec((few, height, columns_all), lambda i: (i, 0, 0)),
            whole(plain.shape),
            whole((bands, kinds)),
        ],
        out_specs=[whole((ext, half, span))] * 2,
        out_shape=[jax.ShapeDtypeStruct((ext, half, span), BF)] * 2,
        scratch_shapes=[
            pltpu.VMEM((chunks, SUB * kinds, span), F32),
            pltpu.VMEM((chunks, few, SUB, span), F32),
            pltpu.VMEM((few, 4 * LANES, 2 * LANES), BF),
            pltpu.VMEM((few, 2, ext, height), BF),
            pltpu.VMEM((2, bands_here, 1, 2 * LANES), F32),
        ],
        compiler_params=pltpu.CompilerParams(vmem_limit_bytes=VMEM_LIMIT),
        cost_estimate=pl.CostEstimate(
            flops=bands_here * 2 * 96 * 512 * 256, bytes_accessed=observed.size * 2, transcendentals=0
        ),
        name="adjoint",
    )(place, observed, plain, spectral_basis)


    part = group_size(bands, 32)
    deep = sum(end - start for start, end in packed_blocks(columns, halo))
    taps_spec = pl.BlockSpec((part, 2 * taps), lambda i: (i, 0))
    smem = pl.BlockSpec(memory_space=pltpu.SMEM)
    params = pltpu.CompilerParams(vmem_limit_bytes=SMALL_LIMIT)
    gr, sk, pk = pl.pallas_call(
        functools.partial(gram_rows_kernel, height * n_row, radius),
        grid=(bands // part,),
        in_specs=[smem, taps_spec, pl.BlockSpec((part, kinds), lambda i: (i, 0))],
        out_specs=[
            pl.BlockSpec((part, height, LANES), lambda i: (i, 0, 0)),
            pl.BlockSpec((part * SUB, SUB * kinds), lambda i: (i, 0)),
            pl.BlockSpec((1, SUB * kinds, part * SUB), lambda i: (i, 0, 0)),
        ],
        out_shape=[
            jax.ShapeDtypeStruct((bands, height, LANES), BF),
            jax.ShapeDtypeStruct((bands * SUB, SUB * kinds), BF),
            jax.ShapeDtypeStruct((bands // part, SUB * kinds, part * SUB), BF),
        ],
        compiler_params=params,
        cost_estimate=pl.CostEstimate(
            flops=bands * 2 * LANES**3, bytes_accessed=bands * height * LANES * 2, transcendentals=0
        ),
        name="gram_rows",
    )(place, every, basis_all)
    gl = pl.pallas_call(
        functools.partial(gram_columns_kernel, columns, columns_all, radius),
        grid=(bands // part,),
        in_specs=[smem, taps_spec],
        out_specs=pl.BlockSpec((part, deep, LANES), lambda i: (i, 0, 0)),
        out_shape=jax.ShapeDtypeStruct((bands, deep, LANES), BF),
        compiler_params=params,
        cost_estimate=pl.CostEstimate(
            flops=bands * 2 * (2 * LANES) ** 3, bytes_accessed=bands * deep * LANES * 2, transcendentals=0
        ),
        name="gram_columns",
    )(place, every)

    pairs = [(i, i ^ 1) for i in range(n_band)]
    got = lax.ppermute(give, "band", pairs)
    wide = min(columns_all, 2 * columns + (2 * halo if chips > 2 else halo))
    wide_lanes = round_up(wide, LANES)
    starts = [min(max(2 * columns * c - halo, 0), columns_all - wide) for c in range(chips)]
    vmem = pl.BlockSpec(memory_space=pltpu.VMEM)
    shape = lambda rows, kind: jax.ShapeDtypeStruct((rows, half, wide_lanes), kind)
    sends = pl.pallas_call(
        functools.partial(split_kernel, starts, wide, radius),
        in_specs=[smem, vmem, vmem],
        out_shape=[
            shape(rows, F32 if rows == height and hop == 0 else BF)
            for hop in range(chips)
            for rows in (radius, height, radius)
        ],
        compiler_params=pltpu.CompilerParams(vmem_limit_bytes=VMEM_LIMIT),
        name="split",
    )(place, keep, got)

    def moves(hop, step):
        return [
            (b * n_row + r, (b + 2 * hop) % n_band * n_row + r + step)
            for b in range(n_band)
            for r in range(n_row)
            if 0 <= r + step < n_row
        ]

    parts = []
    axes = ("band", "row")
    for hop in range(chips):
        above, here, below = sends[3 * hop : 3 * hop + 3]
        after = lax.ppermute(above, axes, moves(hop, -1))
        before = lax.ppermute(below, axes, moves(hop, 1))
        if hop:
            here = lax.ppermute(here, axes, moves(hop, 0))
        parts += [before, here, after]
    parts[1], gr, sk, pk = lax.optimization_barrier((parts[1], gr, sk, pk))
    total = pl.pallas_call(
        functools.partial(merge_kernel, radius),
        out_shape=shape(height, F32),
        compiler_params=params,
        name="merge",
    )(*parts)
    other = lax.ppermute(total, "band", pairs)
    window, v0 = pl.pallas_call(
        functools.partial(window_kernel, starts, wide, columns, halo),
        in_specs=[smem, vmem, vmem],
        out_shape=[
            jax.ShapeDtypeStruct((height, kinds, lanes), BF),
            jax.ShapeDtypeStruct((height, kinds, lanes), F32),
        ],
        compiler_params=params,
        name="window",
    )(place, total, other)
    v0 = jnp.swapaxes(v0, 0, 1)

    group = part
    ridge = jnp.broadcast_to(ridge_weights[:, None, None], (kinds, SUB, lanes))
    tall = height + 2 * halo

    def normal_map(pieces, own, first):
        window = [pltpu.VMEM((tall, kinds, lanes), BF)] if not first else []
        return pl.pallas_call(
            functools.partial(first_kernel if first else second_kernel, columns, halo, group),
            grid=(bands // group,),
            in_specs=[vmem] * (len(pieces) + 6),
            out_specs=[vmem, vmem],
            out_shape=[
                jax.ShapeDtypeStruct((kinds, height, lanes), F32),
                jax.ShapeDtypeStruct((SUB, LANES), F32),
            ],
            scratch_shapes=[
                pltpu.VMEM((height // SUB, SUB * kinds, lanes), F32),
                pltpu.VMEM((group, tall, lanes), BF),
                pltpu.VMEM((height // SUB, group, SUB, lanes), F32),
            ]
            + window,
            compiler_params=pltpu.CompilerParams(vmem_limit_bytes=SMALL_LIMIT),
            cost_estimate=pl.CostEstimate(
                flops=bands * 2 * 32 * 512 * 256, bytes_accessed=bands * deep * LANES * 2, transcendentals=0
            ),
            name="normal",
        )(*pieces, own, ridge, sk, pk, gr, gl)

    before, after = shift_both(window[:halo], window[height - halo :], "row")
    v1, sums1 = normal_map([before, window, after], v0, True)
    near = jnp.swapaxes(v1.astype(BF), 0, 1)
    main = jax.ShapeDtypeStruct((main_rows(columns, halo), kinds, LANES), BF)
    side = jax.ShapeDtypeStruct((strip_plan(height, halo)[1], kinds, LANES), BF)
    up, down, left, right = pl.pallas_call(
        functools.partial(pack_kernel, columns, halo),
        out_shape=[main, main, side, side],
        compiler_params=pltpu.CompilerParams(vmem_limit_bytes=SMALL_LIMIT),
        name="pack",
    )(near)
    before, after = shift_both(up, down, "row")
    from_left, from_right = shift_both(left, right, "band")
    corners = jnp.concatenate([from_left, from_right], axis=0)
    corner_before, corner_after = shift_both(corners, corners, "row")
    pieces = [near, before, after, from_left, from_right, corner_before, corner_after]
    v2, sums2 = normal_map(pieces, v1, False)

    sums = jnp.concatenate([sums1[:3], sums2[:1], jnp.zeros((SUB - 4, LANES), F32)])
    mine = jnp.broadcast_to(sums[None], (n_band * n_row, SUB, LANES))
    shared = lax.all_to_all(mine, ("band", "row"), 0, 0, tiled=True)
    out = jax.ShapeDtypeStruct((kinds, height, columns), F32)
    return pl.pallas_call(
        combine_kernel,
        out_shape=[out, out],
        compiler_params=pltpu.CompilerParams(vmem_limit_bytes=SMALL_LIMIT),
        name="combine",
    )(shared, v0, v1, v2)


def solution(mesh):
    in_specs = (P("band", "row", None), P("band", None), P("band", None), P(), P())
    out_specs = (P(None, "row", "band"), P(None, "row", "band"))
    return jax.shard_map(local, mesh=mesh, in_specs=in_specs, out_specs=out_specs, check_vma=False)
```

```python
import functools

import jax
import jax.numpy as jnp
from jax import lax
from jax.experimental import pallas as pl
from jax.experimental.pallas import tpu as pltpu
from jax.sharding import PartitionSpec as P

LANES = 128
SUB = 8
BF = jnp.bfloat16
F32 = jnp.float32
VMEM_LIMIT = 50 * 1024 * 1024
SMALL_LIMIT = 20 * 1024 * 1024


def round_up(value, unit):
    return (value + unit - 1) // unit * unit


def group_size(count, most):
    return max(size for size in range(1, most + 1) if count % size == 0)


def packed_blocks(columns, halo):
    out = []
    for first in range(0, columns, LANES):
        out.append((first, round_up(min(first + LANES, columns) + 2 * halo, 2 * SUB)))
    return out


def dot(lhs, rhs):
    return lax.dot_general(lhs, rhs, (((1,), (0,)), ((), ())), preferred_element_type=F32)


def toeplitz(taps, rows, shift):
    lanes = taps.shape[1]
    pieces = []
    for first in range(0, rows, LANES):
        count = min(LANES, rows - first)
        wide = jnp.broadcast_to(taps, (count, lanes))
        pieces.append(pltpu.roll(wide, (shift + first) % lanes, 1, stride=1, stride_axis=0))
    return jnp.concatenate(pieces, axis=0) if len(pieces) > 1 else pieces[0]


def chosen(shape, rule, kind=BF):
    row = lax.broadcasted_iota(jnp.int32, shape, 0)
    lane = lax.broadcasted_iota(jnp.int32, shape, 1)
    return jnp.where(rule(row, lane), 1.0, 0.0).astype(kind)


def placed_taps(both, places, kind):
    count = both.shape[1] // 2
    picks = []
    for first, lead, flip in places:

        def rule(row, lane):
            at = lane - lead
            here = (at >= 0) & (at < count)
            return here & (row == first + (count - 1 - at if flip else at))

        picks.append(chosen((both.shape[1], 2 * LANES), rule, kind))
    done = lax.dot_general(
        both.astype(kind),
        jnp.concatenate(picks, axis=1),
        (((1,), (0,)), ((), ())),
        precision=lax.Precision.HIGHEST if kind == F32 else None,
        preferred_element_type=F32,
    )
    return [done[:, i * 2 * LANES : (i + 1) * 2 * LANES] for i in range(len(places))]


def dot_rows(lhs, rhs):
    return lax.dot_general(lhs, rhs, (((1,), (1,)), ((), ())), preferred_element_type=F32)


def strip_plan(rows, width):
    beside = max(n for n in range(1, rows + 1) if rows % n == 0 and n * width <= LANES)
    return beside, rows // beside


def turn_lanes(cells, amount):
    rows, kinds, lanes = cells.shape
    flat = pltpu.roll(cells.reshape(rows * kinds, lanes), amount % lanes, 1)
    return flat.reshape(rows, kinds, lanes)


def keep_lanes(cells, first, width):
    lane = lax.broadcasted_iota(jnp.int32, cells.shape, 2)
    return jnp.where((lane >= first) & (lane < first + width), cells, 0.0)


def packed_strip(cells, first, width):
    beside, rows = strip_plan(cells.shape[0], width)
    total = None
    for g in range(beside):
        part = turn_lanes(cells[g * rows : (g + 1) * rows], g * width - first)[:, :, :LANES]
        part = keep_lanes(part, g * width, width)
        total = part if total is None else total + part
    return total


def unpacked_strip(packed, count, width, first, lanes):
    beside, rows = strip_plan(count, width)
    wide = packed.astype(F32)
    if lanes > LANES:
        rest = jnp.zeros(packed.shape[:2] + (lanes - LANES,), F32)
        wide = jnp.concatenate([wide, rest], axis=2)
    return jnp.concatenate(
        [keep_lanes(turn_lanes(wide, first - g * width), first, width) for g in range(beside)], axis=0
    )


def main_rows(columns, halo):
    full = columns // LANES
    rest = columns - full * LANES
    return full * halo + (strip_plan(halo, rest)[1] if rest else 0)


def packed_main(cells, columns):
    full = columns // LANES
    rest = columns - full * LANES
    parts = [cells[:, :, t * LANES : (t + 1) * LANES] for t in range(full)]
    if rest:
        parts.append(packed_strip(cells, full * LANES, rest))
    return jnp.concatenate(parts, axis=0)


def unpacked_main(packed, columns, halo, lanes):
    full = columns // LANES
    rest = columns - full * LANES
    kinds = packed.shape[1]
    total = jnp.zeros((halo, kinds, lanes), F32)
    for t in range(full):
        part = packed[t * halo : (t + 1) * halo]
        total = total + unpacked_wide(part, t * LANES + halo, lanes)
    if rest:
        total = total + unpacked_strip(packed[full * halo :], halo, rest, full * LANES + halo, lanes)
    return total


def unpacked_wide(part, first, lanes):
    wide = part.astype(F32)
    if lanes > LANES:
        rest = jnp.zeros(part.shape[:2] + (lanes - LANES,), F32)
        wide = jnp.concatenate([wide, rest], axis=2)
    return turn_lanes(wide, first)


def pack_kernel(columns, halo, near_ref, up_ref, down_ref):
    cells = near_ref[...].astype(F32)
    height = cells.shape[0]
    up_ref[...] = packed_main(cells[:halo], columns).astype(BF)
    down_ref[...] = packed_main(cells[height - halo :], columns).astype(BF)


def tall_rows(columns, halo, near_ref, before_ref, after_ref):
    lanes = near_ref.shape[2]
    return [turn_lanes(near_ref[...].astype(F32), halo)] + [
        unpacked_main(ref[...], columns, halo, lanes) for ref in (before_ref, after_ref)
    ]


def side_kernel(columns, halo, near_ref, before_ref, after_ref, left_ref, right_ref):
    cells = jnp.concatenate(tall_rows(columns, halo, near_ref, before_ref, after_ref), axis=0)
    left_ref[...] = packed_strip(cells, halo, halo).astype(BF)
    right_ref[...] = packed_strip(cells, columns, halo).astype(BF)


def window_pieces(columns, halo, near_ref, before_ref, after_ref, left_ref, right_ref, p_ref):
    height, _, lanes = near_ref.shape
    tall = height + 2 * halo
    sides = unpacked_strip(left_ref[...], tall, halo, 0, lanes)
    sides = sides + unpacked_strip(right_ref[...], tall, halo, columns + halo, lanes)
    at = 0
    for rows, to in zip(tall_rows(columns, halo, near_ref, before_ref, after_ref), (halo, 0, halo + height)):
        count = rows.shape[0]
        p_ref[to : to + count] = (rows + sides[at : at + count]).astype(BF)
        at += count


def adjoint_kernel(
    columns, radius, place_ref, obs_ref, taps_ref, basis_ref, give_ref, keep_ref, acc, ys, mats, rows, lines
):
    step = pl.program_id(0)
    group, height, _ = obs_ref.shape
    span = ys.shape[3]
    width = 2 * LANES
    tiles = span // width
    chunks = ys.shape[0]
    ext = chunks * SUB
    edge = 2 * SUB
    last = columns // LANES * LANES
    batch = group_size(group, 7)

    blank_rows = jnp.zeros((LANES - edge, width), BF)

    @pl.when(step == 0)
    def _():
        for b in range(group):
            mats[b, : LANES - edge] = blank_rows
            mats[b, LANES + width + edge :] = blank_rows
        both = taps_ref[...]
        taps = both.shape[1] // 2
        for i, line in enumerate(placed_taps(both, [(taps, -radius % SUB, False), (0, 0, True)], F32)):
            lines[i] = line[:, None]

    @pl.loop(0, group, step=batch)
    def _(start):
        near = lax.broadcasted_iota(jnp.int32, (edge, width), 1) < LANES
        blank = jnp.zeros((edge, width), BF)
        for b in range(batch):
            b = start + b
            ring = toeplitz(lines[0, step * group + b], width, -round_up(radius, SUB)).astype(BF)
            top, bottom = ring[:edge], ring[width - edge :]
            mats[b, LANES - edge : LANES] = jnp.where(near, bottom, blank)
            mats[b, LANES : LANES + edge] = jnp.where(near, top, blank)
            mats[b, LANES + edge : LANES + width - edge] = ring[edge : width - edge]
            mats[b, LANES + width - edge : LANES + width] = jnp.where(near, blank, bottom)
            mats[b, LANES + width : LANES + width + edge] = jnp.where(near, blank, top)
            reach = toeplitz(lines[1, step * group + b][:, :LANES], ext, -2 * radius)[:, :height]
            high = reach.astype(BF)
            rows[b, 0] = high
            rows[b, 1] = (reach - high.astype(F32)).astype(BF)

    @pl.loop(0, group, step=batch)
    def _(start):
        fields = []
        for b in range(batch):
            cells = obs_ref[start + b]
            pieces = [jnp.zeros((height, LANES), BF), cells[:, :last]]
            if columns > last:
                fill = jnp.zeros((height, LANES - (columns - last)), BF)
                pieces.append(jnp.concatenate([cells[:, last:], fill], axis=1))
            have = sum(piece.shape[1] for piece in pieces)
            if have < span + width:
                pieces.append(jnp.zeros((height, span + width - have), BF))
            padded = jnp.concatenate(pieces, axis=1)
            stacked = jnp.concatenate(
                [padded[:, t * width : t * width + 2 * width] for t in range(tiles)], axis=0
            )
            mixed = dot(stacked, mats[start + b]).astype(BF)
            fields.append(
                jnp.concatenate([mixed[t * height : (t + 1) * height] for t in range(tiles)], axis=1)
            )
        for b in range(batch):
            done = dot(rows[start + b, 0], fields[b]) + dot(rows[start + b, 1], fields[b])
            for c in range(chunks):
                ys[c, start + b] = done[c * SUB : (c + 1) * SUB]

    bands, kinds = basis_ref.shape
    first = place_ref[0] + step * group
    turn = place_ref[1]
    pick = chosen((SUB * kinds, kinds), lambda row, lane: lane == (row + turn) % kinds)
    wide = dot_rows(pick, basis_ref[...]).astype(BF)
    here = chosen((bands, group * SUB), lambda row, lane: row == first + lane // SUB)
    same = chosen((SUB * kinds, group * SUB), lambda row, lane: row // kinds == lane % SUB, F32)
    mix = (dot(wide, here) * same).astype(BF)
    for c in range(chunks):
        cells = ys[c].reshape(group * SUB, span).astype(BF)
        total = dot(mix, cells).reshape(SUB, kinds, span)
        half = kinds // 2
        here = slice(c * SUB, (c + 1) * SUB)

        if acc.shape[0] == ext:
            @pl.when(step == 0)
            def _():
                acc[here] = total

            @pl.when(step > 0)
            def _():
                acc[here] += total

            total = acc[here]
        give_ref[here] = total[:, :half].astype(BF)
        keep_ref[here] = total[:, half:].astype(BF)


def inside(lanes, first, count, limit):
    lane = lax.broadcasted_iota(jnp.int32, (1, lanes), 1)
    at = lane + first
    return jnp.where((at >= 0) & (at < limit) & (lane < count), 1.0, 0.0)


def gram_columns_kernel(columns, columns_all, radius, place_ref, taps_ref, gl_ref):
    halo = 2 * radius
    size = 2 * LANES
    blocks = packed_blocks(columns, halo)
    tall = max(end for _, end in blocks)
    inner = round_up(columns + halo, 2 * SUB)
    both = taps_ref[...]
    taps = both.shape[1] // 2
    line, back = placed_taps(both, [(taps, 0, False), (taps, 0, True)], BF)
    mask = inside(size, place_ref[2], columns + halo, columns_all)
    for b in range(both.shape[0]):
        left = (toeplitz(back[b : b + 1], tall, -halo) * mask).astype(BF)
        right = toeplitz(line[b : b + 1], inner, -halo).astype(BF)
        right = jnp.concatenate([right, jnp.zeros((size - inner, size), BF)], axis=0)
        done = dot(left, right).astype(BF)
        at = 0
        for i, (start, end) in enumerate(blocks):
            gl_ref[b, at : at + end - start] = done[start:end, i * LANES : (i + 1) * LANES]
            at += end - start


def gram_rows_kernel(rows_all, radius, place_ref, taps_ref, basis_ref, gr_ref, sk_ref, pk_ref):
    halo = 2 * radius
    group, height, lanes = gr_ref.shape
    both = taps_ref[...]
    line, back = [part[:, :lanes] for part in placed_taps(both, [(0, 0, False), (0, 0, True)], BF)]
    mask = inside(lanes, place_ref[3], height + halo, rows_all)
    for b in range(group):
        left = (toeplitz(back[b : b + 1], height, 0) * mask).astype(BF)
        right = toeplitz(line[b : b + 1], lanes, 0).astype(BF)
        gr_ref[b] = dot(left, right).astype(BF)
    basis = basis_ref[...]
    kinds = basis.shape[1]
    up = chosen((group * SUB, group), lambda row, lane: row // SUB == lane)
    out = chosen((kinds, SUB * kinds), lambda row, lane: row == lane % kinds)
    same = chosen((group * SUB, SUB * kinds), lambda row, lane: row % SUB == lane // kinds, F32)
    sk_ref[...] = (dot(dot(up, basis).astype(BF), out) * same).astype(BF)
    up = chosen((SUB * kinds, kinds), lambda row, lane: row // SUB == lane)
    out = chosen((group, group * SUB), lambda row, lane: row == lane // SUB)
    same = chosen((SUB * kinds, group * SUB), lambda row, lane: row % SUB == lane % SUB, F32)
    pk_ref[0] = (dot(dot_rows(up, basis).astype(BF), out) * same).astype(BF)


def lane_window(cells, first, width, lanes):
    have = cells.shape[1]
    base = max(first, 0) // LANES * LANES
    stop = min(have, round_up(first + width, LANES))
    part = cells[:, base:stop]
    size = max(stop - base, lanes)
    if size > stop - base:
        part = jnp.concatenate([part, jnp.zeros((cells.shape[0], size - (stop - base)), F32)], axis=1)
    if (base - first) % size:
        part = pltpu.roll(part, (base - first) % size, 1)
    lane = lax.broadcasted_iota(jnp.int32, (cells.shape[0], lanes), 1)
    low, high = max(0, -first), min(width, have - first)
    return jnp.where((lane >= low) & (lane < high), part[:, :lanes], 0.0)


def split_kernel(starts, wide, radius, place_ref, keep_ref, got_ref, *out_refs):
    chips = len(starts)
    ext, half, span = keep_ref.shape
    lanes = out_refs[0].shape[2]
    unit = 4
    for chip in range(chips):

        @pl.when(place_ref[4] == chip)
        def _():
            for r in range(0, ext, unit):
                pair = keep_ref[r : r + unit].astype(F32) + got_ref[r : r + unit].astype(F32)
                flat = pair.reshape(unit * half, span)
                for hop in range(chips):
                    part = lane_window(flat, starts[(chip + hop) % chips], wide, lanes)
                    part = part.reshape(unit, half, lanes)
                    above, here, below = out_refs[3 * hop : 3 * hop + 3]
                    if r < radius:
                        above[r : r + unit] = part.astype(above.dtype)
                    elif r < ext - radius:
                        here[r - radius : r - radius + unit] = part.astype(here.dtype)
                    else:
                        below[r - ext + radius : r - ext + radius + unit] = part.astype(below.dtype)


def merge_kernel(radius, *refs):
    *in_refs, out_ref = refs
    height = out_ref.shape[0]
    total = in_refs[1][...].astype(F32)
    for i in range(4, len(in_refs), 3):
        total = total + in_refs[i][...].astype(F32)
    first = sum(in_refs[i][...].astype(F32) for i in range(0, len(in_refs), 3))
    last = sum(in_refs[i][...].astype(F32) for i in range(2, len(in_refs), 3))
    out_ref[:radius] = total[:radius] + first
    out_ref[radius : height - radius] = total[radius : height - radius]
    out_ref[height - radius :] = total[height - radius :] + last


def window_kernel(starts, wide, columns, halo, place_ref, mine_ref, other_ref, window_ref, own_ref):
    height, half, lanes_in = mine_ref.shape
    lanes = window_ref.shape[2]
    unit = 4
    for band in range(2 * len(starts)):
        first = band * columns - starts[band // 2]

        @pl.when(place_ref[5] == band)
        def _():
            for r in range(0, height, unit):
                for core in range(2):
                    source = mine_ref if core == band % 2 else other_ref
                    flat = source[r : r + unit].reshape(unit * half, lanes_in)
                    kinds = slice(core * half, (core + 1) * half)
                    part = lane_window(flat, first - halo, columns + 2 * halo, lanes)
                    window_ref[r : r + unit, kinds] = part.reshape(unit, half, lanes).astype(BF)
                    part = lane_window(flat, first, columns, lanes)
                    own_ref[r : r + unit, kinds] = part.reshape(unit, half, lanes)


def first_kernel(columns, halo, group, before, window, after, *rest):
    normal_kernel(columns, halo, group, True, (before, window, after), *rest)


def second_kernel(columns, halo, group, near_ref, before, after, left, right, *rest):
    *rest, p_ref = rest

    @pl.when(pl.program_id(0) == 0)
    def _():
        window_pieces(columns, halo, near_ref, before, after, left, right, p_ref)

    normal_kernel(columns, halo, group, False, (p_ref,), *rest)


def normal_kernel(
    columns, halo, group, first, p_refs, own_ref, ridge_ref, sk_ref, pk_ref, gr_ref, gl_ref, out_ref, sums_ref, acc, xs, ys
):
    step = pl.program_id(0)
    height = gr_ref.shape[1]
    from_band = step * group
    _, kinds, lanes = p_refs[0].shape
    sources = [(ref, s) for ref in p_refs for s in range(0, ref.shape[0], SUB)]
    ext = SUB * len(sources)
    chunks = height // SUB

    @pl.when(step == 0)
    def _():
        acc[...] = jnp.zeros_like(acc)

    spread = sk_ref[pl.ds(pl.multiple_of(from_band * SUB, group * SUB), group * SUB)]
    for c in range(0, ext, 2 * SUB):
        halves = []
        for ref, s in sources[c // SUB : c // SUB + 2]:
            cells = ref[s : s + SUB].reshape(SUB * kinds, lanes)
            halves.append(dot(spread, cells).reshape(group, SUB, lanes))
        xs[:, c : c + 2 * SUB, :] = jnp.concatenate(halves, axis=1).astype(BF)

    blocks = packed_blocks(columns, halo)
    mids = [dot(gr_ref[from_band + b, :, :ext], xs[b]).astype(BF) for b in range(group)]
    for b in range(group):
        parts = []
        at = 0
        for i in range(lanes // LANES):
            if i < len(blocks):
                start, end = blocks[i]
                part = [gl_ref[from_band + b, at : at + end - start]]
                at += end - start
                if start:
                    part = [jnp.zeros((start, LANES), BF)] + part
                if end < lanes:
                    part = part + [jnp.zeros((lanes - end, LANES), BF)]
                parts.append(jnp.concatenate(part, axis=0))
            else:
                parts.append(jnp.zeros((lanes, LANES), BF))
        done = dot(mids[b], jnp.concatenate(parts, axis=1))
        for c in range(chunks):
            ys[c, b] = done[c * SUB : (c + 1) * SUB]

    gather = pk_ref[step]
    for c in range(chunks):
        acc[c] += dot(gather, ys[c].reshape(group * SUB, lanes).astype(BF))

    @pl.when(step == pl.num_programs(0) - 1)
    def _():
        lane = lax.broadcasted_iota(jnp.int32, (kinds, SUB, lanes), 2)
        totals = [jnp.zeros((SUB, lanes), F32) for _ in range(3)]
        for c in range(chunks):
            own = own_ref[:, c * SUB : (c + 1) * SUB, :]
            image = acc[c].reshape(kinds, SUB, lanes) + ridge_ref[...] * own
            image = jnp.where(lane < columns, image, 0.0)
            out_ref[:, c * SUB : (c + 1) * SUB, :] = image
            pairs = [own * image]
            if first:
                pairs += [own * own, image * image]
            for i, pair in enumerate(pairs):
                totals[i] = totals[i] + jnp.sum(pair, axis=0)
        flat = [
            jnp.sum(
                jnp.concatenate(
                    [total[:, i : i + LANES] for i in range(0, lanes, LANES)], axis=0
                ),
                axis=0,
                keepdims=True,
            )
            for total in totals
        ]
        row = lax.broadcasted_iota(jnp.int32, (SUB, LANES), 0)
        packed = jnp.zeros((SUB, LANES), F32)
        for i, line in enumerate(flat):
            packed = packed + jnp.where(row == i, jnp.broadcast_to(line, (SUB, LANES)), 0.0)
        sums_ref[...] = packed


def combine_kernel(shared_ref, v0_ref, v1_ref, v2_ref, coef_ref, res_ref):
    columns = coef_ref.shape[2]
    lines = jnp.sum(shared_ref[...], axis=0)
    v01, v00, v11, v12 = [jnp.sum(lines[i : i + 1], axis=1, keepdims=True) for i in range(4)]
    alpha = v00 / v01
    norm = v00 - 2.0 * alpha * v01 + alpha * alpha * v11
    lead = 1.0 + norm / v00
    product = lead * lead * v01 - 2.0 * lead * alpha * v11 + alpha * alpha * v12
    second = norm / product
    one = alpha + second * lead
    two = second * alpha
    for k in range(coef_ref.shape[0]):
        v0, v1, v2 = v0_ref[k], v1_ref[k], v2_ref[k]
        coef_ref[k] = (one * v0 - two * v1)[:, :columns]
        res_ref[k] = (v0 - one * v1 + two * v2)[:, :columns]


def shift_both(low_edge, high_edge, axis):
    count = lax.axis_size(axis)
    from_before = lax.ppermute(high_edge, axis, [(i, i + 1) for i in range(count - 1)])
    from_after = lax.ppermute(low_edge, axis, [(i + 1, i) for i in range(count - 1)])
    return from_before, from_after


def local(observed, row_taps, col_taps, spectral_basis, ridge_weights):
    bands_here, height, columns_all = observed.shape
    taps = row_taps.shape[1]
    radius = (taps - 1) // 2
    halo = 2 * radius
    bands, kinds = spectral_basis.shape
    n_band = lax.axis_size("band")
    n_row = lax.axis_size("row")
    columns = columns_all // n_band
    lanes = round_up(columns + 2 * halo, 2 * LANES)
    me_band = lax.axis_index("band")
    me_row = lax.axis_index("row")
    core = me_band % 2
    chip = me_band // 2
    chips = n_band // 2

    plain = jnp.concatenate([row_taps, col_taps], axis=1)
    everyone = [(plain, me_band)]
    for hop in range(1, n_band):
        moves = [(i, (i + hop) % n_band) for i in range(n_band)]
        everyone.append((lax.ppermute(plain, "band", moves), (me_band - hop) % n_band))
    basis_all = jnp.concatenate(
        [lax.dynamic_slice_in_dim(spectral_basis, at * bands_here, bands_here, 0) for _, at in everyone]
    )
    every = jnp.concatenate([values for values, _ in everyone])

    half = kinds // 2
    place = jnp.stack(
        [
            me_band * bands_here,
            half * (1 - core),
            me_band * columns - radius,
            me_row * height - radius,
            chip,
            me_band,
        ]
    ).astype(jnp.int32)
    whole = lambda shape: pl.BlockSpec(shape, lambda i: (0,) * len(shape))

    few = group_size(bands_here, 64)
    span = round_up(columns_all, 2 * LANES)
    ext = height + 2 * radius
    chunks = ext // SUB
    give, keep = pl.pallas_call(
        functools.partial(adjoint_kernel, columns_all, radius),
        grid=(bands_here // few,),
        in_specs=[
            pl.BlockSpec(memory_space=pltpu.SMEM),
            pl.BlockSpec((few, height, columns_all), lambda i: (i, 0, 0)),
            whole(plain.shape),
            whole((bands, kinds)),
        ],
        out_specs=[whole((ext, half, span))] * 2,
        out_shape=[jax.ShapeDtypeStruct((ext, half, span), BF)] * 2,
        scratch_shapes=[
            pltpu.VMEM((ext if few < bands_here else SUB, kinds, span), F32),
            pltpu.VMEM((chunks, few, SUB, span), F32),
            pltpu.VMEM((few, 4 * LANES, 2 * LANES), BF),
            pltpu.VMEM((few, 2, ext, height), BF),
            pltpu.VMEM((2, bands_here, 1, 2 * LANES), F32),
        ],
        compiler_params=pltpu.CompilerParams(vmem_limit_bytes=VMEM_LIMIT),
        cost_estimate=pl.CostEstimate(
            flops=bands_here * 2 * 96 * 512 * 256, bytes_accessed=observed.size * 2, transcendentals=0
        ),
        name="adjoint",
    )(place, observed, plain, spectral_basis)


    part = group_size(bands, 32)
    deep = sum(end - start for start, end in packed_blocks(columns, halo))
    taps_spec = pl.BlockSpec((part, 2 * taps), lambda i: (i, 0))
    smem = pl.BlockSpec(memory_space=pltpu.SMEM)
    params = pltpu.CompilerParams(vmem_limit_bytes=SMALL_LIMIT)
    gr, sk, pk = pl.pallas_call(
        functools.partial(gram_rows_kernel, height * n_row, radius),
        grid=(bands // part,),
        in_specs=[smem, taps_spec, pl.BlockSpec((part, kinds), lambda i: (i, 0))],
        out_specs=[
            pl.BlockSpec((part, height, LANES), lambda i: (i, 0, 0)),
            pl.BlockSpec((part * SUB, SUB * kinds), lambda i: (i, 0)),
            pl.BlockSpec((1, SUB * kinds, part * SUB), lambda i: (i, 0, 0)),
        ],
        out_shape=[
            jax.ShapeDtypeStruct((bands, height, LANES), BF),
            jax.ShapeDtypeStruct((bands * SUB, SUB * kinds), BF),
            jax.ShapeDtypeStruct((bands // part, SUB * kinds, part * SUB), BF),
        ],
        compiler_params=params,
        cost_estimate=pl.CostEstimate(
            flops=bands * 2 * LANES**3, bytes_accessed=bands * height * LANES * 2, transcendentals=0
        ),
        name="gram_rows",
    )(place, every, basis_all)
    gl = pl.pallas_call(
        functools.partial(gram_columns_kernel, columns, columns_all, radius),
        grid=(bands // part,),
        in_specs=[smem, taps_spec],
        out_specs=pl.BlockSpec((part, deep, LANES), lambda i: (i, 0, 0)),
        out_shape=jax.ShapeDtypeStruct((bands, deep, LANES), BF),
        compiler_params=params,
        cost_estimate=pl.CostEstimate(
            flops=bands * 2 * (2 * LANES) ** 3, bytes_accessed=bands * deep * LANES * 2, transcendentals=0
        ),
        name="gram_columns",
    )(place, every)

    pairs = [(i, i ^ 1) for i in range(n_band)]
    got = lax.ppermute(give, "band", pairs)
    wide = min(columns_all, 2 * columns + (2 * halo if chips > 2 else halo))
    wide_lanes = round_up(wide, LANES)
    starts = [min(max(2 * columns * c - halo, 0), columns_all - wide) for c in range(chips)]
    vmem = pl.BlockSpec(memory_space=pltpu.VMEM)
    shape = lambda rows, kind: jax.ShapeDtypeStruct((rows, half, wide_lanes), kind)
    sends = pl.pallas_call(
        functools.partial(split_kernel, starts, wide, radius),
        in_specs=[smem, vmem, vmem],
        out_shape=[
            shape(rows, F32 if rows == height and hop == 0 else BF)
            for hop in range(chips)
            for rows in (radius, height, radius)
        ],
        compiler_params=pltpu.CompilerParams(vmem_limit_bytes=VMEM_LIMIT),
        name="split",
    )(place, keep, got)

    def moves(hop, step):
        return [
            (b * n_row + r, (b + 2 * hop) % n_band * n_row + r + step)
            for b in range(n_band)
            for r in range(n_row)
            if 0 <= r + step < n_row
        ]

    parts = []
    axes = ("band", "row")
    for hop in range(chips):
        above, here, below = sends[3 * hop : 3 * hop + 3]
        after = lax.ppermute(above, axes, moves(hop, -1))
        before = lax.ppermute(below, axes, moves(hop, 1))
        if hop:
            here = lax.ppermute(here, axes, moves(hop, 0))
        parts += [before, here, after]
    parts[1], gr, sk, pk = lax.optimization_barrier((parts[1], gr, sk, pk))
    total = pl.pallas_call(
        functools.partial(merge_kernel, radius),
        out_shape=shape(height, F32),
        compiler_params=params,
        name="merge",
    )(*parts)
    other = lax.ppermute(total, "band", pairs)
    window, v0 = pl.pallas_call(
        functools.partial(window_kernel, starts, wide, columns, halo),
        in_specs=[smem, vmem, vmem],
        out_shape=[
            jax.ShapeDtypeStruct((height, kinds, lanes), BF),
            jax.ShapeDtypeStruct((height, kinds, lanes), F32),
        ],
        compiler_params=params,
        name="window",
    )(place, total, other)
    v0 = jnp.swapaxes(v0, 0, 1)

    group = part
    ridge = jnp.broadcast_to(ridge_weights[:, None, None], (kinds, SUB, lanes))
    tall = height + 2 * halo

    def normal_map(pieces, own, first):
        window = [pltpu.VMEM((tall, kinds, lanes), BF)] if not first else []
        return pl.pallas_call(
            functools.partial(first_kernel if first else second_kernel, columns, halo, group),
            grid=(bands // group,),
            in_specs=[vmem] * (len(pieces) + 6),
            out_specs=[vmem, vmem],
            out_shape=[
                jax.ShapeDtypeStruct((kinds, height, lanes), F32),
                jax.ShapeDtypeStruct((SUB, LANES), F32),
            ],
            scratch_shapes=[
                pltpu.VMEM((height // SUB, SUB * kinds, lanes), F32),
                pltpu.VMEM((group, tall, lanes), BF),
                pltpu.VMEM((height // SUB, group, SUB, lanes), F32),
            ]
            + window,
            compiler_params=pltpu.CompilerParams(vmem_limit_bytes=SMALL_LIMIT),
            cost_estimate=pl.CostEstimate(
                flops=bands * 2 * 32 * 512 * 256, bytes_accessed=bands * deep * LANES * 2, transcendentals=0
            ),
            name="normal",
        )(*pieces, own, ridge, sk, pk, gr, gl)

    before, after = shift_both(window[:halo], window[height - halo :], "row")
    v1, sums1 = normal_map([before, window, after], v0, True)
    near = jnp.swapaxes(v1.astype(BF), 0, 1)
    main = jax.ShapeDtypeStruct((main_rows(columns, halo), kinds, LANES), BF)
    up, down = pl.pallas_call(
        functools.partial(pack_kernel, columns, halo),
        out_shape=[main, main],
        compiler_params=params,
        name="pack",
    )(near)
    before, after = shift_both(up, down, "row")
    side = jax.ShapeDtypeStruct((strip_plan(tall, halo)[1], kinds, LANES), BF)
    left, right = pl.pallas_call(
        functools.partial(side_kernel, columns, halo),
        out_shape=[side, side],
        compiler_params=params,
        name="sides",
    )(near, before, after)
    left, right = shift_both(left, right, "band")
    pieces = [near, before, after, left, right]
    v2, sums2 = normal_map(pieces, v1, False)

    sums = jnp.concatenate([sums1[:3], sums2[:1], jnp.zeros((SUB - 4, LANES), F32)])
    mine = jnp.broadcast_to(sums[None], (n_band * n_row, SUB, LANES))
    shared = lax.all_to_all(mine, ("band", "row"), 0, 0, tiled=True)
    out = jax.ShapeDtypeStruct((kinds, height, columns), F32)
    return pl.pallas_call(
        combine_kernel,
        out_shape=[out, out],
        compiler_params=pltpu.CompilerParams(vmem_limit_bytes=SMALL_LIMIT),
        name="combine",
    )(shared, v0, v1, v2)


def solution(mesh):
    in_specs = (P("band", "row", None), P("band", None), P("band", None), P(), P())
    out_specs = (P(None, "row", "band"), P(None, "row", "band"))
    return jax.shard_map(local, mesh=mesh, in_specs=in_specs, out_specs=out_specs, check_vma=False)
```

```python
import functools

import jax
import jax.numpy as jnp
from jax import lax
from jax.experimental import pallas as pl
from jax.experimental.pallas import tpu as pltpu
from jax.sharding import PartitionSpec as P

LANES = 128
SUB = 8
BF = jnp.bfloat16
F32 = jnp.float32
VMEM_LIMIT = 50 * 1024 * 1024
SMALL_LIMIT = 20 * 1024 * 1024


def round_up(value, unit):
    return (value + unit - 1) // unit * unit


def group_size(count, most):
    return max(size for size in range(1, most + 1) if count % size == 0)


def packed_blocks(columns, halo):
    out = []
    for first in range(0, columns, LANES):
        out.append((first, round_up(min(first + LANES, columns) + 2 * halo, 2 * SUB)))
    return out


def dot(lhs, rhs):
    return lax.dot_general(lhs, rhs, (((1,), (0,)), ((), ())), preferred_element_type=F32)


def toeplitz(taps, rows, shift):
    lanes = taps.shape[1]
    pieces = []
    for first in range(0, rows, LANES):
        count = min(LANES, rows - first)
        wide = jnp.broadcast_to(taps, (count, lanes))
        pieces.append(pltpu.roll(wide, (shift + first) % lanes, 1, stride=1, stride_axis=0))
    return jnp.concatenate(pieces, axis=0) if len(pieces) > 1 else pieces[0]


def chosen(shape, rule, kind=BF):
    row = lax.broadcasted_iota(jnp.int32, shape, 0)
    lane = lax.broadcasted_iota(jnp.int32, shape, 1)
    return jnp.where(rule(row, lane), 1.0, 0.0).astype(kind)


def placed_taps(both, places, kind):
    count = both.shape[1] // 2
    picks = []
    for first, lead, flip in places:

        def rule(row, lane):
            at = lane - lead
            here = (at >= 0) & (at < count)
            return here & (row == first + (count - 1 - at if flip else at))

        picks.append(chosen((both.shape[1], 2 * LANES), rule, kind))
    done = lax.dot_general(
        both.astype(kind),
        jnp.concatenate(picks, axis=1),
        (((1,), (0,)), ((), ())),
        precision=lax.Precision.HIGHEST if kind == F32 else None,
        preferred_element_type=F32,
    )
    return [done[:, i * 2 * LANES : (i + 1) * 2 * LANES] for i in range(len(places))]


def dot_rows(lhs, rhs):
    return lax.dot_general(lhs, rhs, (((1,), (1,)), ((), ())), preferred_element_type=F32)


def strip_plan(rows, width):
    beside = max(n for n in range(1, rows + 1) if rows % n == 0 and n * width <= LANES)
    return beside, rows // beside


def turn_lanes(cells, amount):
    rows, kinds, lanes = cells.shape
    flat = pltpu.roll(cells.reshape(rows * kinds, lanes), amount % lanes, 1)
    return flat.reshape(rows, kinds, lanes)


def keep_lanes(cells, first, width):
    lane = lax.broadcasted_iota(jnp.int32, cells.shape, 2)
    return jnp.where((lane >= first) & (lane < first + width), cells, 0.0)


def packed_strip(cells, first, width):
    beside, rows = strip_plan(cells.shape[0], width)
    total = None
    for g in range(beside):
        part = turn_lanes(cells[g * rows : (g + 1) * rows], g * width - first)[:, :, :LANES]
        part = keep_lanes(part, g * width, width)
        total = part if total is None else total + part
    return total


def unpacked_strip(packed, count, width, first, lanes):
    beside, rows = strip_plan(count, width)
    wide = packed.astype(F32)
    if lanes > LANES:
        rest = jnp.zeros(packed.shape[:2] + (lanes - LANES,), F32)
        wide = jnp.concatenate([wide, rest], axis=2)
    return jnp.concatenate(
        [keep_lanes(turn_lanes(wide, first - g * width), first, width) for g in range(beside)], axis=0
    )


def main_rows(columns, halo):
    full = columns // LANES
    rest = columns - full * LANES
    return full * halo + (strip_plan(halo, rest)[1] if rest else 0)


def packed_main(cells, columns):
    full = columns // LANES
    rest = columns - full * LANES
    parts = [cells[:, :, t * LANES : (t + 1) * LANES] for t in range(full)]
    if rest:
        parts.append(packed_strip(cells, full * LANES, rest))
    return jnp.concatenate(parts, axis=0)


def unpacked_main(packed, columns, halo, lanes):
    full = columns // LANES
    rest = columns - full * LANES
    kinds = packed.shape[1]
    total = jnp.zeros((halo, kinds, lanes), F32)
    for t in range(full):
        part = packed[t * halo : (t + 1) * halo]
        total = total + unpacked_wide(part, t * LANES + halo, lanes)
    if rest:
        total = total + unpacked_strip(packed[full * halo :], halo, rest, full * LANES + halo, lanes)
    return total


def unpacked_wide(part, first, lanes):
    wide = part.astype(F32)
    if lanes > LANES:
        rest = jnp.zeros(part.shape[:2] + (lanes - LANES,), F32)
        wide = jnp.concatenate([wide, rest], axis=2)
    return turn_lanes(wide, first)


def pack_kernel(columns, halo, near_ref, up_ref, down_ref):
    cells = near_ref[...].astype(F32)
    height = cells.shape[0]
    up_ref[...] = packed_main(cells[:halo], columns).astype(BF)
    down_ref[...] = packed_main(cells[height - halo :], columns).astype(BF)


def tall_rows(columns, halo, near_ref, before_ref, after_ref):
    lanes = near_ref.shape[2]
    return [turn_lanes(near_ref[...].astype(F32), halo)] + [
        unpacked_main(ref[...], columns, halo, lanes) for ref in (before_ref, after_ref)
    ]


def side_kernel(columns, halo, near_ref, before_ref, after_ref, left_ref, right_ref):
    cells = jnp.concatenate(tall_rows(columns, halo, near_ref, before_ref, after_ref), axis=0)
    left_ref[...] = packed_strip(cells, halo, halo).astype(BF)
    right_ref[...] = packed_strip(cells, columns, halo).astype(BF)


def window_pieces(columns, halo, near_ref, before_ref, after_ref, left_ref, right_ref, p_ref):
    height, _, lanes = near_ref.shape
    tall = height + 2 * halo
    sides = unpacked_strip(left_ref[...], tall, halo, 0, lanes)
    sides = sides + unpacked_strip(right_ref[...], tall, halo, columns + halo, lanes)
    at = 0
    for rows, to in zip(tall_rows(columns, halo, near_ref, before_ref, after_ref), (halo, 0, halo + height)):
        count = rows.shape[0]
        p_ref[to : to + count] = (rows + sides[at : at + count]).astype(BF)
        at += count


def adjoint_kernel(
    columns, radius, place_ref, obs_ref, taps_ref, basis_ref, give_ref, keep_ref, acc, ys, mats, rows, lines
):
    step = pl.program_id(0)
    group, height, _ = obs_ref.shape
    span = ys.shape[3]
    width = 2 * LANES
    tiles = span // width
    chunks = ys.shape[0]
    ext = chunks * SUB
    edge = 2 * SUB
    last = columns // LANES * LANES
    batch = group_size(group, 7)

    blank_rows = jnp.zeros((LANES - edge, width), BF)

    @pl.when(step == 0)
    def _():
        for b in range(group):
            mats[b, : LANES - edge] = blank_rows
            mats[b, LANES + width + edge :] = blank_rows
        both = taps_ref[...]
        taps = both.shape[1] // 2
        for i, line in enumerate(placed_taps(both, [(taps, -radius % SUB, False), (0, 0, True)], F32)):
            lines[i] = line[:, None]

    @pl.loop(0, group, step=batch)
    def _(start):
        near = lax.broadcasted_iota(jnp.int32, (edge, width), 1) < LANES
        blank = jnp.zeros((edge, width), BF)
        for b in range(batch):
            b = start + b
            ring = toeplitz(lines[0, step * group + b], width, -round_up(radius, SUB)).astype(BF)
            top, bottom = ring[:edge], ring[width - edge :]
            mats[b, LANES - edge : LANES] = jnp.where(near, bottom, blank)
            mats[b, LANES : LANES + edge] = jnp.where(near, top, blank)
            mats[b, LANES + edge : LANES + width - edge] = ring[edge : width - edge]
            mats[b, LANES + width - edge : LANES + width] = jnp.where(near, blank, bottom)
            mats[b, LANES + width : LANES + width + edge] = jnp.where(near, blank, top)
            reach = toeplitz(lines[1, step * group + b][:, :LANES], ext, -2 * radius)[:, :height]
            high = reach.astype(BF)
            rows[b, 0] = high
            rows[b, 1] = (reach - high.astype(F32)).astype(BF)

    @pl.loop(0, group, step=batch)
    def _(start):
        fields = []
        for b in range(batch):
            cells = obs_ref[start + b]
            pieces = [jnp.zeros((height, LANES), BF), cells[:, :last]]
            if columns > last:
                fill = jnp.zeros((height, LANES - (columns - last)), BF)
                pieces.append(jnp.concatenate([cells[:, last:], fill], axis=1))
            have = sum(piece.shape[1] for piece in pieces)
            if have < span + width:
                pieces.append(jnp.zeros((height, span + width - have), BF))
            padded = jnp.concatenate(pieces, axis=1)
            stacked = jnp.concatenate(
                [padded[:, t * width : t * width + 2 * width] for t in range(tiles)], axis=0
            )
            mixed = dot(stacked, mats[start + b]).astype(BF)
            fields.append(
                jnp.concatenate([mixed[t * height : (t + 1) * height] for t in range(tiles)], axis=1)
            )
        for b in range(batch):
            done = dot(rows[start + b, 0], fields[b]) + dot(rows[start + b, 1], fields[b])
            for c in range(chunks):
                ys[c, start + b] = done[c * SUB : (c + 1) * SUB]

    bands, kinds = basis_ref.shape
    first = place_ref[0] + step * group
    turn = place_ref[1]
    pick = chosen((SUB * kinds, kinds), lambda row, lane: lane == (row + turn) % kinds)
    wide = dot_rows(pick, basis_ref[...]).astype(BF)
    here = chosen((bands, group * SUB), lambda row, lane: row == first + lane // SUB)
    same = chosen((SUB * kinds, group * SUB), lambda row, lane: row // kinds == lane % SUB, F32)
    mix = (dot(wide, here) * same).astype(BF)
    for c in range(chunks):
        cells = ys[c].reshape(group * SUB, span).astype(BF)
        total = dot(mix, cells).reshape(SUB, kinds, span)
        half = kinds // 2
        here = slice(c * SUB, (c + 1) * SUB)

        if acc.shape[0] == ext:
            @pl.when(step == 0)
            def _():
                acc[here] = total

            @pl.when(step > 0)
            def _():
                acc[here] += total

            total = acc[here]
        give_ref[here] = total[:, :half].astype(BF)
        keep_ref[here] = total[:, half:].astype(BF)


def inside(lanes, first, count, limit):
    lane = lax.broadcasted_iota(jnp.int32, (1, lanes), 1)
    at = lane + first
    return jnp.where((at >= 0) & (at < limit) & (lane < count), 1.0, 0.0)


def gram_columns_kernel(columns, columns_all, radius, place_ref, taps_ref, gl_ref):
    halo = 2 * radius
    size = 2 * LANES
    blocks = packed_blocks(columns, halo)
    tall = max(end for _, end in blocks)
    inner = round_up(columns + halo, 2 * SUB)
    both = taps_ref[...]
    taps = both.shape[1] // 2
    line, back = placed_taps(both, [(taps, 0, False), (taps, 0, True)], BF)
    mask = inside(size, place_ref[2], columns + halo, columns_all)
    for b in range(both.shape[0]):
        left = (toeplitz(back[b : b + 1], tall, -halo) * mask).astype(BF)
        right = toeplitz(line[b : b + 1], inner, -halo).astype(BF)
        right = jnp.concatenate([right, jnp.zeros((size - inner, size), BF)], axis=0)
        done = dot(left, right).astype(BF)
        at = 0
        for i, (start, end) in enumerate(blocks):
            gl_ref[b, at : at + end - start] = done[start:end, i * LANES : (i + 1) * LANES]
            at += end - start


def gram_rows_kernel(rows_all, radius, place_ref, taps_ref, basis_ref, gr_ref, sk_ref, pk_ref):
    halo = 2 * radius
    group, height, lanes = gr_ref.shape
    both = taps_ref[...]
    line, back = [part[:, :lanes] for part in placed_taps(both, [(0, 0, False), (0, 0, True)], BF)]
    mask = inside(lanes, place_ref[3], height + halo, rows_all)
    for b in range(group):
        left = (toeplitz(back[b : b + 1], height, 0) * mask).astype(BF)
        right = toeplitz(line[b : b + 1], lanes, 0).astype(BF)
        gr_ref[b] = dot(left, right).astype(BF)
    basis = basis_ref[...].astype(BF)
    kinds = basis.shape[1]
    up = chosen((group * SUB, group), lambda row, lane: row // SUB == lane)
    out = chosen((kinds, SUB * kinds), lambda row, lane: row == lane % kinds)
    same = chosen((group * SUB, SUB * kinds), lambda row, lane: row % SUB == lane // kinds, F32)
    sk_ref[...] = (dot(dot(up, basis).astype(BF), out) * same).astype(BF)
    up = chosen((SUB * kinds, kinds), lambda row, lane: row // SUB == lane)
    out = chosen((group, group * SUB), lambda row, lane: row == lane // SUB)
    same = chosen((SUB * kinds, group * SUB), lambda row, lane: row % SUB == lane % SUB, F32)
    pk_ref[0] = (dot(dot_rows(up, basis).astype(BF), out) * same).astype(BF)


def lane_window(cells, first, width, lanes):
    have = cells.shape[1]
    base = max(first, 0) // LANES * LANES
    stop = min(have, round_up(first + width, LANES))
    part = cells[:, base:stop]
    size = max(stop - base, lanes)
    if size > stop - base:
        part = jnp.concatenate([part, jnp.zeros((cells.shape[0], size - (stop - base)), F32)], axis=1)
    if (base - first) % size:
        part = pltpu.roll(part, (base - first) % size, 1)
    lane = lax.broadcasted_iota(jnp.int32, (cells.shape[0], lanes), 1)
    low, high = max(0, -first), min(width, have - first)
    return jnp.where((lane >= low) & (lane < high), part[:, :lanes], 0.0)


def split_kernel(starts, wide, radius, place_ref, keep_ref, got_ref, *out_refs):
    chips = len(starts)
    ext, half, span = keep_ref.shape
    lanes = out_refs[0].shape[2]
    unit = 4
    for chip in range(chips):

        @pl.when(place_ref[4] == chip)
        def _():
            for r in range(0, ext, unit):
                pair = keep_ref[r : r + unit].astype(F32) + got_ref[r : r + unit].astype(F32)
                flat = pair.reshape(unit * half, span)
                for hop in range(chips):
                    part = lane_window(flat, starts[(chip + hop) % chips], wide, lanes)
                    part = part.reshape(unit, half, lanes)
                    above, here, below = out_refs[3 * hop : 3 * hop + 3]
                    if r < radius:
                        above[r : r + unit] = part.astype(above.dtype)
                    elif r < ext - radius:
                        here[r - radius : r - radius + unit] = part.astype(here.dtype)
                    else:
                        below[r - ext + radius : r - ext + radius + unit] = part.astype(below.dtype)


def merge_kernel(radius, *refs):
    *in_refs, out_ref = refs
    height = out_ref.shape[0]
    total = in_refs[1][...].astype(F32)
    for i in range(4, len(in_refs), 3):
        total = total + in_refs[i][...].astype(F32)
    first = sum(in_refs[i][...].astype(F32) for i in range(0, len(in_refs), 3))
    last = sum(in_refs[i][...].astype(F32) for i in range(2, len(in_refs), 3))
    out_ref[:radius] = total[:radius] + first
    out_ref[radius : height - radius] = total[radius : height - radius]
    out_ref[height - radius :] = total[height - radius :] + last


def window_kernel(starts, wide, columns, halo, place_ref, mine_ref, other_ref, window_ref, own_ref):
    height, half, lanes_in = mine_ref.shape
    lanes = window_ref.shape[2]
    unit = 4
    for band in range(2 * len(starts)):
        first = band * columns - starts[band // 2]

        @pl.when(place_ref[5] == band)
        def _():
            for r in range(0, height, unit):
                for core in range(2):
                    source = mine_ref if core == band % 2 else other_ref
                    flat = source[r : r + unit].reshape(unit * half, lanes_in)
                    kinds = slice(core * half, (core + 1) * half)
                    part = lane_window(flat, first - halo, columns + 2 * halo, lanes)
                    window_ref[r : r + unit, kinds] = part.reshape(unit, half, lanes).astype(BF)
                    part = lane_window(flat, first, columns, lanes)
                    own_ref[r : r + unit, kinds] = part.reshape(unit, half, lanes)


def first_kernel(columns, halo, group, before, window, after, *rest):
    normal_kernel(columns, halo, group, True, (before, window, after), *rest)


def second_kernel(columns, halo, group, near_ref, before, after, left, right, *rest):
    *rest, p_ref = rest

    @pl.when(pl.program_id(0) == 0)
    def _():
        window_pieces(columns, halo, near_ref, before, after, left, right, p_ref)

    normal_kernel(columns, halo, group, False, (p_ref,), *rest)


def normal_kernel(
    columns, halo, group, first, p_refs, own_ref, ridge_ref, sk_ref, pk_ref, gr_ref, gl_ref, out_ref, sums_ref, acc, xs, ys
):
    step = pl.program_id(0)
    height = gr_ref.shape[1]
    from_band = step * group
    _, kinds, lanes = p_refs[0].shape
    sources = [(ref, s) for ref in p_refs for s in range(0, ref.shape[0], SUB)]
    ext = SUB * len(sources)
    chunks = height // SUB

    @pl.when(step == 0)
    def _():
        acc[...] = jnp.zeros_like(acc)

    spread = sk_ref[pl.ds(pl.multiple_of(from_band * SUB, group * SUB), group * SUB)]
    for c in range(0, ext, 2 * SUB):
        halves = []
        for ref, s in sources[c // SUB : c // SUB + 2]:
            cells = ref[s : s + SUB].reshape(SUB * kinds, lanes)
            halves.append(dot(spread, cells).reshape(group, SUB, lanes))
        xs[:, c : c + 2 * SUB, :] = jnp.concatenate(halves, axis=1).astype(BF)

    blocks = packed_blocks(columns, halo)
    mids = [dot(gr_ref[from_band + b, :, :ext], xs[b]).astype(BF) for b in range(group)]
    for b in range(group):
        parts = []
        at = 0
        for i in range(lanes // LANES):
            if i < len(blocks):
                start, end = blocks[i]
                part = [gl_ref[from_band + b, at : at + end - start]]
                at += end - start
                if start:
                    part = [jnp.zeros((start, LANES), BF)] + part
                if end < lanes:
                    part = part + [jnp.zeros((lanes - end, LANES), BF)]
                parts.append(jnp.concatenate(part, axis=0))
            else:
                parts.append(jnp.zeros((lanes, LANES), BF))
        done = dot(mids[b], jnp.concatenate(parts, axis=1))
        for c in range(chunks):
            ys[c, b] = done[c * SUB : (c + 1) * SUB]

    gather = pk_ref[step]
    for c in range(chunks):
        acc[c] += dot(gather, ys[c].reshape(group * SUB, lanes).astype(BF))

    @pl.when(step == pl.num_programs(0) - 1)
    def _():
        lane = lax.broadcasted_iota(jnp.int32, (kinds, SUB, lanes), 2)
        totals = [jnp.zeros((SUB, lanes), F32) for _ in range(3)]
        for c in range(chunks):
            own = own_ref[:, c * SUB : (c + 1) * SUB, :]
            image = acc[c].reshape(kinds, SUB, lanes) + ridge_ref[...] * own
            image = jnp.where(lane < columns, image, 0.0)
            out_ref[:, c * SUB : (c + 1) * SUB, :] = image
            pairs = [own * image]
            if first:
                pairs += [own * own, image * image]
            for i, pair in enumerate(pairs):
                totals[i] = totals[i] + jnp.sum(pair, axis=0)
        flat = [
            jnp.sum(
                jnp.concatenate(
                    [total[:, i : i + LANES] for i in range(0, lanes, LANES)], axis=0
                ),
                axis=0,
                keepdims=True,
            )
            for total in totals
        ]
        row = lax.broadcasted_iota(jnp.int32, (SUB, LANES), 0)
        packed = jnp.zeros((SUB, LANES), F32)
        for i, line in enumerate(flat):
            packed = packed + jnp.where(row == i, jnp.broadcast_to(line, (SUB, LANES)), 0.0)
        sums_ref[...] = packed


def combine_kernel(shared_ref, v0_ref, v1_ref, v2_ref, coef_ref, res_ref):
    columns = coef_ref.shape[2]
    lines = jnp.sum(shared_ref[...], axis=0)
    v01, v00, v11, v12 = [jnp.sum(lines[i : i + 1], axis=1, keepdims=True) for i in range(4)]
    alpha = v00 / v01
    norm = v00 - 2.0 * alpha * v01 + alpha * alpha * v11
    lead = 1.0 + norm / v00
    product = lead * lead * v01 - 2.0 * lead * alpha * v11 + alpha * alpha * v12
    second = norm / product
    one = alpha + second * lead
    two = second * alpha
    for k in range(coef_ref.shape[0]):
        v0, v1, v2 = v0_ref[k], v1_ref[k], v2_ref[k]
        coef_ref[k] = (one * v0 - two * v1)[:, :columns]
        res_ref[k] = (v0 - one * v1 + two * v2)[:, :columns]


def shift_both(low_edge, high_edge, axis):
    count = lax.axis_size(axis)
    from_before = lax.ppermute(high_edge, axis, [(i, i + 1) for i in range(count - 1)])
    from_after = lax.ppermute(low_edge, axis, [(i + 1, i) for i in range(count - 1)])
    return from_before, from_after


def local(observed, row_taps, col_taps, spectral_basis, ridge_weights):
    bands_here, height, columns_all = observed.shape
    taps = row_taps.shape[1]
    radius = (taps - 1) // 2
    halo = 2 * radius
    bands, kinds = spectral_basis.shape
    n_band = lax.axis_size("band")
    n_row = lax.axis_size("row")
    columns = columns_all // n_band
    lanes = round_up(columns + 2 * halo, 2 * LANES)
    me_band = lax.axis_index("band")
    me_row = lax.axis_index("row")
    core = me_band % 2
    chip = me_band // 2
    chips = n_band // 2

    plain = jnp.concatenate([row_taps, col_taps], axis=1)
    everyone = [(plain, me_band)]
    for hop in range(1, n_band):
        moves = [(i, (i + hop) % n_band) for i in range(n_band)]
        everyone.append((lax.ppermute(plain, "band", moves), (me_band - hop) % n_band))
    basis_all = jnp.concatenate(
        [lax.dynamic_slice_in_dim(spectral_basis, at * bands_here, bands_here, 0) for _, at in everyone]
    )
    every = jnp.concatenate([values for values, _ in everyone])

    half = kinds // 2
    place = jnp.stack(
        [
            me_band * bands_here,
            half * (1 - core),
            me_band * columns - radius,
            me_row * height - radius,
            chip,
            me_band,
        ]
    ).astype(jnp.int32)
    whole = lambda shape: pl.BlockSpec(shape, lambda i: (0,) * len(shape))

    few = group_size(bands_here, 64)
    span = round_up(columns_all, 2 * LANES)
    ext = height + 2 * radius
    chunks = ext // SUB
    give, keep = pl.pallas_call(
        functools.partial(adjoint_kernel, columns_all, radius),
        grid=(bands_here // few,),
        in_specs=[
            pl.BlockSpec(memory_space=pltpu.SMEM),
            pl.BlockSpec((few, height, columns_all), lambda i: (i, 0, 0)),
            whole(plain.shape),
            whole((bands, kinds)),
        ],
        out_specs=[whole((ext, half, span))] * 2,
        out_shape=[jax.ShapeDtypeStruct((ext, half, span), BF)] * 2,
        scratch_shapes=[
            pltpu.VMEM((ext if few < bands_here else SUB, kinds, span), F32),
            pltpu.VMEM((chunks, few, SUB, span), F32),
            pltpu.VMEM((few, 4 * LANES, 2 * LANES), BF),
            pltpu.VMEM((few, 2, ext, height), BF),
            pltpu.VMEM((2, bands_here, 1, 2 * LANES), F32),
        ],
        compiler_params=pltpu.CompilerParams(vmem_limit_bytes=VMEM_LIMIT),
        cost_estimate=pl.CostEstimate(
            flops=bands_here * 2 * 96 * 512 * 256, bytes_accessed=observed.size * 2, transcendentals=0
        ),
        name="adjoint",
    )(place, observed, plain, spectral_basis)


    part = group_size(bands, 64)
    deep = sum(end - start for start, end in packed_blocks(columns, halo))
    taps_spec = pl.BlockSpec((part, 2 * taps), lambda i: (i, 0))
    smem = pl.BlockSpec(memory_space=pltpu.SMEM)
    params = pltpu.CompilerParams(vmem_limit_bytes=SMALL_LIMIT)
    gr, sk, pk = pl.pallas_call(
        functools.partial(gram_rows_kernel, height * n_row, radius),
        grid=(bands // part,),
        in_specs=[smem, taps_spec, pl.BlockSpec((part, kinds), lambda i: (i, 0))],
        out_specs=[
            pl.BlockSpec((part, height, LANES), lambda i: (i, 0, 0)),
            pl.BlockSpec((part * SUB, SUB * kinds), lambda i: (i, 0)),
            pl.BlockSpec((1, SUB * kinds, part * SUB), lambda i: (i, 0, 0)),
        ],
        out_shape=[
            jax.ShapeDtypeStruct((bands, height, LANES), BF),
            jax.ShapeDtypeStruct((bands * SUB, SUB * kinds), BF),
            jax.ShapeDtypeStruct((bands // part, SUB * kinds, part * SUB), BF),
        ],
        compiler_params=params,
        cost_estimate=pl.CostEstimate(
            flops=bands * 2 * LANES**3, bytes_accessed=bands * height * LANES * 2, transcendentals=0
        ),
        name="gram_rows",
    )(place, every, basis_all.astype(F32))
    gl = pl.pallas_call(
        functools.partial(gram_columns_kernel, columns, columns_all, radius),
        grid=(bands // part,),
        in_specs=[smem, taps_spec],
        out_specs=pl.BlockSpec((part, deep, LANES), lambda i: (i, 0, 0)),
        out_shape=jax.ShapeDtypeStruct((bands, deep, LANES), BF),
        compiler_params=params,
        cost_estimate=pl.CostEstimate(
            flops=bands * 2 * (2 * LANES) ** 3, bytes_accessed=bands * deep * LANES * 2, transcendentals=0
        ),
        name="gram_columns",
    )(place, every)

    pairs = [(i, i ^ 1) for i in range(n_band)]
    got = lax.ppermute(give, "band", pairs)
    wide = min(columns_all, 2 * columns + (2 * halo if chips > 2 else halo))
    wide_lanes = round_up(wide, LANES)
    starts = [min(max(2 * columns * c - halo, 0), columns_all - wide) for c in range(chips)]
    vmem = pl.BlockSpec(memory_space=pltpu.VMEM)
    shape = lambda rows, kind: jax.ShapeDtypeStruct((rows, half, wide_lanes), kind)
    sends = pl.pallas_call(
        functools.partial(split_kernel, starts, wide, radius),
        in_specs=[smem, vmem, vmem],
        out_shape=[
            shape(rows, F32 if rows == height and hop == 0 else BF)
            for hop in range(chips)
            for rows in (radius, height, radius)
        ],
        compiler_params=pltpu.CompilerParams(vmem_limit_bytes=VMEM_LIMIT),
        name="split",
    )(place, keep, got)

    def moves(hop, step):
        return [
            (b * n_row + r, (b + 2 * hop) % n_band * n_row + r + step)
            for b in range(n_band)
            for r in range(n_row)
            if 0 <= r + step < n_row
        ]

    parts = []
    axes = ("band", "row")
    for hop in range(chips):
        above, here, below = sends[3 * hop : 3 * hop + 3]
        after = lax.ppermute(above, axes, moves(hop, -1))
        before = lax.ppermute(below, axes, moves(hop, 1))
        if hop:
            here = lax.ppermute(here, axes, moves(hop, 0))
        parts += [before, here, after]
    parts[1], gr, sk, pk = lax.optimization_barrier((parts[1], gr, sk, pk))
    total = pl.pallas_call(
        functools.partial(merge_kernel, radius),
        out_shape=shape(height, F32),
        compiler_params=params,
        name="merge",
    )(*parts)
    other = lax.ppermute(total, "band", pairs)
    window, v0 = pl.pallas_call(
        functools.partial(window_kernel, starts, wide, columns, halo),
        in_specs=[smem, vmem, vmem],
        out_shape=[
            jax.ShapeDtypeStruct((height, kinds, lanes), BF),
            jax.ShapeDtypeStruct((height, kinds, lanes), F32),
        ],
        compiler_params=params,
        name="window",
    )(place, total, other)
    v0 = jnp.swapaxes(v0, 0, 1)

    group = part
    ridge = jnp.broadcast_to(ridge_weights[:, None, None], (kinds, SUB, lanes))
    tall = height + 2 * halo

    def normal_map(pieces, own, first):
        window = [pltpu.VMEM((tall, kinds, lanes), BF)] if not first else []
        return pl.pallas_call(
            functools.partial(first_kernel if first else second_kernel, columns, halo, group),
            grid=(bands // group,),
            in_specs=[vmem] * (len(pieces) + 6),
            out_specs=[vmem, vmem],
            out_shape=[
                jax.ShapeDtypeStruct((kinds, height, lanes), F32),
                jax.ShapeDtypeStruct((SUB, LANES), F32),
            ],
            scratch_shapes=[
                pltpu.VMEM((height // SUB, SUB * kinds, lanes), F32),
                pltpu.VMEM((group, tall, lanes), BF),
                pltpu.VMEM((height // SUB, group, SUB, lanes), F32),
            ]
            + window,
            compiler_params=pltpu.CompilerParams(vmem_limit_bytes=SMALL_LIMIT),
            cost_estimate=pl.CostEstimate(
                flops=bands * 2 * 32 * 512 * 256, bytes_accessed=bands * deep * LANES * 2, transcendentals=0
            ),
            name="normal",
        )(*pieces, own, ridge, sk, pk, gr, gl)

    before, after = shift_both(window[:halo], window[height - halo :], "row")
    v1, sums1 = normal_map([before, window, after], v0, True)
    near = jnp.swapaxes(v1.astype(BF), 0, 1)
    main = jax.ShapeDtypeStruct((main_rows(columns, halo), kinds, LANES), BF)
    up, down = pl.pallas_call(
        functools.partial(pack_kernel, columns, halo),
        out_shape=[main, main],
        compiler_params=params,
        name="pack",
    )(near)
    before, after = shift_both(up, down, "row")
    side = jax.ShapeDtypeStruct((strip_plan(tall, halo)[1], kinds, LANES), BF)
    left, right = pl.pallas_call(
        functools.partial(side_kernel, columns, halo),
        out_shape=[side, side],
        compiler_params=params,
        name="sides",
    )(near, before, after)
    left, right = shift_both(left, right, "band")
    pieces = [near, before, after, left, right]
    v2, sums2 = normal_map(pieces, v1, False)

    sums = jnp.concatenate([sums1[:3], sums2[:1], jnp.zeros((SUB - 4, LANES), F32)])
    mine = jnp.broadcast_to(sums[None], (n_band * n_row, SUB, LANES))
    shared = lax.all_to_all(mine, ("band", "row"), 0, 0, tiled=True)
    out = jax.ShapeDtypeStruct((kinds, height, columns), F32)
    return pl.pallas_call(
        combine_kernel,
        out_shape=[out, out],
        compiler_params=pltpu.CompilerParams(vmem_limit_bytes=SMALL_LIMIT),
        name="combine",
    )(shared, v0, v1, v2)


def solution(mesh):
    in_specs = (P("band", "row", None), P("band", None), P("band", None), P(), P())
    out_specs = (P(None, "row", "band"), P(None, "row", "band"))
    return jax.shard_map(local, mesh=mesh, in_specs=in_specs, out_specs=out_specs, check_vma=False)
```

```python
import functools

import jax
import jax.numpy as jnp
from jax import lax
from jax.experimental import pallas as pl
from jax.experimental.pallas import tpu as pltpu
from jax.sharding import PartitionSpec as P

LANES = 128
SUB = 8
BF = jnp.bfloat16
F32 = jnp.float32
VMEM_LIMIT = 50 * 1024 * 1024
SMALL_LIMIT = 20 * 1024 * 1024


def round_up(value, unit):
    return (value + unit - 1) // unit * unit


def group_size(count, most):
    return max(size for size in range(1, most + 1) if count % size == 0)


def packed_blocks(columns, halo):
    out = []
    for first in range(0, columns, LANES):
        out.append((first, round_up(min(first + LANES, columns) + 2 * halo, 2 * SUB)))
    return out


def dot(lhs, rhs):
    return lax.dot_general(lhs, rhs, (((1,), (0,)), ((), ())), preferred_element_type=F32)


def toeplitz(taps, rows, shift):
    lanes = taps.shape[1]
    pieces = []
    for first in range(0, rows, LANES):
        count = min(LANES, rows - first)
        wide = jnp.broadcast_to(taps, (count, lanes))
        pieces.append(pltpu.roll(wide, (shift + first) % lanes, 1, stride=1, stride_axis=0))
    return jnp.concatenate(pieces, axis=0) if len(pieces) > 1 else pieces[0]


def chosen(shape, rule, kind=BF):
    row = lax.broadcasted_iota(jnp.int32, shape, 0)
    lane = lax.broadcasted_iota(jnp.int32, shape, 1)
    return jnp.where(rule(row, lane), 1.0, 0.0).astype(kind)


def placed_taps(both, places, kind, axis=1):
    count = both.shape[axis] // 2
    picks = []
    for first, lead, flip in places:

        def rule(row, lane):
            at = lane - lead
            here = (at >= 0) & (at < count)
            return here & (row == first + (count - 1 - at if flip else at))

        picks.append(chosen((both.shape[axis], 2 * LANES), rule, kind))
    done = lax.dot_general(
        both.astype(kind),
        jnp.concatenate(picks, axis=1),
        (((axis,), (0,)), ((), ())),
        precision=lax.Precision.HIGHEST if kind == F32 else None,
        preferred_element_type=F32,
    )
    return [done[:, i * 2 * LANES : (i + 1) * 2 * LANES] for i in range(len(places))]


def dot_rows(lhs, rhs):
    return lax.dot_general(lhs, rhs, (((1,), (1,)), ((), ())), preferred_element_type=F32)


def strip_plan(rows, width):
    beside = max(n for n in range(1, rows + 1) if rows % n == 0 and n * width <= LANES)
    return beside, rows // beside


def turn_lanes(cells, amount):
    rows, kinds, lanes = cells.shape
    flat = pltpu.roll(cells.reshape(rows * kinds, lanes), amount % lanes, 1)
    return flat.reshape(rows, kinds, lanes)


def keep_lanes(cells, first, width):
    lane = lax.broadcasted_iota(jnp.int32, cells.shape, 2)
    return jnp.where((lane >= first) & (lane < first + width), cells, 0.0)


def packed_strip(cells, first, width):
    beside, rows = strip_plan(cells.shape[0], width)
    total = None
    for g in range(beside):
        part = turn_lanes(cells[g * rows : (g + 1) * rows], g * width - first)[:, :, :LANES]
        part = keep_lanes(part, g * width, width)
        total = part if total is None else total + part
    return total


def unpacked_strip(packed, count, width, first, lanes):
    beside, rows = strip_plan(count, width)
    wide = packed.astype(F32)
    if lanes > LANES:
        rest = jnp.zeros(packed.shape[:2] + (lanes - LANES,), F32)
        wide = jnp.concatenate([wide, rest], axis=2)
    return jnp.concatenate(
        [keep_lanes(turn_lanes(wide, first - g * width), first, width) for g in range(beside)], axis=0
    )


def main_rows(columns, halo):
    full = columns // LANES
    rest = columns - full * LANES
    return full * halo + (strip_plan(halo, rest)[1] if rest else 0)


def packed_main(cells, columns):
    full = columns // LANES
    rest = columns - full * LANES
    parts = [cells[:, :, t * LANES : (t + 1) * LANES] for t in range(full)]
    if rest:
        parts.append(packed_strip(cells, full * LANES, rest))
    return jnp.concatenate(parts, axis=0)


def unpacked_main(packed, columns, halo, lanes):
    full = columns // LANES
    rest = columns - full * LANES
    kinds = packed.shape[1]
    total = jnp.zeros((halo, kinds, lanes), F32)
    for t in range(full):
        part = packed[t * halo : (t + 1) * halo]
        total = total + unpacked_wide(part, t * LANES + halo, lanes)
    if rest:
        total = total + unpacked_strip(packed[full * halo :], halo, rest, full * LANES + halo, lanes)
    return total


def unpacked_wide(part, first, lanes):
    wide = part.astype(F32)
    if lanes > LANES:
        rest = jnp.zeros(part.shape[:2] + (lanes - LANES,), F32)
        wide = jnp.concatenate([wide, rest], axis=2)
    return turn_lanes(wide, first)


def pack_kernel(columns, halo, near_ref, up_ref, down_ref):
    cells = near_ref[...].astype(F32)
    height = cells.shape[0]
    up_ref[...] = packed_main(cells[:halo], columns).astype(BF)
    down_ref[...] = packed_main(cells[height - halo :], columns).astype(BF)


def tall_rows(columns, halo, near_ref, before_ref, after_ref):
    lanes = near_ref.shape[2]
    return [turn_lanes(near_ref[...].astype(F32), halo)] + [
        unpacked_main(ref[...], columns, halo, lanes) for ref in (before_ref, after_ref)
    ]


def side_kernel(columns, halo, near_ref, before_ref, after_ref, left_ref, right_ref):
    cells = jnp.concatenate(tall_rows(columns, halo, near_ref, before_ref, after_ref), axis=0)
    left_ref[...] = packed_strip(cells, halo, halo).astype(BF)
    right_ref[...] = packed_strip(cells, columns, halo).astype(BF)


def window_pieces(columns, halo, near_ref, before_ref, after_ref, left_ref, right_ref, p_ref):
    height, _, lanes = near_ref.shape
    tall = height + 2 * halo
    sides = unpacked_strip(left_ref[...], tall, halo, 0, lanes)
    sides = sides + unpacked_strip(right_ref[...], tall, halo, columns + halo, lanes)
    at = 0
    for rows, to in zip(tall_rows(columns, halo, near_ref, before_ref, after_ref), (halo, 0, halo + height)):
        count = rows.shape[0]
        p_ref[to : to + count] = (rows + sides[at : at + count]).astype(BF)
        at += count


def adjoint_kernel(
    columns, radius, place_ref, obs_ref, taps_ref, basis_ref, give_ref, keep_ref, acc, ys, mats, rows, lines
):
    step = pl.program_id(0)
    group, height, _ = obs_ref.shape
    span = ys.shape[3]
    width = 2 * LANES
    tiles = span // width
    chunks = ys.shape[0]
    ext = chunks * SUB
    edge = 2 * SUB
    last = columns // LANES * LANES
    batch = group_size(group, 7)

    blank_rows = jnp.zeros((LANES - edge, width), BF)

    @pl.when(step == 0)
    def _():
        for b in range(group):
            mats[b, : LANES - edge] = blank_rows
            mats[b, LANES + width + edge :] = blank_rows
        both = taps_ref[...]
        taps = both.shape[0] // 2
        places = [(taps, -radius % SUB, False), (0, 0, True)]
        for i, line in enumerate(placed_taps(both, places, F32, 0)):
            lines[i] = line[:, None]

    @pl.loop(0, group, step=batch)
    def _(start):
        near = lax.broadcasted_iota(jnp.int32, (edge, width), 1) < LANES
        blank = jnp.zeros((edge, width), BF)
        for b in range(batch):
            b = start + b
            ring = toeplitz(lines[0, step * group + b], width, -round_up(radius, SUB)).astype(BF)
            top, bottom = ring[:edge], ring[width - edge :]
            mats[b, LANES - edge : LANES] = jnp.where(near, bottom, blank)
            mats[b, LANES : LANES + edge] = jnp.where(near, top, blank)
            mats[b, LANES + edge : LANES + width - edge] = ring[edge : width - edge]
            mats[b, LANES + width - edge : LANES + width] = jnp.where(near, blank, bottom)
            mats[b, LANES + width : LANES + width + edge] = jnp.where(near, blank, top)
            reach = toeplitz(lines[1, step * group + b][:, :LANES], ext, -2 * radius)[:, :height]
            high = reach.astype(BF)
            rows[b, 0] = high
            rows[b, 1] = (reach - high.astype(F32)).astype(BF)

    @pl.loop(0, group, step=batch)
    def _(start):
        fields = []
        for b in range(batch):
            cells = obs_ref[start + b]
            pieces = [jnp.zeros((height, LANES), BF), cells[:, :last]]
            if columns > last:
                fill = jnp.zeros((height, LANES - (columns - last)), BF)
                pieces.append(jnp.concatenate([cells[:, last:], fill], axis=1))
            have = sum(piece.shape[1] for piece in pieces)
            if have < span + width:
                pieces.append(jnp.zeros((height, span + width - have), BF))
            padded = jnp.concatenate(pieces, axis=1)
            stacked = jnp.concatenate(
                [padded[:, t * width : t * width + 2 * width] for t in range(tiles)], axis=0
            )
            mixed = dot(stacked, mats[start + b]).astype(BF)
            fields.append(
                jnp.concatenate([mixed[t * height : (t + 1) * height] for t in range(tiles)], axis=1)
            )
        for b in range(batch):
            done = dot(rows[start + b, 0], fields[b]) + dot(rows[start + b, 1], fields[b])
            for c in range(chunks):
                ys[c, start + b] = done[c * SUB : (c + 1) * SUB]

    kinds, bands = basis_ref.shape
    first = place_ref[0] + step * group
    turn = place_ref[1]
    pick = chosen((SUB * kinds, kinds), lambda row, lane: lane == (row + turn) % kinds)
    wide = dot(pick, basis_ref[...]).astype(BF)
    here = chosen((bands, group * SUB), lambda row, lane: row == first + lane // SUB)
    same = chosen((SUB * kinds, group * SUB), lambda row, lane: row // kinds == lane % SUB, F32)
    mix = (dot(wide, here) * same).astype(BF)
    for c in range(chunks):
        cells = ys[c].reshape(group * SUB, span).astype(BF)
        total = dot(mix, cells).reshape(SUB, kinds, span)
        half = kinds // 2
        here = slice(c * SUB, (c + 1) * SUB)

        if acc.shape[0] == ext:
            @pl.when(step == 0)
            def _():
                acc[here] = total

            @pl.when(step > 0)
            def _():
                acc[here] += total

            total = acc[here]
        give_ref[here] = total[:, :half].astype(BF)
        keep_ref[here] = total[:, half:].astype(BF)


def inside(lanes, first, count, limit):
    lane = lax.broadcasted_iota(jnp.int32, (1, lanes), 1)
    at = lane + first
    return jnp.where((at >= 0) & (at < limit) & (lane < count), 1.0, 0.0)


def gram_columns_kernel(columns, columns_all, radius, place_ref, taps_ref, gl_ref):
    halo = 2 * radius
    size = 2 * LANES
    blocks = packed_blocks(columns, halo)
    tall = max(end for _, end in blocks)
    inner = round_up(columns + halo, 2 * SUB)
    both = taps_ref[...]
    taps = both.shape[1] // 2
    line, back = placed_taps(both, [(taps, 0, False), (taps, 0, True)], BF)
    mask = inside(size, place_ref[2], columns + halo, columns_all)
    for b in range(both.shape[0]):
        left = (toeplitz(back[b : b + 1], tall, -halo) * mask).astype(BF)
        right = toeplitz(line[b : b + 1], inner, -halo).astype(BF)
        right = jnp.concatenate([right, jnp.zeros((size - inner, size), BF)], axis=0)
        done = dot(left, right).astype(BF)
        at = 0
        for i, (start, end) in enumerate(blocks):
            gl_ref[b, at : at + end - start] = done[start:end, i * LANES : (i + 1) * LANES]
            at += end - start


def gram_rows_kernel(rows_all, radius, place_ref, taps_ref, basis_ref, gr_ref, sk_ref, pk_ref):
    halo = 2 * radius
    group, height, lanes = gr_ref.shape
    both = taps_ref[...]
    line, back = [part[:, :lanes] for part in placed_taps(both, [(0, 0, False), (0, 0, True)], BF)]
    mask = inside(lanes, place_ref[3], height + halo, rows_all)
    for b in range(group):
        left = (toeplitz(back[b : b + 1], height, 0) * mask).astype(BF)
        right = toeplitz(line[b : b + 1], lanes, 0).astype(BF)
        gr_ref[b] = dot(left, right).astype(BF)
    basis = basis_ref[...].astype(BF)
    kinds = basis.shape[1]
    up = chosen((group * SUB, group), lambda row, lane: row // SUB == lane)
    out = chosen((kinds, SUB * kinds), lambda row, lane: row == lane % kinds)
    same = chosen((group * SUB, SUB * kinds), lambda row, lane: row % SUB == lane // kinds, F32)
    sk_ref[...] = (dot(dot(up, basis).astype(BF), out) * same).astype(BF)
    up = chosen((SUB * kinds, kinds), lambda row, lane: row // SUB == lane)
    out = chosen((group, group * SUB), lambda row, lane: row == lane // SUB)
    same = chosen((SUB * kinds, group * SUB), lambda row, lane: row % SUB == lane % SUB, F32)
    pk_ref[0] = (dot(dot_rows(up, basis).astype(BF), out) * same).astype(BF)


def lane_window(cells, first, width, lanes):
    have = cells.shape[1]
    base = max(first, 0) // LANES * LANES
    stop = min(have, round_up(first + width, LANES))
    part = cells[:, base:stop]
    size = max(stop - base, lanes)
    if size > stop - base:
        part = jnp.concatenate([part, jnp.zeros((cells.shape[0], size - (stop - base)), F32)], axis=1)
    if (base - first) % size:
        part = pltpu.roll(part, (base - first) % size, 1)
    lane = lax.broadcasted_iota(jnp.int32, (cells.shape[0], lanes), 1)
    low, high = max(0, -first), min(width, have - first)
    return jnp.where((lane >= low) & (lane < high), part[:, :lanes], 0.0)


def split_kernel(starts, wide, radius, place_ref, keep_ref, got_ref, *out_refs):
    chips = len(starts)
    ext, half, span = keep_ref.shape
    lanes = out_refs[0].shape[2]
    unit = 4
    for chip in range(chips):

        @pl.when(place_ref[4] == chip)
        def _():
            for r in range(0, ext, unit):
                pair = keep_ref[r : r + unit].astype(F32) + got_ref[r : r + unit].astype(F32)
                flat = pair.reshape(unit * half, span)
                for hop in range(chips):
                    part = lane_window(flat, starts[(chip + hop) % chips], wide, lanes)
                    part = part.reshape(unit, half, lanes)
                    above, here, below = out_refs[3 * hop : 3 * hop + 3]
                    if r < radius:
                        above[r : r + unit] = part.astype(above.dtype)
                    elif r < ext - radius:
                        here[r - radius : r - radius + unit] = part.astype(here.dtype)
                    else:
                        below[r - ext + radius : r - ext + radius + unit] = part.astype(below.dtype)


def merge_kernel(radius, *refs):
    *in_refs, out_ref = refs
    height = out_ref.shape[0]
    total = in_refs[1][...].astype(F32)
    for i in range(4, len(in_refs), 3):
        total = total + in_refs[i][...].astype(F32)
    first = sum(in_refs[i][...].astype(F32) for i in range(0, len(in_refs), 3))
    last = sum(in_refs[i][...].astype(F32) for i in range(2, len(in_refs), 3))
    out_ref[:radius] = total[:radius] + first
    out_ref[radius : height - radius] = total[radius : height - radius]
    out_ref[height - radius :] = total[height - radius :] + last


def window_kernel(starts, wide, columns, halo, place_ref, mine_ref, other_ref, window_ref, own_ref):
    height, half, lanes_in = mine_ref.shape
    lanes = window_ref.shape[2]
    unit = 4
    for band in range(2 * len(starts)):
        first = band * columns - starts[band // 2]

        @pl.when(place_ref[5] == band)
        def _():
            for r in range(0, height, unit):
                for core in range(2):
                    source = mine_ref if core == band % 2 else other_ref
                    flat = source[r : r + unit].reshape(unit * half, lanes_in)
                    kinds = slice(core * half, (core + 1) * half)
                    part = lane_window(flat, first - halo, columns + 2 * halo, lanes)
                    window_ref[r : r + unit, kinds] = part.reshape(unit, half, lanes).astype(BF)
                    part = lane_window(flat, first, columns, lanes)
                    own_ref[r : r + unit, kinds] = part.reshape(unit, half, lanes)


def first_kernel(columns, halo, group, before, window, after, *rest):
    normal_kernel(columns, halo, group, True, (before, window, after), *rest)


def second_kernel(columns, halo, group, near_ref, before, after, left, right, *rest):
    *rest, p_ref = rest

    @pl.when(pl.program_id(0) == 0)
    def _():
        window_pieces(columns, halo, near_ref, before, after, left, right, p_ref)

    normal_kernel(columns, halo, group, False, (p_ref,), *rest)


def normal_kernel(
    columns, halo, group, first, p_refs, own_ref, ridge_ref, sk_ref, pk_ref, gr_ref, gl_ref, out_ref, sums_ref, acc, xs, ys
):
    step = pl.program_id(0)
    height = gr_ref.shape[1]
    from_band = step * group
    _, kinds, lanes = p_refs[0].shape
    sources = [(ref, s) for ref in p_refs for s in range(0, ref.shape[0], SUB)]
    ext = SUB * len(sources)
    chunks = height // SUB

    @pl.when(step == 0)
    def _():
        acc[...] = jnp.zeros_like(acc)

    spread = sk_ref[pl.ds(pl.multiple_of(from_band * SUB, group * SUB), group * SUB)]
    for c in range(0, ext, 2 * SUB):
        halves = []
        for ref, s in sources[c // SUB : c // SUB + 2]:
            cells = ref[s : s + SUB].reshape(SUB * kinds, lanes)
            halves.append(dot(spread, cells).reshape(group, SUB, lanes))
        xs[:, c : c + 2 * SUB, :] = jnp.concatenate(halves, axis=1).astype(BF)

    blocks = packed_blocks(columns, halo)
    mids = [dot(gr_ref[from_band + b, :, :ext], xs[b]).astype(BF) for b in range(group)]
    for b in range(group):
        parts = []
        at = 0
        for i in range(lanes // LANES):
            if i < len(blocks):
                start, end = blocks[i]
                part = [gl_ref[from_band + b, at : at + end - start]]
                at += end - start
                if start:
                    part = [jnp.zeros((start, LANES), BF)] + part
                if end < lanes:
                    part = part + [jnp.zeros((lanes - end, LANES), BF)]
                parts.append(jnp.concatenate(part, axis=0))
            else:
                parts.append(jnp.zeros((lanes, LANES), BF))
        done = dot(mids[b], jnp.concatenate(parts, axis=1))
        for c in range(chunks):
            ys[c, b] = done[c * SUB : (c + 1) * SUB]

    gather = pk_ref[step]
    for c in range(chunks):
        acc[c] += dot(gather, ys[c].reshape(group * SUB, lanes).astype(BF))

    @pl.when(step == pl.num_programs(0) - 1)
    def _():
        lane = lax.broadcasted_iota(jnp.int32, (kinds, SUB, lanes), 2)
        totals = [jnp.zeros((SUB, lanes), F32) for _ in range(3)]
        for c in range(chunks):
            own = own_ref[:, c * SUB : (c + 1) * SUB, :]
            image = acc[c].reshape(kinds, SUB, lanes) + ridge_ref[...] * own
            image = jnp.where(lane < columns, image, 0.0)
            out_ref[:, c * SUB : (c + 1) * SUB, :] = image
            pairs = [own * image]
            if first:
                pairs += [own * own, image * image]
            for i, pair in enumerate(pairs):
                totals[i] = totals[i] + jnp.sum(pair, axis=0)
        flat = [
            jnp.sum(
                jnp.concatenate(
                    [total[:, i : i + LANES] for i in range(0, lanes, LANES)], axis=0
                ),
                axis=0,
                keepdims=True,
            )
            for total in totals
        ]
        row = lax.broadcasted_iota(jnp.int32, (SUB, LANES), 0)
        packed = jnp.zeros((SUB, LANES), F32)
        for i, line in enumerate(flat):
            packed = packed + jnp.where(row == i, jnp.broadcast_to(line, (SUB, LANES)), 0.0)
        sums_ref[...] = packed


def combine_kernel(shared_ref, v0_ref, v1_ref, v2_ref, coef_ref, res_ref):
    columns = coef_ref.shape[2]
    lines = jnp.sum(shared_ref[...], axis=0)
    v01, v00, v11, v12 = [jnp.sum(lines[i : i + 1], axis=1, keepdims=True) for i in range(4)]
    alpha = v00 / v01
    norm = v00 - 2.0 * alpha * v01 + alpha * alpha * v11
    lead = 1.0 + norm / v00
    product = lead * lead * v01 - 2.0 * lead * alpha * v11 + alpha * alpha * v12
    second = norm / product
    one = alpha + second * lead
    two = second * alpha
    for k in range(coef_ref.shape[0]):
        v0, v1, v2 = v0_ref[k], v1_ref[k], v2_ref[k]
        coef_ref[k] = (one * v0 - two * v1)[:, :columns]
        res_ref[k] = (v0 - one * v1 + two * v2)[:, :columns]


def shift_both(low_edge, high_edge, axis):
    count = lax.axis_size(axis)
    from_before = lax.ppermute(high_edge, axis, [(i, i + 1) for i in range(count - 1)])
    from_after = lax.ppermute(low_edge, axis, [(i + 1, i) for i in range(count - 1)])
    return from_before, from_after


def local(observed, row_taps, col_taps, spectral_basis, ridge_weights):
    bands_here, height, columns_all = observed.shape
    taps = row_taps.shape[1]
    radius = (taps - 1) // 2
    halo = 2 * radius
    bands, kinds = spectral_basis.shape
    n_band = lax.axis_size("band")
    n_row = lax.axis_size("row")
    columns = columns_all // n_band
    lanes = round_up(columns + 2 * halo, 2 * LANES)
    me_band = lax.axis_index("band")
    me_row = lax.axis_index("row")
    core = me_band % 2
    chip = me_band // 2
    chips = n_band // 2

    plain = jnp.concatenate([row_taps.T, col_taps.T], axis=0)
    everyone = [(plain, me_band)]
    for hop in range(1, n_band):
        moves = [(i, (i + hop) % n_band) for i in range(n_band)]
        everyone.append((lax.ppermute(plain, "band", moves), (me_band - hop) % n_band))
    basis_all = jnp.concatenate(
        [lax.dynamic_slice_in_dim(spectral_basis, at * bands_here, bands_here, 0) for _, at in everyone]
    )
    every = jnp.concatenate([values for values, _ in everyone], axis=1).T

    half = kinds // 2
    place = jnp.stack(
        [
            me_band * bands_here,
            half * (1 - core),
            me_band * columns - radius,
            me_row * height - radius,
            chip,
            me_band,
        ]
    ).astype(jnp.int32)
    whole = lambda shape: pl.BlockSpec(shape, lambda i: (0,) * len(shape))

    few = group_size(bands_here, 64)
    span = round_up(columns_all, 2 * LANES)
    ext = height + 2 * radius
    chunks = ext // SUB
    give, keep = pl.pallas_call(
        functools.partial(adjoint_kernel, columns_all, radius),
        grid=(bands_here // few,),
        in_specs=[
            pl.BlockSpec(memory_space=pltpu.SMEM),
            pl.BlockSpec((few, height, columns_all), lambda i: (i, 0, 0)),
            whole(plain.shape),
            whole((kinds, bands)),
        ],
        out_specs=[whole((ext, half, span))] * 2,
        out_shape=[jax.ShapeDtypeStruct((ext, half, span), BF)] * 2,
        scratch_shapes=[
            pltpu.VMEM((ext if few < bands_here else SUB, kinds, span), F32),
            pltpu.VMEM((chunks, few, SUB, span), F32),
            pltpu.VMEM((few, 4 * LANES, 2 * LANES), BF),
            pltpu.VMEM((few, 2, ext, height), BF),
            pltpu.VMEM((2, bands_here, 1, 2 * LANES), F32),
        ],
        compiler_params=pltpu.CompilerParams(vmem_limit_bytes=VMEM_LIMIT),
        cost_estimate=pl.CostEstimate(
            flops=bands_here * 2 * 96 * 512 * 256, bytes_accessed=observed.size * 2, transcendentals=0
        ),
        name="adjoint",
    )(place, observed, plain, spectral_basis.T)


    part = group_size(bands, 64)
    deep = sum(end - start for start, end in packed_blocks(columns, halo))
    taps_spec = pl.BlockSpec((part, 2 * taps), lambda i: (i, 0))
    smem = pl.BlockSpec(memory_space=pltpu.SMEM)
    params = pltpu.CompilerParams(vmem_limit_bytes=SMALL_LIMIT)
    gr, sk, pk = pl.pallas_call(
        functools.partial(gram_rows_kernel, height * n_row, radius),
        grid=(bands // part,),
        in_specs=[smem, taps_spec, pl.BlockSpec((part, kinds), lambda i: (i, 0))],
        out_specs=[
            pl.BlockSpec((part, height, LANES), lambda i: (i, 0, 0)),
            pl.BlockSpec((part * SUB, SUB * kinds), lambda i: (i, 0)),
            pl.BlockSpec((1, SUB * kinds, part * SUB), lambda i: (i, 0, 0)),
        ],
        out_shape=[
            jax.ShapeDtypeStruct((bands, height, LANES), BF),
            jax.ShapeDtypeStruct((bands * SUB, SUB * kinds), BF),
            jax.ShapeDtypeStruct((bands // part, SUB * kinds, part * SUB), BF),
        ],
        compiler_params=params,
        cost_estimate=pl.CostEstimate(
            flops=bands * 2 * LANES**3, bytes_accessed=bands * height * LANES * 2, transcendentals=0
        ),
        name="gram_rows",
    )(place, every, basis_all.astype(F32))
    gl = pl.pallas_call(
        functools.partial(gram_columns_kernel, columns, columns_all, radius),
        grid=(bands // part,),
        in_specs=[smem, taps_spec],
        out_specs=pl.BlockSpec((part, deep, LANES), lambda i: (i, 0, 0)),
        out_shape=jax.ShapeDtypeStruct((bands, deep, LANES), BF),
        compiler_params=params,
        cost_estimate=pl.CostEstimate(
            flops=bands * 2 * (2 * LANES) ** 3, bytes_accessed=bands * deep * LANES * 2, transcendentals=0
        ),
        name="gram_columns",
    )(place, every)

    pairs = [(i, i ^ 1) for i in range(n_band)]
    got = lax.ppermute(give, "band", pairs)
    wide = min(columns_all, 2 * columns + (2 * halo if chips > 2 else halo))
    wide_lanes = round_up(wide, LANES)
    starts = [min(max(2 * columns * c - halo, 0), columns_all - wide) for c in range(chips)]
    vmem = pl.BlockSpec(memory_space=pltpu.VMEM)
    shape = lambda rows, kind: jax.ShapeDtypeStruct((rows, half, wide_lanes), kind)
    sends = pl.pallas_call(
        functools.partial(split_kernel, starts, wide, radius),
        in_specs=[smem, vmem, vmem],
        out_shape=[
            shape(rows, F32 if rows == height and hop == 0 else BF)
            for hop in range(chips)
            for rows in (radius, height, radius)
        ],
        compiler_params=pltpu.CompilerParams(vmem_limit_bytes=VMEM_LIMIT),
        name="split",
    )(place, keep, got)

    def moves(hop, step):
        return [
            (b * n_row + r, (b + 2 * hop) % n_band * n_row + r + step)
            for b in range(n_band)
            for r in range(n_row)
            if 0 <= r + step < n_row
        ]

    parts = []
    axes = ("band", "row")
    for hop in range(chips):
        above, here, below = sends[3 * hop : 3 * hop + 3]
        after = lax.ppermute(above, axes, moves(hop, -1))
        before = lax.ppermute(below, axes, moves(hop, 1))
        if hop:
            here = lax.ppermute(here, axes, moves(hop, 0))
        parts += [before, here, after]
    parts[1], gr, sk, pk = lax.optimization_barrier((parts[1], gr, sk, pk))
    total = pl.pallas_call(
        functools.partial(merge_kernel, radius),
        out_shape=shape(height, F32),
        compiler_params=params,
        name="merge",
    )(*parts)
    other = lax.ppermute(total, "band", pairs)
    window, v0 = pl.pallas_call(
        functools.partial(window_kernel, starts, wide, columns, halo),
        in_specs=[smem, vmem, vmem],
        out_shape=[
            jax.ShapeDtypeStruct((height, kinds, lanes), BF),
            jax.ShapeDtypeStruct((height, kinds, lanes), F32),
        ],
        compiler_params=params,
        name="window",
    )(place, total, other)
    v0 = jnp.swapaxes(v0, 0, 1)

    group = part
    ridge = jnp.broadcast_to(ridge_weights[:, None, None], (kinds, SUB, lanes))
    tall = height + 2 * halo

    def normal_map(pieces, own, first):
        window = [pltpu.VMEM((tall, kinds, lanes), BF)] if not first else []
        return pl.pallas_call(
            functools.partial(first_kernel if first else second_kernel, columns, halo, group),
            grid=(bands // group,),
            in_specs=[vmem] * (len(pieces) + 6),
            out_specs=[vmem, vmem],
            out_shape=[
                jax.ShapeDtypeStruct((kinds, height, lanes), F32),
                jax.ShapeDtypeStruct((SUB, LANES), F32),
            ],
            scratch_shapes=[
                pltpu.VMEM((height // SUB, SUB * kinds, lanes), F32),
                pltpu.VMEM((group, tall, lanes), BF),
                pltpu.VMEM((height // SUB, group, SUB, lanes), F32),
            ]
            + window,
            compiler_params=pltpu.CompilerParams(vmem_limit_bytes=SMALL_LIMIT),
            cost_estimate=pl.CostEstimate(
                flops=bands * 2 * 32 * 512 * 256, bytes_accessed=bands * deep * LANES * 2, transcendentals=0
            ),
            name="normal",
        )(*pieces, own, ridge, sk, pk, gr, gl)

    before, after = shift_both(window[:halo], window[height - halo :], "row")
    v1, sums1 = normal_map([before, window, after], v0, True)
    near = jnp.swapaxes(v1.astype(BF), 0, 1)
    main = jax.ShapeDtypeStruct((main_rows(columns, halo), kinds, LANES), BF)
    up, down = pl.pallas_call(
        functools.partial(pack_kernel, columns, halo),
        out_shape=[main, main],
        compiler_params=params,
        name="pack",
    )(near)
    before, after = shift_both(up, down, "row")
    side = jax.ShapeDtypeStruct((strip_plan(tall, halo)[1], kinds, LANES), BF)
    left, right = pl.pallas_call(
        functools.partial(side_kernel, columns, halo),
        out_shape=[side, side],
        compiler_params=params,
        name="sides",
    )(near, before, after)
    left, right = shift_both(left, right, "band")
    pieces = [near, before, after, left, right]
    v2, sums2 = normal_map(pieces, v1, False)

    sums = jnp.concatenate([sums1[:3], sums2[:1], jnp.zeros((SUB - 4, LANES), F32)])
    mine = jnp.broadcast_to(sums[None], (n_band * n_row, SUB, LANES))
    shared = lax.all_to_all(mine, ("band", "row"), 0, 0, tiled=True)
    out = jax.ShapeDtypeStruct((kinds, height, columns), F32)
    return pl.pallas_call(
        combine_kernel,
        out_shape=[out, out],
        compiler_params=pltpu.CompilerParams(vmem_limit_bytes=SMALL_LIMIT),
        name="combine",
    )(shared, v0, v1, v2)


def solution(mesh):
    in_specs = (P("band", "row", None), P("band", None), P("band", None), P(), P())
    out_specs = (P(None, "row", "band"), P(None, "row", "band"))
    return jax.shard_map(local, mesh=mesh, in_specs=in_specs, out_specs=out_specs, check_vma=False)
```
